32 devices in a mesh: grp: 2 (over y), wide: 4 (over z), narrow: 4 (over x, core).
Axes of the slice: x: 2, y: 2, z: 4, core: 2. Of those that a mesh axis runs over, the one named last changes fastest.
Arguments:
- queries: bfloat16 [2, 128, 32, 128], P(None, ('grp', 'wide'), 'narrow'), parts along dimension 1
- key_cache: bfloat16 [2, 128, 64, 4, 128], P(None, ('grp', 'wide'), None, 'narrow'), parts along dimension 1
- cached_value_rows: bfloat16 [2, 128, 64, 4, 128], P(None, ('grp', 'wide'), None, 'narrow'), parts along dimension 1, may hold values from -5 to 5
- lengths: int32 [2, 128], P(None, ('grp', 'wide')), parts along dimension 1, may hold values from 8 to 64, as said below
- residual: bfloat16 [2, 128, 2048], P(None, ('grp', 'wide'), 'narrow'), parts along dimension 1, may hold values from -6 to 6
- w_out: bfloat16 [4096, 2048], P('narrow', 'wide'), may hold values from -0.09375 to 0.09375
- norm_gain: float32 [2048], replicated, may hold values from 0.1 to 1.9
- expert_ids: int32 [2, 128, 8], P(None, ('grp', 'wide')), parts along dimension 1, may hold values from 0 to 63, all different within a row; in each aligned block of 16 rows (0 to 15, 16 to 31, ..., all dimensions but the last counted through in order) at most 3 rows name the same one
- route_weights: float32 [2, 128, 8], P(None, ('grp', 'wide')), parts along dimension 1, may hold values from 0.05 to 1
- w_gate: bfloat16 [64, 2048, 1024], P('wide', None, 'narrow'), may hold values from -0.125 to 0.125
- w_up: bfloat16 [64, 2048, 1024], P('wide', None, 'narrow'), may hold values from -0.125 to 0.125
- w_down: bfloat16 [64, 1024, 2048], P('wide', 'narrow'), may hold values from -0.1875 to 0.1875
Outputs:
- layer_out: bfloat16 [2, 128, 2048], P(None, ('grp', 'wide'), 'narrow'), parts along dimension 1
The draws below stay inside these ranges and needn't reach their ends.
There are 2 independent parts, one for each index of `grp`. The reference program is written for one: setup_inputs(seed, part) draws one part's arguments, and reference() takes and returns one part's arrays. A program takes and returns all parts, laid end to end along the dimension named above; an argument that names none is the same for every part. Nothing has to cross between parts.
Inputs may be any that keep to these rules, and one draw needn't show every extreme that they name: `expert_ids`: the 8 experts of a row differ. Among the rows of one device in one microbatch (16 rows, aligned blocks) no expert is named by more than 3 rows; every expert is named by some row. `lengths`: the first request of each microbatch uses all 64 positions.
All inputs are finite; a program needn't handle non-finite values.
Results may differ from the reference program's by a relative error of at most 0.015.
Values may be sent and summed in bfloat16 or wider, within the bound.
No kernel may reach another device: no remote copies, remote signals or barrier semaphores. Data moves between devices by JAX's collectives and lax.ppermute only.
A program may use at most 192 MiB of HBM per device.

```python
import math
import jax
import jax.numpy as jnp
import numpy as np
from jax import lax

D = 2048
QUERY_HEADS = 32
KEY_VALUE_HEADS = 4
HEAD_WIDTH = 128
FF = 1024
EXPERTS = 64
TOP = 8
MICROBATCH_COUNT = 2
ROWS_DEV = 16
CONTEXT_SLOTS = 64
CAP = 3
REQUEST_ROWS = 64
N_WIDE = 4
N_NARROW = 4


def draw_queries(key, part):
    key = jax.random.fold_in(key, 11)
    base_offset = jnp.clip(jax.random.normal(key, (MICROBATCH_COUNT, REQUEST_ROWS, QUERY_HEADS, HEAD_WIDTH), jnp.float32), -5.0, 5.0)
    return base_offset.astype(jnp.bfloat16)


def draw_key_cache(key, part):
    key = jax.random.fold_in(key, 12)
    base_offset = jnp.clip(jax.random.normal(key, (MICROBATCH_COUNT, REQUEST_ROWS, CONTEXT_SLOTS, KEY_VALUE_HEADS, HEAD_WIDTH), jnp.float32), -5.0, 5.0)
    return base_offset.astype(jnp.bfloat16)


def draw_lengths(key, part):
    key = jax.random.fold_in(key, 13)
    drawn = jax.random.randint(key, (MICROBATCH_COUNT, REQUEST_ROWS), CONTEXT_SLOTS // 8, CONTEXT_SLOTS + 1)
    return drawn.at[:, 0].set(CONTEXT_SLOTS).astype(jnp.int32)


def steps_of(own_key, shape, shards, low, top_value):
    def one(dim, shards_of):
        steps = jax.random.uniform(jax.random.fold_in(jax.random.fold_in(own_key, 6), dim), (shards_of,), jnp.float32, low / len(shards), top_value / len(shards))
        return jnp.repeat(jnp.exp(steps), shape[dim] // shards_of).reshape((-1,) + (1,) * (len(shape) - dim - 1))

    gain = one(*shards[0])
    for cut in shards[1:]:
        gain = gain * one(*cut)
    return gain


def assign_block(own_key, own, number, rows, amount, top, bound, slope):
    ranking = jax.random.permutation(own_key, amount)
    heavy_load, ordinary = portions_of(amount, rows * top, bound, slope, True), portions_of(amount, rows * top, bound, slope, False)
    places = jnp.arange(amount)

    def named(sizes, offset_by):
        used = int((sizes > 0).sum())
        fixed = max(1, used // 4)
        moved = fixed + (places - fixed + offset_by * (used - fixed)) % max(1, amount - fixed)
        return jnp.zeros((amount,), jnp.int32).at[ranking[jnp.where(places < fixed, places, moved)]].set(jnp.asarray(sizes, jnp.int32))

    sizes = jnp.where(number % 4 == 0, named(heavy_load, number // 4), named(ordinary, number - number // 4 - 1))
    mixed = jax.random.permutation(jax.random.fold_in(own, 3), amount)
    donor, taker = mixed[0:amount // 2 * 2:2], mixed[1:amount // 2 * 2:2]
    room = jnp.minimum(sizes[donor] - 1, bound - sizes[taker]) // 2
    room = jnp.where((donor == ranking[0]) | (taker == ranking[0]) | (sizes[taker] == 0), 0, jnp.maximum(room, 0))
    moved = jax.random.randint(jax.random.fold_in(own, 4), (amount // 2,), 0, 1 << 20) % (room + 1)
    sizes = sizes.at[donor].add(-moved).at[taker].add(moved)
    labels = jnp.searchsorted(jnp.cumsum(sizes), jnp.arange(rows * top), side="right").astype(jnp.int32)
    table = labels.reshape(top, rows).T
    table = table[jax.random.permutation(jax.random.fold_in(own, 1), rows)]
    offset_by = jax.random.randint(jax.random.fold_in(own, 2), (rows, 1), 0, top)
    return jnp.take_along_axis(table, (jnp.arange(top)[None, :] + offset_by) % top, axis=1)


def portions_of(amount, total, limit, slope, full):
    weights = [(1 << 20) // math.isqrt(rank ** slope) + 1 for rank in range(1, amount + 1)]
    largest = limit if full else min(limit, max(-(-total // amount), total * weights[0] // sum(weights)))
    least = 1 if total - largest >= amount - 1 else 0
    counts, rest = [largest] + [least] * (amount - 1), total - largest - least * (amount - 1)
    while rest > 0:
        free = [i for i in range(1, amount) if counts[i] < largest] or [i for i in range(1, amount) if counts[i] < limit]
        pool, left = sum([weights[i] for i in free]), rest
        for i in free:
            more = min(limit - counts[i], max(1, left * weights[i] // pool), rest)
            counts[i] = counts[i] + more
            rest = rest - more
    return np.array(counts)


def noise(own_key, extent, scale, reach, cuts=(), held_as=jnp.bfloat16):
    entries = scale * jax.random.normal(own_key, extent, jnp.float32)
    if cuts:
        entries = entries * steps_of(own_key, extent, cuts, -0.22, 0.18)
    return jnp.clip(entries, -reach, reach).astype(held_as)


def setup_inputs(seed: int = 0, part: int = 0) -> dict:
    arg_keys = jax.random.split(jax.random.key(seed), 13)
    part_splits = jax.random.split(jax.random.fold_in(arg_keys[12], part), 13)
    queries = draw_queries(jax.random.fold_in(jax.random.fold_in(arg_keys[12], part), 71), part)
    key_cache = draw_key_cache(jax.random.fold_in(jax.random.fold_in(arg_keys[12], part), 71), part)
    cached_value_rows = noise(part_splits[2], (MICROBATCH_COUNT, REQUEST_ROWS, CONTEXT_SLOTS, KEY_VALUE_HEADS, HEAD_WIDTH), 1.0, 5.0, ((1, 4), (3, 4)))
    lengths = draw_lengths(jax.random.fold_in(jax.random.fold_in(arg_keys[12], part), 71), part)
    residual = noise(part_splits[4], (MICROBATCH_COUNT, REQUEST_ROWS, D), 1.0, 6.0, ((1, 4), (2, 4)))
    w_out = noise(arg_keys[5], (QUERY_HEADS * HEAD_WIDTH, D), (QUERY_HEADS * HEAD_WIDTH) ** -0.5, 0.09375, ((0, 4), (1, 4)))
    norm_gain = jnp.clip(1.0 + 0.18 * jax.random.normal(arg_keys[6], (D,), jnp.float32), 0.1, 1.9)
    expert_ids_keys = jax.random.split(jax.random.fold_in(part_splits[7], 1), MICROBATCH_COUNT * REQUEST_ROWS // ROWS_DEV)
    expert_ids_turns = jax.random.permutation(jax.random.fold_in(part_splits[7], 3), MICROBATCH_COUNT * REQUEST_ROWS // ROWS_DEV)
    expert_ids = jax.vmap(lambda own, number: assign_block(jax.random.fold_in(part_splits[7], 2), own, number, ROWS_DEV, EXPERTS, TOP, CAP, 2))(expert_ids_keys, expert_ids_turns).reshape((MICROBATCH_COUNT, REQUEST_ROWS, TOP))
    route_weights = jnp.clip(jnp.exp(math.log(1.0) - 2.9957323 * jax.random.uniform(part_splits[8], (MICROBATCH_COUNT, REQUEST_ROWS, TOP), jnp.float32) ** steps_of(part_splits[8], (MICROBATCH_COUNT, REQUEST_ROWS, TOP), ((1, 4),), -0.2, 0.2)), 0.05, 1.0)
    w_gate = noise(arg_keys[9], (EXPERTS, D, FF), D ** -0.5, 0.125, ((0, 4), (2, 4)))
    w_up = noise(arg_keys[10], (EXPERTS, D, FF), D ** -0.5, 0.125, ((0, 4), (2, 4)))
    w_down = noise(arg_keys[11], (EXPERTS, FF, D), FF ** -0.5, 0.1875, ((0, 4), (1, 4)))
    return {"queries": queries, "key_cache": key_cache, "cached_value_rows": cached_value_rows, "lengths": lengths, "residual": residual, "w_out": w_out, "norm_gain": norm_gain, "expert_ids": expert_ids, "route_weights": route_weights, "w_gate": w_gate, "w_up": w_up, "w_down": w_down}


def rounded(value):
    return lax.optimization_barrier(value.astype(jnp.bfloat16)).astype(jnp.float32)

def reference(queries, key_cache, cached_value_rows, lengths, residual, w_out, norm_gain, expert_ids, route_weights, w_gate, w_up, w_down):
    query_group = QUERY_HEADS // KEY_VALUE_HEADS
    width = FF // N_NARROW
    outputs = []
    for index_values in range(MICROBATCH_COUNT):
        query_rows = queries[index_values].astype(jnp.float32).reshape(REQUEST_ROWS, KEY_VALUE_HEADS, query_group, HEAD_WIDTH)
        keys = key_cache[index_values].astype(jnp.float32)
        scores = jnp.einsum('rkgd,rckd->rkgc', query_rows, keys) / math.sqrt(HEAD_WIDTH)
        usable = jnp.arange(CONTEXT_SLOTS)[None, :] < lengths[index_values][:, None]
        scores = jnp.where(usable[:, None, None, :], scores, -1e+30)
        largest = lax.optimization_barrier(jnp.max(scores, axis=-1, keepdims=True))
        weight = jnp.exp(scores - largest)
        probs = (weight / lax.optimization_barrier(jnp.sum(weight, axis=-1, keepdims=True))).astype(jnp.bfloat16)
        attended = jnp.einsum('rkgc,rckd->rkgd', probs.astype(jnp.float32), cached_value_rows[index_values].astype(jnp.float32))
        attended = attended.astype(jnp.bfloat16).reshape(REQUEST_ROWS, QUERY_HEADS * HEAD_WIDTH)
        projected = jnp.dot(attended, w_out, preferred_element_type=jnp.float32)
        stream = (residual[index_values].astype(jnp.float32) + projected).astype(jnp.bfloat16)
        chosen = expert_ids[index_values]
        blocks = chosen.reshape(N_WIDE, ROWS_DEV * TOP)
        onehot = (blocks[:, :, None] == jnp.arange(EXPERTS, dtype=jnp.int32)[None, None, :]).astype(jnp.int32)
        rank = lax.optimization_barrier(jnp.sum(onehot * (jnp.cumsum(onehot, axis=1) - onehot), axis=-1))
        slot = (jnp.arange(N_WIDE, dtype=jnp.int32)[:, None] * CAP + rank).reshape(-1).astype(jnp.int32)
        owner = chosen.reshape(-1).astype(jnp.int32)
        source = jnp.repeat(jnp.arange(REQUEST_ROWS, dtype=jnp.int32), TOP)
        buffer = jnp.zeros((EXPERTS, N_WIDE * CAP, D), jnp.bfloat16).at[owner, slot].set(stream[source])
        values = buffer.astype(jnp.float32)
        square = lax.optimization_barrier(jnp.mean(values * values, axis=-1, keepdims=True))
        normed = (values * lax.rsqrt(square + 1e-06) * norm_gain).astype(jnp.bfloat16).astype(jnp.float32)
        gate = jnp.einsum('esd,edf->esf', normed, w_gate.astype(jnp.float32))
        upper = jnp.einsum('esd,edf->esf', normed, w_up.astype(jnp.float32))
        hidden = (jax.nn.silu(gate) * upper).astype(jnp.bfloat16).astype(jnp.float32)
        total = jnp.zeros((EXPERTS, N_WIDE * CAP, D), jnp.float32)
        for block in range(N_NARROW):
            term = jnp.einsum('esf,efd->esd', hidden[:, :, block * width:(block + 1) * width], w_down[:, block * width:(block + 1) * width, :].astype(jnp.float32))
            total = total + rounded(term)
        expert_out = total.astype(jnp.bfloat16)
        picked = expert_out[owner, slot].astype(jnp.float32).reshape(REQUEST_ROWS, TOP, D)
        mixed = lax.optimization_barrier(jnp.sum(picked * route_weights[index_values][:, :, None], axis=1))
        outputs.append((stream.astype(jnp.float32) + mixed).astype(jnp.bfloat16))
    return jnp.stack(outputs)
```

```python
import math

import jax
import jax.numpy as jnp
from jax import lax
from jax.experimental import pallas as pl
from jax.experimental.pallas import tpu as pltpu
from jax.sharding import PartitionSpec as P

EXPERTS = 64
CAP = 3


def attend(query_rows, keys, values, valid_len):
    row_count, q_heads, head_size = query_rows.shape
    slot_count = keys.shape[1]
    kv_heads = keys.shape[2]
    flat_keys = keys.reshape(row_count, slot_count, kv_heads * head_size)
    flat_values = values.reshape(row_count, slot_count, kv_heads * head_size)
    position = jnp.arange(slot_count)
    usable = position[None, :] < valid_len[:, None]
    scores = jnp.einsum(
        "rgd,rcd->rgc", query_rows, flat_keys, preferred_element_type=jnp.float32
    ) / math.sqrt(head_size)
    scores = jnp.where(usable[:, None, :], scores, -1e30)
    largest = jnp.max(scores, axis=-1, keepdims=True)
    weight = jnp.exp(scores - largest)
    probs = (weight / jnp.sum(weight, axis=-1, keepdims=True)).astype(jnp.bfloat16)
    mixed = jnp.einsum("rgc,rcd->rgd", probs, flat_values, preferred_element_type=jnp.float32)
    results = mixed.astype(jnp.bfloat16)
    return results.reshape(row_count, q_heads * head_size)


def route_tables(chosen, weights, expert_count, capacity):
    row_count, top_count = chosen.shape
    pairs = chosen.reshape(-1)
    onehot = (pairs[:, None] == jnp.arange(expert_count)[None, :]).astype(jnp.int32)
    before = jnp.cumsum(onehot, axis=0) - onehot
    rank = jnp.sum(onehot * before, axis=1)
    slot = pairs * capacity + rank
    select = (slot[:, None] == jnp.arange(expert_count * capacity)[None, :]).astype(jnp.float32)
    select = select.reshape(row_count, top_count, expert_count * capacity)
    dispatch = jnp.sum(select, axis=1).astype(jnp.bfloat16)
    combine = jnp.sum(select * weights[:, :, None], axis=1)
    return (dispatch, combine)


def expert_block(pieces, norm_gain, w_gate, w_up, w_down):
    parts_count = pieces.shape[0]
    local_experts, model_width, hidden_width = w_gate.shape
    part_width = model_width // parts_count
    values = pieces.astype(jnp.float32)
    square = jnp.mean(values * values, axis=(0, 4), keepdims=True)
    gain_parts = norm_gain.reshape(parts_count, 1, 1, 1, part_width)
    normed = (values * lax.rsqrt(square + 1e-06) * gain_parts).astype(jnp.bfloat16)
    gate_parts = w_gate.reshape(local_experts, parts_count, part_width, hidden_width)
    up_parts = w_up.reshape(local_experts, parts_count, part_width, hidden_width)
    gate = jnp.einsum("nsjcd,jndf->sjcf", normed, gate_parts, preferred_element_type=jnp.float32)
    upper = jnp.einsum("nsjcd,jndf->sjcf", normed, up_parts, preferred_element_type=jnp.float32)
    hidden = (jax.nn.silu(gate) * upper).astype(jnp.bfloat16)
    narrow_count = lax.axis_size("narrow")
    down_parts = w_down.reshape(
        local_experts, w_down.shape[1], narrow_count, model_width // narrow_count
    )
    partial_out = jnp.einsum(
        "sjcf,jfnd->nsjcd", hidden, down_parts, preferred_element_type=jnp.float32
    )
    summed = lax.psum_scatter(
        partial_out.astype(jnp.bfloat16), "narrow", scatter_dimension=0, tiled=True
    ).astype(jnp.float32)[0]
    return lax.all_to_all(
        summed.astype(jnp.bfloat16), "wide", split_axis=0, concat_axis=0, tiled=True
    )


def local(
    queries,
    key_cache,
    cached_value_rows,
    lengths,
    residual,
    w_out,
    norm_gain,
    expert_ids,
    route_weights,
    w_gate,
    w_up,
    w_down,
):
    micro_count = queries.shape[0]
    wide_count = lax.axis_size("wide")
    local_experts = w_gate.shape[0]
    capacity = CAP
    attended = [
        attend(
            queries[index_values],
            key_cache[index_values],
            cached_value_rows[index_values],
            lengths[index_values],
        )
        for index_values in range(micro_count)
    ]
    terms = []
    for index_values in range(micro_count):
        columns = jnp.dot(
            lax.all_gather(attended[index_values], "wide", axis=0, tiled=True),
            w_out,
            preferred_element_type=jnp.float32,
        )
        terms.append(
            lax.all_to_all(
                columns.astype(jnp.bfloat16), "wide", split_axis=0, concat_axis=1, tiled=True
            ).astype(columns.dtype)
        )
    partial_sum = jnp.stack(terms)
    projected = lax.psum_scatter(
        partial_sum.astype(jnp.bfloat16), "narrow", scatter_dimension=2, tiled=True
    ).astype(jnp.float32)
    stream = (residual.astype(jnp.float32) + projected).astype(jnp.bfloat16)
    outputs = []
    for index_values in range(micro_count):
        dispatch, combine = route_tables(
            expert_ids[index_values], route_weights[index_values], EXPERTS, capacity
        )
        packed = lax.dot_general(
            dispatch,
            stream[index_values],
            (((0,), (0,)), ((), ())),
            preferred_element_type=jnp.float32,
        )
        packed = packed.astype(jnp.bfloat16).reshape(
            wide_count, local_experts, capacity, stream.shape[2]
        )
        back = (
            lambda rows_in: expert_block(
                lax.all_gather(rows_in[None], "narrow", axis=0, tiled=True),
                norm_gain,
                w_gate,
                w_up,
                w_down,
            )
        )(lax.all_to_all(packed, "wide", split_axis=0, concat_axis=0, tiled=True))
        returned = back.reshape(wide_count * local_experts * capacity, back.shape[3]).astype(
            jnp.float32
        )
        mixed = jnp.dot(combine, returned, precision=lax.Precision.HIGHEST)
        outputs.append((stream[index_values].astype(jnp.float32) + mixed).astype(jnp.bfloat16))
    return jnp.stack(outputs)


def flip_permute(value, axis, mask):
    size = lax.axis_size(axis)
    return lax.ppermute(value, axis, [(i, i ^ mask) for i in range(size)])


def attend_kernel(len_ref, q_ref, k_ref, v_ref, ids_ref, wts_ref, out_ref, mixed_ref):
    rows, heads = out_ref.shape[0], q_ref.shape[0] // out_ref.shape[0]
    width = q_ref.shape[1]
    slots = k_ref.shape[0] // rows
    group = 256 // slots
    micro, per_micro = len_ref.shape
    row_request = lax.broadcasted_iota(jnp.int32, (group * heads, group * slots), 0) // heads
    column = lax.broadcasted_iota(jnp.int32, (group * heads, group * slots), 1)
    place = column - row_request * slots
    for g in range(rows // group):
        limit = jnp.zeros_like(place)
        for i in range(group):
            r = g * group + i
            limit = jnp.where(row_request == i, len_ref[r // per_micro, r % per_micro], limit)
        q = q_ref[g * group * heads:(g + 1) * group * heads, :]
        k = k_ref[g * group * slots:(g + 1) * group * slots, :]
        v = v_ref[g * group * slots:(g + 1) * group * slots, :]
        scores = lax.dot_general(
            q, k, (((1,), (1,)), ((), ())), preferred_element_type=jnp.float32
        ) * (1.0 / math.sqrt(width))
        usable = (place >= 0) & (place < limit)
        scores = jnp.where(usable, scores, -1e30)
        weight = jnp.exp(scores - jnp.max(scores, axis=-1, keepdims=True))
        probs = (weight / jnp.sum(weight, axis=-1, keepdims=True)).astype(jnp.bfloat16)
        mixed_ref[g * group * heads:(g + 1) * group * heads, :] = jnp.dot(
            probs, v, preferred_element_type=jnp.float32
        )
    for h in range(heads):
        out_ref[:, h * width:(h + 1) * width] = mixed_ref[
            pl.ds(h, rows, stride=heads), :
        ].astype(jnp.bfloat16)
    lanes = 64
    expert = lax.broadcasted_iota(jnp.int32, (lanes, per_micro), 0)
    eye = (
        lax.broadcasted_iota(jnp.int32, (per_micro, per_micro), 0)
        == lax.broadcasted_iota(jnp.int32, (per_micro, per_micro), 1)
    ).astype(jnp.bfloat16)
    for m in range(micro):
        total = jnp.zeros((lanes, per_micro), jnp.float32)
        for t in range(ids_ref.shape[1]):
            total += jnp.where(
                expert == ids_ref[m, t:t + 1, :], wts_ref[m, t:t + 1, :], 0.0
            )
        high = total.astype(jnp.bfloat16)
        low = (total - high.astype(jnp.float32)).astype(jnp.bfloat16)
        both = jnp.concatenate([high, low], axis=0)
        out_ref[m * per_micro:(m + 1) * per_micro, heads * width:] = lax.dot_general(
            eye, both, (((1,), (1,)), ((), ())), preferred_element_type=jnp.float32
        ).astype(jnp.bfloat16)


def project_kernel(where_ref, own_ref, got1_ref, got2_ref, got3_ref, w_ref, res_ref,
                   keep_ref, send_ref):
    wide, narrow = where_ref[0], where_ref[1]
    depth = w_ref.shape[0]
    half = keep_ref.shape[1]
    rows = own_ref.shape[0]
    features = jnp.concatenate(
        [r[:, :depth] for r in (own_ref, got1_ref, got2_ref, got3_ref)], axis=0
    )
    mine = pl.ds(pl.multiple_of((narrow & 1) * half, half), half)
    other = pl.ds(pl.multiple_of((1 - (narrow & 1)) * half, half), half)
    spot = pl.ds(pl.multiple_of((wide ^ narrow) * rows, rows), rows)
    keep_ref[...] = jnp.dot(features, w_ref[:, mine], preferred_element_type=jnp.float32)
    keep_ref[spot, :] += res_ref[:, mine].astype(jnp.float32)
    part = jnp.dot(features, w_ref[:, other], preferred_element_type=jnp.float32)
    part_rows = lax.broadcasted_iota(jnp.int32, part.shape, 0) // rows
    extra = res_ref[:, other].astype(jnp.float32)
    extra = jnp.concatenate([extra] * (part.shape[0] // rows), axis=0)
    part = jnp.where(part_rows == (wide ^ narrow), part + extra, part)
    send_ref[...] = part.astype(jnp.bfloat16)


def expert_kernel(where_ref, mine_ref, other_ref, cw0_ref, cw1_ref, cw2_ref, cw3_ref,
                  gain_ref, wg_ref, wu_ref, wd_ref, keep_ref, send_ref, stream_ref,
                  x_ref, hid_ref):
    wide, narrow = where_ref[0], where_ref[1]
    core = narrow & 1
    blocks, total, half = mine_ref.shape
    rows = total // blocks
    experts, depth, width = wg_ref.shape
    square = jnp.zeros((total, 1), jnp.float32)
    for s in range(blocks):
        for piece, side in ((mine_ref, core), (other_ref, 1 - core)):
            place = pl.multiple_of((wide ^ s) * (2 * half) + side * half, half)
            lifted = jnp.concatenate(
                [piece[s, (u ^ s) * rows:((u ^ s) + 1) * rows, :] for u in range(blocks)], axis=0
            )
            x_ref[:, pl.ds(place, half)] = lifted
            value = lifted.astype(jnp.float32)
            square += jnp.sum(value * value, axis=1, keepdims=True)
    own = pl.multiple_of(narrow * (2 * half), 2 * half)
    stream_ref[...] = x_ref[:rows, pl.ds(own, 2 * half)]
    scale = lax.rsqrt(square * (1.0 / depth) + 1e-6)
    for b in range(depth // 512):
        cols = slice(b * 512, (b + 1) * 512)
        x_ref[:, cols] = (
            x_ref[:, cols].astype(jnp.float32) * scale * gain_ref[:, cols]
        ).astype(jnp.bfloat16)
    mix = jnp.concatenate([r[...] for r in (cw0_ref, cw1_ref, cw2_ref, cw3_ref)], axis=0)
    lane = lax.broadcasted_iota(jnp.int32, (mix.shape[1], width), 0) % (mix.shape[1] // 2)

    def one(e, carry):
        gate = jnp.dot(x_ref[...], wg_ref[e], preferred_element_type=jnp.float32)
        upper = jnp.dot(x_ref[...], wu_ref[e], preferred_element_type=jnp.float32)
        pick = (lane == wide * experts + e).astype(jnp.bfloat16)
        share = jnp.dot(mix, pick, preferred_element_type=jnp.float32)
        hidden = gate / (1.0 + jnp.exp(-gate)) * upper * share
        hid_ref[:, pl.ds(pl.multiple_of(e * width, width), width)] = hidden.astype(jnp.bfloat16)
        return carry

    lax.fori_loop(0, experts, one, 0)
    block = 2 * half
    for j in (1, 3, 0, 2):
        out = jnp.dot(
            hid_ref[...],
            wd_ref[:, pl.ds(pl.multiple_of((narrow ^ j) * block, block), block)],
            preferred_element_type=jnp.float32,
        )
        target = send_ref if j & 1 else keep_ref
        target[:, (j >> 1) * block:((j >> 1) + 1) * block] = out.astype(target.dtype)


def local_small(
    queries,
    key_cache,
    cached_value_rows,
    lengths,
    residual,
    w_out,
    norm_gain,
    expert_ids,
    route_weights,
    w_gate,
    w_up,
    w_down,
):
    micro, per_micro, heads, width = queries.shape
    rows = micro * per_micro
    depth, columns = w_out.shape
    experts, model, hidden = w_gate.shape
    half = columns // 2
    vmem = pl.BlockSpec(memory_space=pltpu.VMEM)
    smem = pl.BlockSpec(memory_space=pltpu.SMEM)
    wide, narrow = lax.axis_index("wide"), lax.axis_index("narrow")
    where = jnp.stack([wide, narrow]).astype(jnp.int32)
    size = lax.axis_size("wide")
    turned = lax.ppermute(
        residual.reshape(rows, columns),
        ("wide", "narrow"),
        [(i, (i % size) * size + i // size) for i in range(size * size)],
    )
    payload = pl.pallas_call(
        attend_kernel,
        out_shape=jax.ShapeDtypeStruct((rows, depth + 128), jnp.bfloat16),
        in_specs=[smem] + [vmem] * 5,
        out_specs=vmem,
        scratch_shapes=[pltpu.VMEM((rows * heads, width), jnp.float32)],
        compiler_params=pltpu.CompilerParams(vmem_limit_bytes=8 * 2**20),
    )(
        lengths,
        queries.reshape(rows * heads, width),
        key_cache.reshape(-1, width),
        cached_value_rows.reshape(-1, width),
        expert_ids.transpose(0, 2, 1),
        route_weights.transpose(0, 2, 1),
    )
    others = [flip_permute(payload, "wide", s) for s in (1, 2, 3)]
    keep, send = pl.pallas_call(
        project_kernel,
        out_shape=(
            jax.ShapeDtypeStruct((size * rows, half), jnp.float32),
            jax.ShapeDtypeStruct((size * rows, half), jnp.bfloat16),
        ),
        in_specs=[smem] + [vmem] * 6,
        out_specs=(vmem, vmem),
        compiler_params=pltpu.CompilerParams(vmem_limit_bytes=8 * 2**20),
    )(where, payload, *others, w_out, turned)
    part = (keep + flip_permute(send, "narrow", 1).astype(jnp.float32)).astype(jnp.bfloat16)
    stream = (
        part.astype(jnp.float32) + flip_permute(part, "narrow", 2).astype(jnp.float32)
    ).astype(jnp.bfloat16)
    mine = jnp.stack([stream] + [flip_permute(stream, "wide", s) for s in (1, 2, 3)])
    other = flip_permute(mine, "narrow", 1)
    weights = [
        pltpu.with_memory_space_constraint(w, pltpu.VMEM)
        for w in (w_gate, w_up, w_down.reshape(experts * hidden, model))
    ]
    keep, send, own = pl.pallas_call(
        expert_kernel,
        out_shape=(
            jax.ShapeDtypeStruct((size * rows, model // 2), jnp.float32),
            jax.ShapeDtypeStruct((size * rows, model // 2), jnp.bfloat16),
            jax.ShapeDtypeStruct((rows, columns), jnp.bfloat16),
        ),
        in_specs=[smem] + [vmem] * 10,
        out_specs=(vmem, vmem, vmem),
        scratch_shapes=[
            pltpu.VMEM((size * rows, model), jnp.bfloat16),
            pltpu.VMEM((size * rows, experts * hidden), jnp.bfloat16),
        ],
        compiler_params=pltpu.CompilerParams(vmem_limit_bytes=12 * 2**20),
    )(
        where,
        mine,
        other,
        *[p[:, depth:] for p in [payload] + others],
        norm_gain.reshape(1, model),
        *weights,
    )
    total = keep + flip_permute(send, "narrow", 1).astype(jnp.float32)
    total = total.reshape(size, rows, model // 2)
    leave = total[1:].astype(jnp.bfloat16)
    summed = total[0]
    for s in (1, 2, 3):
        summed = summed + flip_permute(leave[s - 1], "wide", s).astype(jnp.float32)
    cross = flip_permute(summed[:, columns:].astype(jnp.bfloat16), "narrow", 2)
    result = own.astype(jnp.float32) + summed[:, :columns] + cross.astype(jnp.float32)
    return result.astype(jnp.bfloat16).reshape(micro, per_micro, columns)


def solution(mesh):
    in_specs = (
        P(None, ("grp", "wide"), "narrow", None),
        P(None, ("grp", "wide"), None, "narrow", None),
        P(None, ("grp", "wide"), None, "narrow", None),
        P(None, ("grp", "wide")),
        P(None, ("grp", "wide"), "narrow"),
        P("narrow", "wide"),
        P(),
        P(None, ("grp", "wide"), None),
        P(None, ("grp", "wide"), None),
        P("wide", None, "narrow"),
        P("wide", None, "narrow"),
        P("wide", "narrow", None),
    )
    out_specs = P(None, ("grp", "wide"), "narrow")
    small = mesh.shape["wide"] == 4 and mesh.shape["narrow"] == 4
    body = local_small if small else local
    return jax.shard_map(body, mesh=mesh, in_specs=in_specs, out_specs=out_specs, check_vma=False)
```

```python
import math

import jax
import jax.numpy as jnp
from jax import lax
from jax.experimental import pallas as pl
from jax.experimental.pallas import tpu as pltpu
from jax.sharding import PartitionSpec as P

EXPERTS = 64
CAP = 3


def attend(query_rows, keys, values, valid_len):
    row_count, q_heads, head_size = query_rows.shape
    slot_count = keys.shape[1]
    kv_heads = keys.shape[2]
    flat_keys = keys.reshape(row_count, slot_count, kv_heads * head_size)
    flat_values = values.reshape(row_count, slot_count, kv_heads * head_size)
    position = jnp.arange(slot_count)
    usable = position[None, :] < valid_len[:, None]
    scores = jnp.einsum(
        "rgd,rcd->rgc", query_rows, flat_keys, preferred_element_type=jnp.float32
    ) / math.sqrt(head_size)
    scores = jnp.where(usable[:, None, :], scores, -1e30)
    largest = jnp.max(scores, axis=-1, keepdims=True)
    weight = jnp.exp(scores - largest)
    probs = (weight / jnp.sum(weight, axis=-1, keepdims=True)).astype(jnp.bfloat16)
    mixed = jnp.einsum("rgc,rcd->rgd", probs, flat_values, preferred_element_type=jnp.float32)
    results = mixed.astype(jnp.bfloat16)
    return results.reshape(row_count, q_heads * head_size)


def route_tables(chosen, weights, expert_count, capacity):
    row_count, top_count = chosen.shape
    pairs = chosen.reshape(-1)
    onehot = (pairs[:, None] == jnp.arange(expert_count)[None, :]).astype(jnp.int32)
    before = jnp.cumsum(onehot, axis=0) - onehot
    rank = jnp.sum(onehot * before, axis=1)
    slot = pairs * capacity + rank
    select = (slot[:, None] == jnp.arange(expert_count * capacity)[None, :]).astype(jnp.float32)
    select = select.reshape(row_count, top_count, expert_count * capacity)
    dispatch = jnp.sum(select, axis=1).astype(jnp.bfloat16)
    combine = jnp.sum(select * weights[:, :, None], axis=1)
    return (dispatch, combine)


def expert_block(pieces, norm_gain, w_gate, w_up, w_down):
    parts_count = pieces.shape[0]
    local_experts, model_width, hidden_width = w_gate.shape
    part_width = model_width // parts_count
    values = pieces.astype(jnp.float32)
    square = jnp.mean(values * values, axis=(0, 4), keepdims=True)
    gain_parts = norm_gain.reshape(parts_count, 1, 1, 1, part_width)
    normed = (values * lax.rsqrt(square + 1e-06) * gain_parts).astype(jnp.bfloat16)
    gate_parts = w_gate.reshape(local_experts, parts_count, part_width, hidden_width)
    up_parts = w_up.reshape(local_experts, parts_count, part_width, hidden_width)
    gate = jnp.einsum("nsjcd,jndf->sjcf", normed, gate_parts, preferred_element_type=jnp.float32)
    upper = jnp.einsum("nsjcd,jndf->sjcf", normed, up_parts, preferred_element_type=jnp.float32)
    hidden = (jax.nn.silu(gate) * upper).astype(jnp.bfloat16)
    narrow_count = lax.axis_size("narrow")
    down_parts = w_down.reshape(
        local_experts, w_down.shape[1], narrow_count, model_width // narrow_count
    )
    partial_out = jnp.einsum(
        "sjcf,jfnd->nsjcd", hidden, down_parts, preferred_element_type=jnp.float32
    )
    summed = lax.psum_scatter(
        partial_out.astype(jnp.bfloat16), "narrow", scatter_dimension=0, tiled=True
    ).astype(jnp.float32)[0]
    return lax.all_to_all(
        summed.astype(jnp.bfloat16), "wide", split_axis=0, concat_axis=0, tiled=True
    )


def local(
    queries,
    key_cache,
    cached_value_rows,
    lengths,
    residual,
    w_out,
    norm_gain,
    expert_ids,
    route_weights,
    w_gate,
    w_up,
    w_down,
):
    micro_count = queries.shape[0]
    wide_count = lax.axis_size("wide")
    local_experts = w_gate.shape[0]
    capacity = CAP
    attended = [
        attend(
            queries[index_values],
            key_cache[index_values],
            cached_value_rows[index_values],
            lengths[index_values],
        )
        for index_values in range(micro_count)
    ]
    terms = []
    for index_values in range(micro_count):
        columns = jnp.dot(
            lax.all_gather(attended[index_values], "wide", axis=0, tiled=True),
            w_out,
            preferred_element_type=jnp.float32,
        )
        terms.append(
            lax.all_to_all(
                columns.astype(jnp.bfloat16), "wide", split_axis=0, concat_axis=1, tiled=True
            ).astype(columns.dtype)
        )
    partial_sum = jnp.stack(terms)
    projected = lax.psum_scatter(
        partial_sum.astype(jnp.bfloat16), "narrow", scatter_dimension=2, tiled=True
    ).astype(jnp.float32)
    stream = (residual.astype(jnp.float32) + projected).astype(jnp.bfloat16)
    outputs = []
    for index_values in range(micro_count):
        dispatch, combine = route_tables(
            expert_ids[index_values], route_weights[index_values], EXPERTS, capacity
        )
        packed = lax.dot_general(
            dispatch,
            stream[index_values],
            (((0,), (0,)), ((), ())),
            preferred_element_type=jnp.float32,
        )
        packed = packed.astype(jnp.bfloat16).reshape(
            wide_count, local_experts, capacity, stream.shape[2]
        )
        back = (
            lambda rows_in: expert_block(
                lax.all_gather(rows_in[None], "narrow", axis=0, tiled=True),
                norm_gain,
                w_gate,
                w_up,
                w_down,
            )
        )(lax.all_to_all(packed, "wide", split_axis=0, concat_axis=0, tiled=True))
        returned = back.reshape(wide_count * local_experts * capacity, back.shape[3]).astype(
            jnp.float32
        )
        mixed = jnp.dot(combine, returned, precision=lax.Precision.HIGHEST)
        outputs.append((stream[index_values].astype(jnp.float32) + mixed).astype(jnp.bfloat16))
    return jnp.stack(outputs)


def flip_permute(value, axis, mask):
    size = lax.axis_size(axis)
    return lax.ppermute(value, axis, [(i, i ^ mask) for i in range(size)])


def attend_kernel(*refs):
    given, out_ref, mixed_ref, held, sems = refs[:6], refs[6], refs[7], refs[8:14], refs[14]
    copies = [
        pltpu.make_async_copy(source, target, sems.at[i])
        for i, (source, target) in enumerate(zip(given, held))
    ]
    for copy in copies:
        copy.start()
    for copy in copies:
        copy.wait()
    len_ref, q_ref, k_ref, v_ref, ids_ref, wts_ref = held
    rows, heads = out_ref.shape[0], q_ref.shape[0] // out_ref.shape[0]
    width = q_ref.shape[1]
    slots = k_ref.shape[0] // rows
    group = 256 // slots
    micro, per_micro = len_ref.shape
    row_request = lax.broadcasted_iota(jnp.int32, (group * heads, group * slots), 0) // heads
    column = lax.broadcasted_iota(jnp.int32, (group * heads, group * slots), 1)
    place = column - row_request * slots
    for g in range(rows // group):
        limit = jnp.zeros_like(place)
        for i in range(group):
            r = g * group + i
            limit = jnp.where(row_request == i, len_ref[r // per_micro, r % per_micro], limit)
        q = q_ref[g * group * heads:(g + 1) * group * heads, :]
        k = k_ref[g * group * slots:(g + 1) * group * slots, :]
        v = v_ref[g * group * slots:(g + 1) * group * slots, :]
        scores = lax.dot_general(
            q, k, (((1,), (1,)), ((), ())), preferred_element_type=jnp.float32
        ) * (1.0 / math.sqrt(width))
        usable = (place >= 0) & (place < limit)
        scores = jnp.where(usable, scores, -1e30)
        weight = jnp.exp(scores - jnp.max(scores, axis=-1, keepdims=True))
        probs = (weight / jnp.sum(weight, axis=-1, keepdims=True)).astype(jnp.bfloat16)
        mixed_ref[g * group * heads:(g + 1) * group * heads, :] = jnp.dot(
            probs, v, preferred_element_type=jnp.float32
        )
    for h in range(heads):
        out_ref[:, h * width:(h + 1) * width] = mixed_ref[
            pl.ds(h, rows, stride=heads), :
        ].astype(jnp.bfloat16)
    lanes = 64
    expert = lax.broadcasted_iota(jnp.int32, (lanes, per_micro), 0)
    eye = (
        lax.broadcasted_iota(jnp.int32, (per_micro, per_micro), 0)
        == lax.broadcasted_iota(jnp.int32, (per_micro, per_micro), 1)
    ).astype(jnp.bfloat16)
    for m in range(micro):
        total = jnp.zeros((lanes, per_micro), jnp.float32)
        for t in range(ids_ref.shape[1]):
            total += jnp.where(
                expert == ids_ref[m, t:t + 1, :], wts_ref[m, t:t + 1, :], 0.0
            )
        high = total.astype(jnp.bfloat16)
        low = (total - high.astype(jnp.float32)).astype(jnp.bfloat16)
        both = jnp.concatenate([high, low], axis=0)
        out_ref[m * per_micro:(m + 1) * per_micro, heads * width:] = lax.dot_general(
            eye, both, (((1,), (1,)), ((), ())), preferred_element_type=jnp.float32
        ).astype(jnp.bfloat16)


def project_kernel(where_ref, own_ref, got1_ref, got2_ref, got3_ref, w_ref, res_ref,
                   keep_ref, send_ref):
    wide, narrow = where_ref[0], where_ref[1]
    depth = w_ref.shape[0]
    half = keep_ref.shape[1]
    rows = own_ref.shape[0]
    features = jnp.concatenate(
        [r[:, :depth] for r in (own_ref, got1_ref, got2_ref, got3_ref)], axis=0
    )
    mine = pl.ds(pl.multiple_of((narrow & 1) * half, half), half)
    other = pl.ds(pl.multiple_of((1 - (narrow & 1)) * half, half), half)
    spot = pl.ds(pl.multiple_of((wide ^ narrow) * rows, rows), rows)
    keep_ref[...] = jnp.dot(features, w_ref[:, mine], preferred_element_type=jnp.float32)
    keep_ref[spot, :] += res_ref[:, mine].astype(jnp.float32)
    part = jnp.dot(features, w_ref[:, other], preferred_element_type=jnp.float32)
    part_rows = lax.broadcasted_iota(jnp.int32, part.shape, 0) // rows
    extra = res_ref[:, other].astype(jnp.float32)
    extra = jnp.concatenate([extra] * (part.shape[0] // rows), axis=0)
    part = jnp.where(part_rows == (wide ^ narrow), part + extra, part)
    send_ref[...] = part.astype(jnp.bfloat16)


def expert_kernel(where_ref, mine_ref, other_ref, cw0_ref, cw1_ref, cw2_ref, cw3_ref,
                  gain_ref, wg_ref, wu_ref, wd_ref, keep_ref, send_ref, stream_ref,
                  x_ref, hid_ref):
    wide, narrow = where_ref[0], where_ref[1]
    core = narrow & 1
    blocks, total, half = mine_ref.shape
    rows = total // blocks
    experts, depth, width = wg_ref.shape
    square = jnp.zeros((total, 1), jnp.float32)
    for s in range(blocks):
        for piece, side in ((mine_ref, core), (other_ref, 1 - core)):
            place = pl.multiple_of((wide ^ s) * (2 * half) + side * half, half)
            lifted = jnp.concatenate(
                [piece[s, (u ^ s) * rows:((u ^ s) + 1) * rows, :] for u in range(blocks)], axis=0
            )
            x_ref[:, pl.ds(place, half)] = lifted
            value = lifted.astype(jnp.float32)
            square += jnp.sum(value * value, axis=1, keepdims=True)
    own = pl.multiple_of(narrow * (2 * half), 2 * half)
    stream_ref[...] = x_ref[:rows, pl.ds(own, 2 * half)]
    scale = lax.rsqrt(square * (1.0 / depth) + 1e-6)
    for b in range(depth // 512):
        cols = slice(b * 512, (b + 1) * 512)
        x_ref[:, cols] = (
            x_ref[:, cols].astype(jnp.float32) * scale * gain_ref[:, cols]
        ).astype(jnp.bfloat16)
    mix = jnp.concatenate([r[:, -128:] for r in (cw0_ref, cw1_ref, cw2_ref, cw3_ref)], axis=0)
    lane = lax.broadcasted_iota(jnp.int32, (mix.shape[1], width), 0) % (mix.shape[1] // 2)

    def one(e, carry):
        gate = jnp.dot(x_ref[...], wg_ref[e], preferred_element_type=jnp.float32)
        upper = jnp.dot(x_ref[...], wu_ref[e], preferred_element_type=jnp.float32)
        pick = (lane == wide * experts + e).astype(jnp.bfloat16)
        share = jnp.dot(mix, pick, preferred_element_type=jnp.float32)
        hidden = gate / (1.0 + jnp.exp(-gate)) * upper * share
        hid_ref[:, pl.ds(pl.multiple_of(e * width, width), width)] = hidden.astype(jnp.bfloat16)
        return carry

    lax.fori_loop(0, experts, one, 0)
    block = 2 * half
    for j in (1, 3, 0, 2):
        out = jnp.dot(
            hid_ref[...],
            wd_ref[:, pl.ds(pl.multiple_of((narrow ^ j) * block, block), block)],
            preferred_element_type=jnp.float32,
        )
        target = send_ref if j & 1 else keep_ref
        target[:, (j >> 1) * block:((j >> 1) + 1) * block] = out.astype(target.dtype)


def local_small(
    queries,
    key_cache,
    cached_value_rows,
    lengths,
    residual,
    w_out,
    norm_gain,
    expert_ids,
    route_weights,
    w_gate,
    w_up,
    w_down,
):
    micro, per_micro, heads, width = queries.shape
    rows = micro * per_micro
    depth, columns = w_out.shape
    experts, model, hidden = w_gate.shape
    half = columns // 2
    vmem = pl.BlockSpec(memory_space=pltpu.VMEM)
    smem = pl.BlockSpec(memory_space=pltpu.SMEM)
    wide, narrow = lax.axis_index("wide"), lax.axis_index("narrow")
    where = jnp.stack([wide, narrow]).astype(jnp.int32)
    size = lax.axis_size("wide")
    turned = lax.ppermute(
        residual.reshape(rows, columns),
        ("wide", "narrow"),
        [(i, (i % size) * size + i // size) for i in range(size * size)],
    )
    given = (
        lengths,
        queries.reshape(rows * heads, width),
        key_cache.reshape(-1, width),
        cached_value_rows.reshape(-1, width),
        expert_ids.transpose(0, 2, 1),
        route_weights.transpose(0, 2, 1),
    )
    payload = pl.pallas_call(
        attend_kernel,
        out_shape=jax.ShapeDtypeStruct((rows, depth + 128), jnp.bfloat16),
        in_specs=[pl.BlockSpec(memory_space=pl.ANY)] * 6,
        out_specs=vmem,
        scratch_shapes=[pltpu.VMEM((rows * heads, width), jnp.float32)]
        + [pltpu.SMEM(given[0].shape, given[0].dtype)]
        + [pltpu.VMEM(g.shape, g.dtype) for g in given[1:]]
        + [pltpu.SemaphoreType.DMA((6,))],
        cost_estimate=pl.CostEstimate(flops=2 * 10**10, bytes_accessed=10**8, transcendentals=0),
        compiler_params=pltpu.CompilerParams(vmem_limit_bytes=6 * 2**20),
    )(*[pltpu.with_memory_space_constraint(g, pltpu.HBM) for g in given])
    others = [flip_permute(payload, "wide", s) for s in (1, 2, 3)]
    keep, send = pl.pallas_call(
        project_kernel,
        out_shape=(
            jax.ShapeDtypeStruct((size * rows, half), jnp.float32),
            jax.ShapeDtypeStruct((size * rows, half), jnp.bfloat16),
        ),
        in_specs=[smem] + [vmem] * 6,
        out_specs=(vmem, vmem),
        cost_estimate=pl.CostEstimate(flops=2 * 10**10, bytes_accessed=10**8, transcendentals=0),
        compiler_params=pltpu.CompilerParams(vmem_limit_bytes=6 * 2**20),
    )(where, payload, *others, w_out, turned)
    part = (keep + flip_permute(send, "narrow", 1).astype(jnp.float32)).astype(jnp.bfloat16)
    stream = (
        part.astype(jnp.float32) + flip_permute(part, "narrow", 2).astype(jnp.float32)
    ).astype(jnp.bfloat16)
    mine = jnp.stack([stream] + [flip_permute(stream, "wide", s) for s in (1, 2, 3)])
    other = flip_permute(mine, "narrow", 1)
    weights = [
        pltpu.with_memory_space_constraint(w, pltpu.VMEM)
        for w in (w_gate, w_up, w_down.reshape(experts * hidden, model))
    ]
    keep, send, own = pl.pallas_call(
        expert_kernel,
        out_shape=(
            jax.ShapeDtypeStruct((size * rows, model // 2), jnp.float32),
            jax.ShapeDtypeStruct((size * rows, model // 2), jnp.bfloat16),
            jax.ShapeDtypeStruct((rows, columns), jnp.bfloat16),
        ),
        in_specs=[smem] + [vmem] * 10,
        out_specs=(vmem, vmem, vmem),
        scratch_shapes=[
            pltpu.VMEM((size * rows, model), jnp.bfloat16),
            pltpu.VMEM((size * rows, experts * hidden), jnp.bfloat16),
        ],
        compiler_params=pltpu.CompilerParams(vmem_limit_bytes=12 * 2**20),
    )(
        where,
        mine,
        other,
        payload,
        *others,
        norm_gain.reshape(1, model),
        *weights,
    )
    total = keep + flip_permute(send, "narrow", 1).astype(jnp.float32)
    total = total.reshape(size, rows, model // 2)
    leave = total[1:].astype(jnp.bfloat16)
    summed = total[0]
    for s in (1, 2, 3):
        summed = summed + flip_permute(leave[s - 1], "wide", s).astype(jnp.float32)
    cross = flip_permute(summed[:, columns:].astype(jnp.bfloat16), "narrow", 2)
    result = own.astype(jnp.float32) + summed[:, :columns] + cross.astype(jnp.float32)
    return result.astype(jnp.bfloat16).reshape(micro, per_micro, columns)


def solution(mesh):
    in_specs = (
        P(None, ("grp", "wide"), "narrow", None),
        P(None, ("grp", "wide"), None, "narrow", None),
        P(None, ("grp", "wide"), None, "narrow", None),
        P(None, ("grp", "wide")),
        P(None, ("grp", "wide"), "narrow"),
        P("narrow", "wide"),
        P(),
        P(None, ("grp", "wide"), None),
        P(None, ("grp", "wide"), None),
        P("wide", None, "narrow"),
        P("wide", None, "narrow"),
        P("wide", "narrow", None),
    )
    out_specs = P(None, ("grp", "wide"), "narrow")
    small = mesh.shape["wide"] == 4 and mesh.shape["narrow"] == 4
    body = local_small if small else local
    return jax.shard_map(body, mesh=mesh, in_specs=in_specs, out_specs=out_specs, check_vma=False)
```

```python
import math

import jax
import jax.numpy as jnp
from jax import lax
from jax.experimental import pallas as pl
from jax.experimental.pallas import tpu as pltpu
from jax.sharding import PartitionSpec as P

EXPERTS = 64
CAP = 3


def attend(query_rows, keys, values, valid_len):
    row_count, q_heads, head_size = query_rows.shape
    slot_count = keys.shape[1]
    kv_heads = keys.shape[2]
    flat_keys = keys.reshape(row_count, slot_count, kv_heads * head_size)
    flat_values = values.reshape(row_count, slot_count, kv_heads * head_size)
    position = jnp.arange(slot_count)
    usable = position[None, :] < valid_len[:, None]
    scores = jnp.einsum(
        "rgd,rcd->rgc", query_rows, flat_keys, preferred_element_type=jnp.float32
    ) / math.sqrt(head_size)
    scores = jnp.where(usable[:, None, :], scores, -1e30)
    largest = jnp.max(scores, axis=-1, keepdims=True)
    weight = jnp.exp(scores - largest)
    probs = (weight / jnp.sum(weight, axis=-1, keepdims=True)).astype(jnp.bfloat16)
    mixed = jnp.einsum("rgc,rcd->rgd", probs, flat_values, preferred_element_type=jnp.float32)
    results = mixed.astype(jnp.bfloat16)
    return results.reshape(row_count, q_heads * head_size)


def route_tables(chosen, weights, expert_count, capacity):
    row_count, top_count = chosen.shape
    pairs = chosen.reshape(-1)
    onehot = (pairs[:, None] == jnp.arange(expert_count)[None, :]).astype(jnp.int32)
    before = jnp.cumsum(onehot, axis=0) - onehot
    rank = jnp.sum(onehot * before, axis=1)
    slot = pairs * capacity + rank
    select = (slot[:, None] == jnp.arange(expert_count * capacity)[None, :]).astype(jnp.float32)
    select = select.reshape(row_count, top_count, expert_count * capacity)
    dispatch = jnp.sum(select, axis=1).astype(jnp.bfloat16)
    combine = jnp.sum(select * weights[:, :, None], axis=1)
    return (dispatch, combine)


def expert_block(pieces, norm_gain, w_gate, w_up, w_down):
    parts_count = pieces.shape[0]
    local_experts, model_width, hidden_width = w_gate.shape
    part_width = model_width // parts_count
    values = pieces.astype(jnp.float32)
    square = jnp.mean(values * values, axis=(0, 4), keepdims=True)
    gain_parts = norm_gain.reshape(parts_count, 1, 1, 1, part_width)
    normed = (values * lax.rsqrt(square + 1e-06) * gain_parts).astype(jnp.bfloat16)
    gate_parts = w_gate.reshape(local_experts, parts_count, part_width, hidden_width)
    up_parts = w_up.reshape(local_experts, parts_count, part_width, hidden_width)
    gate = jnp.einsum("nsjcd,jndf->sjcf", normed, gate_parts, preferred_element_type=jnp.float32)
    upper = jnp.einsum("nsjcd,jndf->sjcf", normed, up_parts, preferred_element_type=jnp.float32)
    hidden = (jax.nn.silu(gate) * upper).astype(jnp.bfloat16)
    narrow_count = lax.axis_size("narrow")
    down_parts = w_down.reshape(
        local_experts, w_down.shape[1], narrow_count, model_width // narrow_count
    )
    partial_out = jnp.einsum(
        "sjcf,jfnd->nsjcd", hidden, down_parts, preferred_element_type=jnp.float32
    )
    summed = lax.psum_scatter(
        partial_out.astype(jnp.bfloat16), "narrow", scatter_dimension=0, tiled=True
    ).astype(jnp.float32)[0]
    return lax.all_to_all(
        summed.astype(jnp.bfloat16), "wide", split_axis=0, concat_axis=0, tiled=True
    )


def local(
    queries,
    key_cache,
    cached_value_rows,
    lengths,
    residual,
    w_out,
    norm_gain,
    expert_ids,
    route_weights,
    w_gate,
    w_up,
    w_down,
):
    micro_count = queries.shape[0]
    wide_count = lax.axis_size("wide")
    local_experts = w_gate.shape[0]
    capacity = CAP
    attended = [
        attend(
            queries[index_values],
            key_cache[index_values],
            cached_value_rows[index_values],
            lengths[index_values],
        )
        for index_values in range(micro_count)
    ]
    terms = []
    for index_values in range(micro_count):
        columns = jnp.dot(
            lax.all_gather(attended[index_values], "wide", axis=0, tiled=True),
            w_out,
            preferred_element_type=jnp.float32,
        )
        terms.append(
            lax.all_to_all(
                columns.astype(jnp.bfloat16), "wide", split_axis=0, concat_axis=1, tiled=True
            ).astype(columns.dtype)
        )
    partial_sum = jnp.stack(terms)
    projected = lax.psum_scatter(
        partial_sum.astype(jnp.bfloat16), "narrow", scatter_dimension=2, tiled=True
    ).astype(jnp.float32)
    stream = (residual.astype(jnp.float32) + projected).astype(jnp.bfloat16)
    outputs = []
    for index_values in range(micro_count):
        dispatch, combine = route_tables(
            expert_ids[index_values], route_weights[index_values], EXPERTS, capacity
        )
        packed = lax.dot_general(
            dispatch,
            stream[index_values],
            (((0,), (0,)), ((), ())),
            preferred_element_type=jnp.float32,
        )
        packed = packed.astype(jnp.bfloat16).reshape(
            wide_count, local_experts, capacity, stream.shape[2]
        )
        back = (
            lambda rows_in: expert_block(
                lax.all_gather(rows_in[None], "narrow", axis=0, tiled=True),
                norm_gain,
                w_gate,
                w_up,
                w_down,
            )
        )(lax.all_to_all(packed, "wide", split_axis=0, concat_axis=0, tiled=True))
        returned = back.reshape(wide_count * local_experts * capacity, back.shape[3]).astype(
            jnp.float32
        )
        mixed = jnp.dot(combine, returned, precision=lax.Precision.HIGHEST)
        outputs.append((stream[index_values].astype(jnp.float32) + mixed).astype(jnp.bfloat16))
    return jnp.stack(outputs)


def flip_permute(value, axis, mask):
    size = lax.axis_size(axis)
    return lax.ppermute(value, axis, [(i, i ^ mask) for i in range(size)])


def spread(value):
    got = {s: flip_permute(value, "wide", s) for s in (1, 3, 2)}
    return [got[1], got[2], got[3]]


def attend_kernel(*refs):
    given, out_ref, mixed_ref, held, sems = refs[:6], refs[6], refs[7], refs[8:14], refs[14]
    copies = [
        pltpu.make_async_copy(source, target, sems.at[i])
        for i, (source, target) in enumerate(zip(given, held))
    ]
    for copy in copies:
        copy.start()
    for copy in copies:
        copy.wait()
    len_ref, q_ref, k_ref, v_ref, ids_ref, wts_ref = held
    rows, heads = out_ref.shape[0], q_ref.shape[0] // out_ref.shape[0]
    width = q_ref.shape[1]
    slots = k_ref.shape[0] // rows
    group = 256 // slots
    micro, per_micro = len_ref.shape
    row_request = lax.broadcasted_iota(jnp.int32, (group * heads, group * slots), 0) // heads
    column = lax.broadcasted_iota(jnp.int32, (group * heads, group * slots), 1)
    place = column - row_request * slots
    scores = []
    limits = []
    for g in range(rows // group):
        limit = jnp.zeros_like(place)
        for i in range(group):
            r = g * group + i
            limit = jnp.where(row_request == i, len_ref[r // per_micro, r % per_micro], limit)
        limits.append(limit)
        scores.append(
            lax.dot_general(
                q_ref[g * group * heads:(g + 1) * group * heads, :],
                k_ref[g * group * slots:(g + 1) * group * slots, :],
                (((1,), (1,)), ((), ())),
                preferred_element_type=jnp.float32,
            )
        )
    place = jnp.concatenate([place] * len(scores), axis=0)
    usable = (place >= 0) & (place < jnp.concatenate(limits, axis=0))
    scores = jnp.concatenate(scores, axis=0) * (1.0 / math.sqrt(width))
    scores = jnp.where(usable, scores, -1e30)
    weight = jnp.exp(scores - jnp.max(scores, axis=-1, keepdims=True))
    probs = (weight / jnp.sum(weight, axis=-1, keepdims=True)).astype(jnp.bfloat16)
    for g in range(rows // group):
        mixed_ref[g * group * heads:(g + 1) * group * heads, :] = jnp.dot(
            probs[g * group * heads:(g + 1) * group * heads, :],
            v_ref[g * group * slots:(g + 1) * group * slots, :],
            preferred_element_type=jnp.float32,
        )
    for h in range(heads):
        out_ref[:, h * width:(h + 1) * width] = mixed_ref[
            pl.ds(h, rows, stride=heads), :
        ].astype(jnp.bfloat16)
    lanes = 64
    expert = lax.broadcasted_iota(jnp.int32, (lanes, per_micro), 0)
    eye = (
        lax.broadcasted_iota(jnp.int32, (per_micro, per_micro), 0)
        == lax.broadcasted_iota(jnp.int32, (per_micro, per_micro), 1)
    ).astype(jnp.bfloat16)
    for m in range(micro):
        total = jnp.zeros((lanes, per_micro), jnp.float32)
        for t in range(ids_ref.shape[1]):
            total += jnp.where(
                expert == ids_ref[m, t:t + 1, :], wts_ref[m, t:t + 1, :], 0.0
            )
        high = total.astype(jnp.bfloat16)
        low = (total - high.astype(jnp.float32)).astype(jnp.bfloat16)
        both = jnp.concatenate([high, low], axis=0)
        out_ref[m * per_micro:(m + 1) * per_micro, heads * width:] = lax.dot_general(
            eye, both, (((1,), (1,)), ((), ())), preferred_element_type=jnp.float32
        ).astype(jnp.bfloat16)


def project_kernel(where_ref, own_ref, got1_ref, got2_ref, got3_ref, w_ref, res_ref,
                   keep_ref, send_ref):
    wide, narrow = where_ref[0], where_ref[1]
    depth = w_ref.shape[0]
    half = keep_ref.shape[1]
    rows = own_ref.shape[0]
    features = jnp.concatenate(
        [r[:, :depth] for r in (own_ref, got1_ref, got2_ref, got3_ref)], axis=0
    )
    mine = pl.ds(pl.multiple_of((narrow & 1) * half, half), half)
    other = pl.ds(pl.multiple_of((1 - (narrow & 1)) * half, half), half)
    spot = pl.ds(pl.multiple_of((wide ^ narrow) * rows, rows), rows)
    keep_ref[...] = jnp.dot(features, w_ref[:, mine], preferred_element_type=jnp.float32)
    keep_ref[spot, :] += res_ref[:, mine].astype(jnp.float32)
    part = jnp.dot(features, w_ref[:, other], preferred_element_type=jnp.float32)
    part_rows = lax.broadcasted_iota(jnp.int32, part.shape, 0) // rows
    extra = res_ref[:, other].astype(jnp.float32)
    extra = jnp.concatenate([extra] * (part.shape[0] // rows), axis=0)
    part = jnp.where(part_rows == (wide ^ narrow), part + extra, part)
    send_ref[...] = part.astype(jnp.bfloat16)


def expert_kernel(where_ref, mine_ref, other_ref, cw0_ref, cw1_ref, cw2_ref, cw3_ref,
                  gain_ref, wg_ref, wu_ref, wd_ref, keep_ref, send_ref, stream_ref,
                  x_ref, hid_ref, down_ref, sems):
    wide, narrow = where_ref[0], where_ref[1]
    core = narrow & 1
    blocks, total, half = mine_ref.shape
    rows = total // blocks
    experts, depth, width = wg_ref.shape
    block = 2 * half
    order = (1, 3, 0, 2)

    def fetch(i):
        start = pl.multiple_of((narrow ^ order[i]) * block, block)
        slot = i % down_ref.shape[0]
        return pltpu.make_async_copy(
            wd_ref.at[:, pl.ds(start, block)], down_ref.at[slot], sems.at[slot]
        )

    for i in range(down_ref.shape[0]):
        fetch(i).start()
    square = jnp.zeros((total, 1), jnp.float32)
    for s in range(blocks):
        for piece, side in ((mine_ref, core), (other_ref, 1 - core)):
            place = pl.multiple_of((wide ^ s) * (2 * half) + side * half, half)
            lifted = jnp.concatenate(
                [piece[s, (u ^ s) * rows:((u ^ s) + 1) * rows, :] for u in range(blocks)], axis=0
            )
            x_ref[:, pl.ds(place, half)] = lifted
            value = lifted.astype(jnp.float32)
            square += jnp.sum(value * value, axis=1, keepdims=True)
    own = pl.multiple_of(narrow * (2 * half), 2 * half)
    stream_ref[...] = x_ref[:rows, pl.ds(own, 2 * half)]
    scale = lax.rsqrt(square * (1.0 / depth) + 1e-6)
    for b in range(depth // 512):
        cols = slice(b * 512, (b + 1) * 512)
        x_ref[:, cols] = (
            x_ref[:, cols].astype(jnp.float32) * scale * gain_ref[:, cols]
        ).astype(jnp.bfloat16)
    mix = jnp.concatenate([r[:, -128:] for r in (cw0_ref, cw1_ref, cw2_ref, cw3_ref)], axis=0)
    lane = lax.broadcasted_iota(jnp.int32, (mix.shape[1], width), 0) % (mix.shape[1] // 2)

    for e in range(experts):
        gate = jnp.dot(x_ref[...], wg_ref[e], preferred_element_type=jnp.float32)
        upper = jnp.dot(x_ref[...], wu_ref[e], preferred_element_type=jnp.float32)
        pick = (lane == wide * experts + e).astype(jnp.bfloat16)
        share = jnp.dot(mix, pick, preferred_element_type=jnp.float32)
        hidden = gate / (1.0 + jnp.exp(-gate)) * upper * share
        hid_ref[:, e * width:(e + 1) * width] = hidden.astype(jnp.bfloat16)
    for i, j in enumerate(order):
        slot = i % down_ref.shape[0]
        fetch(i).wait()
        out = jnp.dot(hid_ref[...], down_ref[slot], preferred_element_type=jnp.float32)
        target = send_ref if j & 1 else keep_ref
        target[:, (j >> 1) * block:((j >> 1) + 1) * block] = out.astype(target.dtype)
        if i + down_ref.shape[0] < len(order):
            fetch(i + down_ref.shape[0]).start()


def local_small(
    queries,
    key_cache,
    cached_value_rows,
    lengths,
    residual,
    w_out,
    norm_gain,
    expert_ids,
    route_weights,
    w_gate,
    w_up,
    w_down,
):
    micro, per_micro, heads, width = queries.shape
    rows = micro * per_micro
    depth, columns = w_out.shape
    experts, model, hidden = w_gate.shape
    half = columns // 2
    vmem = pl.BlockSpec(memory_space=pltpu.VMEM)
    smem = pl.BlockSpec(memory_space=pltpu.SMEM)
    wide, narrow = lax.axis_index("wide"), lax.axis_index("narrow")
    where = jnp.stack([wide, narrow]).astype(jnp.int32)
    size = lax.axis_size("wide")
    turned = lax.ppermute(
        residual.reshape(rows, columns),
        ("wide", "narrow"),
        [(i, (i % size) * size + i // size) for i in range(size * size)],
    )
    given = (
        lengths,
        queries.reshape(rows * heads, width),
        key_cache.reshape(-1, width),
        cached_value_rows.reshape(-1, width),
        expert_ids.transpose(0, 2, 1),
        route_weights.transpose(0, 2, 1),
    )
    payload = pl.pallas_call(
        attend_kernel,
        out_shape=jax.ShapeDtypeStruct((rows, depth + 128), jnp.bfloat16),
        in_specs=[pl.BlockSpec(memory_space=pl.ANY)] * 6,
        out_specs=vmem,
        scratch_shapes=[pltpu.VMEM((rows * heads, width), jnp.float32)]
        + [pltpu.SMEM(given[0].shape, given[0].dtype)]
        + [pltpu.VMEM(g.shape, g.dtype) for g in given[1:]]
        + [pltpu.SemaphoreType.DMA((6,))],
        cost_estimate=pl.CostEstimate(flops=2 * 10**10, bytes_accessed=10**8, transcendentals=0),
        compiler_params=pltpu.CompilerParams(vmem_limit_bytes=6 * 2**20),
    )(*[pltpu.with_memory_space_constraint(g, pltpu.HBM) for g in given])
    others = spread(payload)
    keep, send = pl.pallas_call(
        project_kernel,
        out_shape=(
            jax.ShapeDtypeStruct((size * rows, half), jnp.float32),
            jax.ShapeDtypeStruct((size * rows, half), jnp.bfloat16),
        ),
        in_specs=[smem] + [vmem] * 6,
        out_specs=(vmem, vmem),
        cost_estimate=pl.CostEstimate(flops=2 * 10**10, bytes_accessed=10**8, transcendentals=0),
        compiler_params=pltpu.CompilerParams(vmem_limit_bytes=6 * 2**20),
    )(where, payload, *others, w_out, turned)
    part = (keep + flip_permute(send, "narrow", 1).astype(jnp.float32)).astype(jnp.bfloat16)
    stream = (
        part.astype(jnp.float32) + flip_permute(part, "narrow", 2).astype(jnp.float32)
    ).astype(jnp.bfloat16)
    mine = jnp.stack([stream] + spread(stream))
    other = flip_permute(mine, "narrow", 1)
    weights = [
        pltpu.with_memory_space_constraint(w, pltpu.VMEM)
        for w in (w_gate, w_up)
    ] + [
        pltpu.with_memory_space_constraint(w_down.reshape(experts * hidden, model), pltpu.HBM)
    ]
    keep, send, own = pl.pallas_call(
        expert_kernel,
        out_shape=(
            jax.ShapeDtypeStruct((size * rows, model // 2), jnp.float32),
            jax.ShapeDtypeStruct((size * rows, model // 2), jnp.bfloat16),
            jax.ShapeDtypeStruct((rows, columns), jnp.bfloat16),
        ),
        in_specs=[smem] + [vmem] * 9 + [pl.BlockSpec(memory_space=pl.ANY)],
        out_specs=(vmem, vmem, vmem),
        scratch_shapes=[
            pltpu.VMEM((size * rows, model), jnp.bfloat16),
            pltpu.VMEM((size * rows, experts * hidden), jnp.bfloat16),
            pltpu.VMEM((3, experts * hidden, columns), jnp.bfloat16),
            pltpu.SemaphoreType.DMA((3,)),
        ],
        compiler_params=pltpu.CompilerParams(vmem_limit_bytes=20 * 2**20),
    )(
        where,
        mine,
        other,
        payload,
        *others,
        norm_gain.reshape(1, model),
        *weights,
    )
    total = keep + flip_permute(send, "narrow", 1).astype(jnp.float32)
    total = total.reshape(size, rows, model // 2)
    leave = total[1:].astype(jnp.bfloat16)
    summed = total[0]
    for s in (2, 1, 3):
        summed = summed + flip_permute(leave[s - 1], "wide", s).astype(jnp.float32)
    cross = flip_permute(summed[:, columns:].astype(jnp.bfloat16), "narrow", 2)
    result = own.astype(jnp.float32) + summed[:, :columns] + cross.astype(jnp.float32)
    return result.astype(jnp.bfloat16).reshape(micro, per_micro, columns)


def solution(mesh):
    in_specs = (
        P(None, ("grp", "wide"), "narrow", None),
        P(None, ("grp", "wide"), None, "narrow", None),
        P(None, ("grp", "wide"), None, "narrow", None),
        P(None, ("grp", "wide")),
        P(None, ("grp", "wide"), "narrow"),
        P("narrow", "wide"),
        P(),
        P(None, ("grp", "wide"), None),
        P(None, ("grp", "wide"), None),
        P("wide", None, "narrow"),
        P("wide", None, "narrow"),
        P("wide", "narrow", None),
    )
    out_specs = P(None, ("grp", "wide"), "narrow")
    small = mesh.shape["wide"] == 4 and mesh.shape["narrow"] == 4
    body = local_small if small else local
    return jax.shard_map(body, mesh=mesh, in_specs=in_specs, out_specs=out_specs, check_vma=False)
```

```python
import math

import jax
import jax.numpy as jnp
from jax import lax
from jax.experimental import pallas as pl
from jax.experimental.pallas import tpu as pltpu
from jax.sharding import PartitionSpec as P

EXPERTS = 64
CAP = 3


def attend(query_rows, keys, values, valid_len):
    row_count, q_heads, head_size = query_rows.shape
    slot_count = keys.shape[1]
    kv_heads = keys.shape[2]
    flat_keys = keys.reshape(row_count, slot_count, kv_heads * head_size)
    flat_values = values.reshape(row_count, slot_count, kv_heads * head_size)
    position = jnp.arange(slot_count)
    usable = position[None, :] < valid_len[:, None]
    scores = jnp.einsum(
        "rgd,rcd->rgc", query_rows, flat_keys, preferred_element_type=jnp.float32
    ) / math.sqrt(head_size)
    scores = jnp.where(usable[:, None, :], scores, -1e30)
    largest = jnp.max(scores, axis=-1, keepdims=True)
    weight = jnp.exp(scores - largest)
    probs = (weight / jnp.sum(weight, axis=-1, keepdims=True)).astype(jnp.bfloat16)
    mixed = jnp.einsum("rgc,rcd->rgd", probs, flat_values, preferred_element_type=jnp.float32)
    results = mixed.astype(jnp.bfloat16)
    return results.reshape(row_count, q_heads * head_size)


def route_tables(chosen, weights, expert_count, capacity):
    row_count, top_count = chosen.shape
    pairs = chosen.reshape(-1)
    onehot = (pairs[:, None] == jnp.arange(expert_count)[None, :]).astype(jnp.int32)
    before = jnp.cumsum(onehot, axis=0) - onehot
    rank = jnp.sum(onehot * before, axis=1)
    slot = pairs * capacity + rank
    select = (slot[:, None] == jnp.arange(expert_count * capacity)[None, :]).astype(jnp.float32)
    select = select.reshape(row_count, top_count, expert_count * capacity)
    dispatch = jnp.sum(select, axis=1).astype(jnp.bfloat16)
    combine = jnp.sum(select * weights[:, :, None], axis=1)
    return (dispatch, combine)


def expert_block(pieces, norm_gain, w_gate, w_up, w_down):
    parts_count = pieces.shape[0]
    local_experts, model_width, hidden_width = w_gate.shape
    part_width = model_width // parts_count
    values = pieces.astype(jnp.float32)
    square = jnp.mean(values * values, axis=(0, 4), keepdims=True)
    gain_parts = norm_gain.reshape(parts_count, 1, 1, 1, part_width)
    normed = (values * lax.rsqrt(square + 1e-06) * gain_parts).astype(jnp.bfloat16)
    gate_parts = w_gate.reshape(local_experts, parts_count, part_width, hidden_width)
    up_parts = w_up.reshape(local_experts, parts_count, part_width, hidden_width)
    gate = jnp.einsum("nsjcd,jndf->sjcf", normed, gate_parts, preferred_element_type=jnp.float32)
    upper = jnp.einsum("nsjcd,jndf->sjcf", normed, up_parts, preferred_element_type=jnp.float32)
    hidden = (jax.nn.silu(gate) * upper).astype(jnp.bfloat16)
    narrow_count = lax.axis_size("narrow")
    down_parts = w_down.reshape(
        local_experts, w_down.shape[1], narrow_count, model_width // narrow_count
    )
    partial_out = jnp.einsum(
        "sjcf,jfnd->nsjcd", hidden, down_parts, preferred_element_type=jnp.float32
    )
    summed = lax.psum_scatter(
        partial_out.astype(jnp.bfloat16), "narrow", scatter_dimension=0, tiled=True
    ).astype(jnp.float32)[0]
    return lax.all_to_all(
        summed.astype(jnp.bfloat16), "wide", split_axis=0, concat_axis=0, tiled=True
    )


def local(
    queries,
    key_cache,
    cached_value_rows,
    lengths,
    residual,
    w_out,
    norm_gain,
    expert_ids,
    route_weights,
    w_gate,
    w_up,
    w_down,
):
    micro_count = queries.shape[0]
    wide_count = lax.axis_size("wide")
    local_experts = w_gate.shape[0]
    capacity = CAP
    attended = [
        attend(
            queries[index_values],
            key_cache[index_values],
            cached_value_rows[index_values],
            lengths[index_values],
        )
        for index_values in range(micro_count)
    ]
    terms = []
    for index_values in range(micro_count):
        columns = jnp.dot(
            lax.all_gather(attended[index_values], "wide", axis=0, tiled=True),
            w_out,
            preferred_element_type=jnp.float32,
        )
        terms.append(
            lax.all_to_all(
                columns.astype(jnp.bfloat16), "wide", split_axis=0, concat_axis=1, tiled=True
            ).astype(columns.dtype)
        )
    partial_sum = jnp.stack(terms)
    projected = lax.psum_scatter(
        partial_sum.astype(jnp.bfloat16), "narrow", scatter_dimension=2, tiled=True
    ).astype(jnp.float32)
    stream = (residual.astype(jnp.float32) + projected).astype(jnp.bfloat16)
    outputs = []
    for index_values in range(micro_count):
        dispatch, combine = route_tables(
            expert_ids[index_values], route_weights[index_values], EXPERTS, capacity
        )
        packed = lax.dot_general(
            dispatch,
            stream[index_values],
            (((0,), (0,)), ((), ())),
            preferred_element_type=jnp.float32,
        )
        packed = packed.astype(jnp.bfloat16).reshape(
            wide_count, local_experts, capacity, stream.shape[2]
        )
        back = (
            lambda rows_in: expert_block(
                lax.all_gather(rows_in[None], "narrow", axis=0, tiled=True),
                norm_gain,
                w_gate,
                w_up,
                w_down,
            )
        )(lax.all_to_all(packed, "wide", split_axis=0, concat_axis=0, tiled=True))
        returned = back.reshape(wide_count * local_experts * capacity, back.shape[3]).astype(
            jnp.float32
        )
        mixed = jnp.dot(combine, returned, precision=lax.Precision.HIGHEST)
        outputs.append((stream[index_values].astype(jnp.float32) + mixed).astype(jnp.bfloat16))
    return jnp.stack(outputs)


def flip_permute(value, axis, mask):
    size = lax.axis_size(axis)
    return lax.ppermute(value, axis, [(i, i ^ mask) for i in range(size)])


def spread(value):
    got = {s: flip_permute(value, "wide", s) for s in (1, 3, 2)}
    return [got[1], got[2], got[3]]


def attend_kernel(*refs):
    given, out_ref, mixed_ref, held, sems = refs[:6], refs[6], refs[7], refs[8:14], refs[14]
    copies = [
        pltpu.make_async_copy(source, target, sems.at[i])
        for i, (source, target) in enumerate(zip(given, held))
    ]
    for copy in copies:
        copy.start()
    for copy in copies:
        copy.wait()
    len_ref, q_ref, k_ref, v_ref, ids_ref, wts_ref = held
    rows, heads = out_ref.shape[0], q_ref.shape[0] // out_ref.shape[0]
    width = q_ref.shape[1]
    slots = k_ref.shape[0] // rows
    group = 256 // slots
    micro, per_micro = len_ref.shape
    row_request = lax.broadcasted_iota(jnp.int32, (group * heads, group * slots), 0) // heads
    column = lax.broadcasted_iota(jnp.int32, (group * heads, group * slots), 1)
    place = column - row_request * slots
    scores = []
    limits = []
    for g in range(rows // group):
        limit = jnp.zeros_like(place)
        for i in range(group):
            r = g * group + i
            limit = jnp.where(row_request == i, len_ref[r // per_micro, r % per_micro], limit)
        limits.append(limit)
        scores.append(
            lax.dot_general(
                q_ref[g * group * heads:(g + 1) * group * heads, :],
                k_ref[g * group * slots:(g + 1) * group * slots, :],
                (((1,), (1,)), ((), ())),
                preferred_element_type=jnp.float32,
            )
        )
    place = jnp.concatenate([place] * len(scores), axis=0)
    usable = (place >= 0) & (place < jnp.concatenate(limits, axis=0))
    scores = jnp.concatenate(scores, axis=0) * (1.0 / math.sqrt(width))
    scores = jnp.where(usable, scores, -1e30)
    weight = jnp.exp(scores - jnp.max(scores, axis=-1, keepdims=True))
    probs = (weight / jnp.sum(weight, axis=-1, keepdims=True)).astype(jnp.bfloat16)
    for g in range(rows // group):
        mixed_ref[g * group * heads:(g + 1) * group * heads, :] = jnp.dot(
            probs[g * group * heads:(g + 1) * group * heads, :],
            v_ref[g * group * slots:(g + 1) * group * slots, :],
            preferred_element_type=jnp.float32,
        )
    for h in range(heads):
        out_ref[:, h * width:(h + 1) * width] = mixed_ref[
            pl.ds(h, rows, stride=heads), :
        ].astype(jnp.bfloat16)
    lanes = 64
    expert = lax.broadcasted_iota(jnp.int32, (lanes, per_micro), 0)
    eye = (
        lax.broadcasted_iota(jnp.int32, (per_micro, per_micro), 0)
        == lax.broadcasted_iota(jnp.int32, (per_micro, per_micro), 1)
    ).astype(jnp.bfloat16)
    for m in range(micro):
        total = jnp.zeros((lanes, per_micro), jnp.float32)
        for t in range(ids_ref.shape[1]):
            total += jnp.where(
                expert == ids_ref[m, t:t + 1, :], wts_ref[m, t:t + 1, :], 0.0
            )
        high = total.astype(jnp.bfloat16)
        low = (total - high.astype(jnp.float32)).astype(jnp.bfloat16)
        both = jnp.concatenate([high, low], axis=0)
        out_ref[m * per_micro:(m + 1) * per_micro, heads * width:] = lax.dot_general(
            eye, both, (((1,), (1,)), ((), ())), preferred_element_type=jnp.float32
        ).astype(jnp.bfloat16)


def project_kernel(where_ref, own_ref, got1_ref, got2_ref, got3_ref, w_ref, res_ref,
                   keep_ref, send_ref, mix_ref):
    wide, narrow = where_ref[0], where_ref[1]
    depth = w_ref.shape[0]
    half = keep_ref.shape[1]
    rows = own_ref.shape[0]
    features = jnp.concatenate(
        [r[:, :depth] for r in (own_ref, got1_ref, got2_ref, got3_ref)], axis=0
    )
    mine = pl.ds(pl.multiple_of((narrow & 1) * half, half), half)
    other = pl.ds(pl.multiple_of((1 - (narrow & 1)) * half, half), half)
    spot = pl.ds(pl.multiple_of((wide ^ narrow) * rows, rows), rows)
    keep_ref[...] = jnp.dot(features, w_ref[:, mine], preferred_element_type=jnp.float32)
    keep_ref[spot, :] += res_ref[:, mine].astype(jnp.float32)
    part = jnp.dot(features, w_ref[:, other], preferred_element_type=jnp.float32)
    part_rows = lax.broadcasted_iota(jnp.int32, part.shape, 0) // rows
    extra = res_ref[:, other].astype(jnp.float32)
    extra = jnp.concatenate([extra] * (part.shape[0] // rows), axis=0)
    part = jnp.where(part_rows == (wide ^ narrow), part + extra, part)
    send_ref[...] = part.astype(jnp.bfloat16)
    mix_ref[...] = jnp.concatenate(
        [r[:, depth:] for r in (own_ref, got1_ref, got2_ref, got3_ref)], axis=0
    )


def expert_kernel(where_ref, mine_ref, other_ref, mix_ref, gain_ref,
                  wg_ref, wu_ref, wd_ref, keep_ref, send_ref, stream_ref,
                  x_ref, hid_ref):
    wide, narrow = where_ref[0], where_ref[1]
    core = narrow & 1
    blocks, total, half = mine_ref.shape
    rows = total // blocks
    experts, depth, width = wg_ref.shape
    block = 2 * half
    square = jnp.zeros((total, 1), jnp.float32)
    for s in range(blocks):
        for piece, side in ((mine_ref, core), (other_ref, 1 - core)):
            place = pl.multiple_of((wide ^ s) * (2 * half) + side * half, half)
            lifted = jnp.concatenate(
                [piece[s, (u ^ s) * rows:((u ^ s) + 1) * rows, :] for u in range(blocks)], axis=0
            )
            x_ref[:, pl.ds(place, half)] = lifted
            value = lifted.astype(jnp.float32)
            square += jnp.sum(value * value, axis=1, keepdims=True)
    own = pl.multiple_of(narrow * (2 * half), 2 * half)
    stream_ref[...] = x_ref[:rows, pl.ds(own, 2 * half)]
    scale = lax.rsqrt(square * (1.0 / depth) + 1e-6)
    for b in range(depth // 512):
        cols = slice(b * 512, (b + 1) * 512)
        x_ref[:, cols] = (
            x_ref[:, cols].astype(jnp.float32) * scale * gain_ref[:, cols]
        ).astype(jnp.bfloat16)
    mix = mix_ref[...]
    lane = lax.broadcasted_iota(jnp.int32, (mix.shape[1], width), 0) % (mix.shape[1] // 2)

    for e in range(experts):
        gate = jnp.dot(x_ref[...], wg_ref[e], preferred_element_type=jnp.float32)
        upper = jnp.dot(x_ref[...], wu_ref[e], preferred_element_type=jnp.float32)
        pick = (lane == wide * experts + e).astype(jnp.bfloat16)
        share = jnp.dot(mix, pick, preferred_element_type=jnp.float32)
        hidden = gate / (1.0 + jnp.exp(-gate)) * upper * share
        hid_ref[:, e * width:(e + 1) * width] = hidden.astype(jnp.bfloat16)
    for j in (1, 3, 0, 2):
        start = pl.multiple_of((narrow ^ j) * block, block)
        out = jnp.dot(
            hid_ref[...], wd_ref[:, pl.ds(start, block)], preferred_element_type=jnp.float32
        )
        target = send_ref if j & 1 else keep_ref
        target[:, (j >> 1) * block:((j >> 1) + 1) * block] = out.astype(target.dtype)


def local_small(
    queries,
    key_cache,
    cached_value_rows,
    lengths,
    residual,
    w_out,
    norm_gain,
    expert_ids,
    route_weights,
    w_gate,
    w_up,
    w_down,
):
    micro, per_micro, heads, width = queries.shape
    rows = micro * per_micro
    depth, columns = w_out.shape
    experts, model, hidden = w_gate.shape
    half = columns // 2
    vmem = pl.BlockSpec(memory_space=pltpu.VMEM)
    smem = pl.BlockSpec(memory_space=pltpu.SMEM)
    wide, narrow = lax.axis_index("wide"), lax.axis_index("narrow")
    where = jnp.stack([wide, narrow]).astype(jnp.int32)
    size = lax.axis_size("wide")
    turned = lax.ppermute(
        residual.reshape(rows, columns),
        ("wide", "narrow"),
        [(i, (i % size) * size + i // size) for i in range(size * size)],
    )
    given = (
        lengths,
        queries.reshape(rows * heads, width),
        key_cache.reshape(-1, width),
        cached_value_rows.reshape(-1, width),
        expert_ids.transpose(0, 2, 1),
        route_weights.transpose(0, 2, 1),
    )
    payload = pl.pallas_call(
        attend_kernel,
        out_shape=jax.ShapeDtypeStruct((rows, depth + 128), jnp.bfloat16),
        in_specs=[pl.BlockSpec(memory_space=pl.ANY)] * 6,
        out_specs=vmem,
        scratch_shapes=[pltpu.VMEM((rows * heads, width), jnp.float32)]
        + [pltpu.SMEM(given[0].shape, given[0].dtype)]
        + [pltpu.VMEM(g.shape, g.dtype) for g in given[1:]]
        + [pltpu.SemaphoreType.DMA((6,))],
        cost_estimate=pl.CostEstimate(flops=20000000000, bytes_accessed=1000000, transcendentals=0),
        compiler_params=pltpu.CompilerParams(vmem_limit_bytes=6 * 2**20),
    )(*[pltpu.with_memory_space_constraint(g, pltpu.HBM) for g in given])
    others = spread(payload)
    keep, send, mix = pl.pallas_call(
        project_kernel,
        out_shape=(
            jax.ShapeDtypeStruct((size * rows, half), jnp.float32),
            jax.ShapeDtypeStruct((size * rows, half), jnp.bfloat16),
            jax.ShapeDtypeStruct((size * rows, 128), jnp.bfloat16),
        ),
        in_specs=[smem] + [vmem] * 6,
        out_specs=(vmem, vmem, vmem),
        cost_estimate=pl.CostEstimate(flops=30000000000, bytes_accessed=1000000, transcendentals=0),
        compiler_params=pltpu.CompilerParams(vmem_limit_bytes=6 * 2**20),
    )(where, payload, *others, w_out, turned)
    part = (keep + flip_permute(send, "narrow", 1).astype(jnp.float32)).astype(jnp.bfloat16)
    stream = (
        part.astype(jnp.float32) + flip_permute(part, "narrow", 2).astype(jnp.float32)
    ).astype(jnp.bfloat16)
    mine = jnp.stack([stream] + spread(stream))
    other = flip_permute(mine, "narrow", 1)
    weights = [
        pltpu.with_memory_space_constraint(w, pltpu.VMEM)
        for w in (w_gate, w_up, w_down.reshape(experts * hidden, model))
    ]
    keep, send, own = pl.pallas_call(
        expert_kernel,
        out_shape=(
            pltpu.VMEM((size * rows, model // 2), jnp.float32),
            pltpu.VMEM((size * rows, model // 2), jnp.bfloat16),
            pltpu.VMEM((rows, columns), jnp.bfloat16),
        ),
        in_specs=[smem] + [vmem] * 7,
        out_specs=(vmem, vmem, vmem),
        scratch_shapes=[
            pltpu.VMEM((size * rows, model), jnp.bfloat16),
            pltpu.VMEM((size * rows, experts * hidden), jnp.bfloat16),
        ],
        compiler_params=pltpu.CompilerParams(vmem_limit_bytes=11 * 2**20),
    )(
        where,
        *[pltpu.with_memory_space_constraint(p, pltpu.VMEM) for p in (mine, other, mix)],
        norm_gain.reshape(1, model),
        *weights,
    )
    total = keep + flip_permute(send, "narrow", 1).astype(jnp.float32)
    total = total.reshape(size, rows, model // 2)
    leave = total[1:].astype(jnp.bfloat16)
    summed = total[0]
    for s in (2, 1, 3):
        summed = summed + flip_permute(leave[s - 1], "wide", s).astype(jnp.float32)
    cross = flip_permute(summed[:, columns:].astype(jnp.bfloat16), "narrow", 2)
    result = own.astype(jnp.float32) + summed[:, :columns] + cross.astype(jnp.float32)
    return result.astype(jnp.bfloat16).reshape(micro, per_micro, columns)


def solution(mesh):
    in_specs = (
        P(None, ("grp", "wide"), "narrow", None),
        P(None, ("grp", "wide"), None, "narrow", None),
        P(None, ("grp", "wide"), None, "narrow", None),
        P(None, ("grp", "wide")),
        P(None, ("grp", "wide"), "narrow"),
        P("narrow", "wide"),
        P(),
        P(None, ("grp", "wide"), None),
        P(None, ("grp", "wide"), None),
        P("wide", None, "narrow"),
        P("wide", None, "narrow"),
        P("wide", "narrow", None),
    )
    out_specs = P(None, ("grp", "wide"), "narrow")
    small = mesh.shape["wide"] == 4 and mesh.shape["narrow"] == 4
    body = local_small if small else local
    return jax.shard_map(body, mesh=mesh, in_specs=in_specs, out_specs=out_specs, check_vma=False)
```

```python
import math

import jax
import jax.numpy as jnp
from jax import lax
from jax.experimental import pallas as pl
from jax.experimental.pallas import tpu as pltpu
from jax.sharding import PartitionSpec as P

EXPERTS = 64
CAP = 3


def attend(query_rows, keys, values, valid_len):
    row_count, q_heads, head_size = query_rows.shape
    slot_count = keys.shape[1]
    kv_heads = keys.shape[2]
    flat_keys = keys.reshape(row_count, slot_count, kv_heads * head_size)
    flat_values = values.reshape(row_count, slot_count, kv_heads * head_size)
    position = jnp.arange(slot_count)
    usable = position[None, :] < valid_len[:, None]
    scores = jnp.einsum(
        "rgd,rcd->rgc", query_rows, flat_keys, preferred_element_type=jnp.float32
    ) / math.sqrt(head_size)
    scores = jnp.where(usable[:, None, :], scores, -1e30)
    largest = jnp.max(scores, axis=-1, keepdims=True)
    weight = jnp.exp(scores - largest)
    probs = (weight / jnp.sum(weight, axis=-1, keepdims=True)).astype(jnp.bfloat16)
    mixed = jnp.einsum("rgc,rcd->rgd", probs, flat_values, preferred_element_type=jnp.float32)
    results = mixed.astype(jnp.bfloat16)
    return results.reshape(row_count, q_heads * head_size)


def route_tables(chosen, weights, expert_count, capacity):
    row_count, top_count = chosen.shape
    pairs = chosen.reshape(-1)
    onehot = (pairs[:, None] == jnp.arange(expert_count)[None, :]).astype(jnp.int32)
    before = jnp.cumsum(onehot, axis=0) - onehot
    rank = jnp.sum(onehot * before, axis=1)
    slot = pairs * capacity + rank
    select = (slot[:, None] == jnp.arange(expert_count * capacity)[None, :]).astype(jnp.float32)
    select = select.reshape(row_count, top_count, expert_count * capacity)
    dispatch = jnp.sum(select, axis=1).astype(jnp.bfloat16)
    combine = jnp.sum(select * weights[:, :, None], axis=1)
    return (dispatch, combine)


def expert_block(pieces, norm_gain, w_gate, w_up, w_down):
    parts_count = pieces.shape[0]
    local_experts, model_width, hidden_width = w_gate.shape
    part_width = model_width // parts_count
    values = pieces.astype(jnp.float32)
    square = jnp.mean(values * values, axis=(0, 4), keepdims=True)
    gain_parts = norm_gain.reshape(parts_count, 1, 1, 1, part_width)
    normed = (values * lax.rsqrt(square + 1e-06) * gain_parts).astype(jnp.bfloat16)
    gate_parts = w_gate.reshape(local_experts, parts_count, part_width, hidden_width)
    up_parts = w_up.reshape(local_experts, parts_count, part_width, hidden_width)
    gate = jnp.einsum("nsjcd,jndf->sjcf", normed, gate_parts, preferred_element_type=jnp.float32)
    upper = jnp.einsum("nsjcd,jndf->sjcf", normed, up_parts, preferred_element_type=jnp.float32)
    hidden = (jax.nn.silu(gate) * upper).astype(jnp.bfloat16)
    narrow_count = lax.axis_size("narrow")
    down_parts = w_down.reshape(
        local_experts, w_down.shape[1], narrow_count, model_width // narrow_count
    )
    partial_out = jnp.einsum(
        "sjcf,jfnd->nsjcd", hidden, down_parts, preferred_element_type=jnp.float32
    )
    summed = lax.psum_scatter(
        partial_out.astype(jnp.bfloat16), "narrow", scatter_dimension=0, tiled=True
    ).astype(jnp.float32)[0]
    return lax.all_to_all(
        summed.astype(jnp.bfloat16), "wide", split_axis=0, concat_axis=0, tiled=True
    )


def local(
    queries,
    key_cache,
    cached_value_rows,
    lengths,
    residual,
    w_out,
    norm_gain,
    expert_ids,
    route_weights,
    w_gate,
    w_up,
    w_down,
):
    micro_count = queries.shape[0]
    wide_count = lax.axis_size("wide")
    local_experts = w_gate.shape[0]
    capacity = CAP
    attended = [
        attend(
            queries[index_values],
            key_cache[index_values],
            cached_value_rows[index_values],
            lengths[index_values],
        )
        for index_values in range(micro_count)
    ]
    terms = []
    for index_values in range(micro_count):
        columns = jnp.dot(
            lax.all_gather(attended[index_values], "wide", axis=0, tiled=True),
            w_out,
            preferred_element_type=jnp.float32,
        )
        terms.append(
            lax.all_to_all(
                columns.astype(jnp.bfloat16), "wide", split_axis=0, concat_axis=1, tiled=True
            ).astype(columns.dtype)
        )
    partial_sum = jnp.stack(terms)
    projected = lax.psum_scatter(
        partial_sum.astype(jnp.bfloat16), "narrow", scatter_dimension=2, tiled=True
    ).astype(jnp.float32)
    stream = (residual.astype(jnp.float32) + projected).astype(jnp.bfloat16)
    outputs = []
    for index_values in range(micro_count):
        dispatch, combine = route_tables(
            expert_ids[index_values], route_weights[index_values], EXPERTS, capacity
        )
        packed = lax.dot_general(
            dispatch,
            stream[index_values],
            (((0,), (0,)), ((), ())),
            preferred_element_type=jnp.float32,
        )
        packed = packed.astype(jnp.bfloat16).reshape(
            wide_count, local_experts, capacity, stream.shape[2]
        )
        back = (
            lambda rows_in: expert_block(
                lax.all_gather(rows_in[None], "narrow", axis=0, tiled=True),
                norm_gain,
                w_gate,
                w_up,
                w_down,
            )
        )(lax.all_to_all(packed, "wide", split_axis=0, concat_axis=0, tiled=True))
        returned = back.reshape(wide_count * local_experts * capacity, back.shape[3]).astype(
            jnp.float32
        )
        mixed = jnp.dot(combine, returned, precision=lax.Precision.HIGHEST)
        outputs.append((stream[index_values].astype(jnp.float32) + mixed).astype(jnp.bfloat16))
    return jnp.stack(outputs)


def flip_permute(value, axis, mask):
    size = lax.axis_size(axis)
    return lax.ppermute(value, axis, [(i, i ^ mask) for i in range(size)])


def spread(value):
    got = {s: flip_permute(value, "wide", s) for s in (1, 3, 2)}
    return [got[1], got[2], got[3]]


def attend_kernel(*refs):
    given, out_ref, mixed_ref, held, sems = refs[:6], refs[6], refs[7], refs[8:14], refs[14]
    copies = [
        pltpu.make_async_copy(source, target, sems.at[i])
        for i, (source, target) in enumerate(zip(given, held))
    ]
    for copy in copies:
        copy.start()
    for copy in copies:
        copy.wait()
    len_ref, q_ref, k_ref, v_ref, ids_ref, wts_ref = held
    rows, heads = out_ref.shape[0], q_ref.shape[0] // out_ref.shape[0]
    width = q_ref.shape[1]
    slots = k_ref.shape[0] // rows
    group = 256 // slots
    micro, per_micro = len_ref.shape
    row_request = lax.broadcasted_iota(jnp.int32, (group * heads, group * slots), 0) // heads
    column = lax.broadcasted_iota(jnp.int32, (group * heads, group * slots), 1)
    place = column - row_request * slots
    scores = []
    limits = []
    for g in range(rows // group):
        limit = jnp.zeros_like(place)
        for i in range(group):
            r = g * group + i
            limit = jnp.where(row_request == i, len_ref[r // per_micro, r % per_micro], limit)
        limits.append(limit)
        scores.append(
            lax.dot_general(
                q_ref[g * group * heads:(g + 1) * group * heads, :],
                k_ref[g * group * slots:(g + 1) * group * slots, :],
                (((1,), (1,)), ((), ())),
                preferred_element_type=jnp.float32,
            )
        )
    place = jnp.concatenate([place] * len(scores), axis=0)
    usable = (place >= 0) & (place < jnp.concatenate(limits, axis=0))
    scores = jnp.concatenate(scores, axis=0) * (1.0 / math.sqrt(width))
    scores = jnp.where(usable, scores, -1e30)
    weight = jnp.exp(scores - jnp.max(scores, axis=-1, keepdims=True))
    probs = (weight / jnp.sum(weight, axis=-1, keepdims=True)).astype(jnp.bfloat16)
    for g in range(rows // group):
        mixed_ref[g * group * heads:(g + 1) * group * heads, :] = jnp.dot(
            probs[g * group * heads:(g + 1) * group * heads, :],
            v_ref[g * group * slots:(g + 1) * group * slots, :],
            preferred_element_type=jnp.float32,
        )
    for h in range(heads):
        out_ref[:, h * width:(h + 1) * width] = mixed_ref[
            pl.ds(h, rows, stride=heads), :
        ].astype(jnp.bfloat16)
    lanes = 64
    expert = lax.broadcasted_iota(jnp.int32, (lanes, per_micro), 0)
    eye = (
        lax.broadcasted_iota(jnp.int32, (per_micro, per_micro), 0)
        == lax.broadcasted_iota(jnp.int32, (per_micro, per_micro), 1)
    ).astype(jnp.bfloat16)
    for m in range(micro):
        total = jnp.zeros((lanes, per_micro), jnp.float32)
        for t in range(ids_ref.shape[1]):
            total += jnp.where(
                expert == ids_ref[m, t:t + 1, :], wts_ref[m, t:t + 1, :], 0.0
            )
        high = total.astype(jnp.bfloat16)
        low = (total - high.astype(jnp.float32)).astype(jnp.bfloat16)
        both = jnp.concatenate([high, low], axis=0)
        out_ref[m * per_micro:(m + 1) * per_micro, heads * width:] = lax.dot_general(
            eye, both, (((1,), (1,)), ((), ())), preferred_element_type=jnp.float32
        ).astype(jnp.bfloat16)


def project_kernel(where_ref, own_ref, got1_ref, got2_ref, got3_ref, w_ref, res_ref,
                   keep_ref, send_ref, mix_ref):
    wide, narrow = where_ref[0], where_ref[1]
    depth = w_ref.shape[0]
    half = keep_ref.shape[1]
    rows = own_ref.shape[0]
    features = jnp.concatenate(
        [r[:, :depth] for r in (own_ref, got1_ref, got2_ref, got3_ref)], axis=0
    )
    mine = pl.ds(pl.multiple_of((narrow & 1) * half, half), half)
    other = pl.ds(pl.multiple_of((1 - (narrow & 1)) * half, half), half)
    spot = pl.ds(pl.multiple_of((wide ^ narrow) * rows, rows), rows)
    keep_ref[...] = jnp.dot(features, w_ref[:, mine], preferred_element_type=jnp.float32)
    keep_ref[spot, :] += res_ref[:, mine].astype(jnp.float32)
    part = jnp.dot(features, w_ref[:, other], preferred_element_type=jnp.float32)
    part_rows = lax.broadcasted_iota(jnp.int32, part.shape, 0) // rows
    extra = res_ref[:, other].astype(jnp.float32)
    extra = jnp.concatenate([extra] * (part.shape[0] // rows), axis=0)
    part = jnp.where(part_rows == (wide ^ narrow), part + extra, part)
    send_ref[...] = part.astype(jnp.bfloat16)
    mix_ref[...] = jnp.concatenate(
        [r[:, depth:] for r in (own_ref, got1_ref, got2_ref, got3_ref)], axis=0
    )


def expert_kernel(where_ref, mine_ref, other_ref, mix_ref, gain_ref,
                  wg_ref, wu_ref, wd_ref, keep_ref, send_ref, stream_ref,
                  x_ref, hid_ref):
    wide, narrow = where_ref[0], where_ref[1]
    core = narrow & 1
    blocks, total, half = mine_ref.shape
    rows = total // blocks
    experts, depth, width = wg_ref.shape
    block = 2 * half
    square = jnp.zeros((total, 1), jnp.float32)
    for s in range(blocks):
        for piece, side in ((mine_ref, core), (other_ref, 1 - core)):
            place = pl.multiple_of((wide ^ s) * (2 * half) + side * half, half)
            lifted = jnp.concatenate(
                [piece[s, (u ^ s) * rows:((u ^ s) + 1) * rows, :] for u in range(blocks)], axis=0
            )
            x_ref[:, pl.ds(place, half)] = lifted
            value = lifted.astype(jnp.float32)
            square += jnp.sum(value * value, axis=1, keepdims=True)
    own = pl.multiple_of(narrow * (2 * half), 2 * half)
    stream_ref[...] = x_ref[:rows, pl.ds(own, 2 * half)]
    scale = lax.rsqrt(square * (1.0 / depth) + 1e-6)
    for b in range(depth // 512):
        cols = slice(b * 512, (b + 1) * 512)
        x_ref[:, cols] = (
            x_ref[:, cols].astype(jnp.float32) * scale * gain_ref[:, cols]
        ).astype(jnp.bfloat16)
    mix = mix_ref[...]
    lane = lax.broadcasted_iota(jnp.int32, (mix.shape[1], width), 0) % (mix.shape[1] // 2)

    for e in range(experts):
        gate = jnp.dot(x_ref[...], wg_ref[e], preferred_element_type=jnp.float32)
        upper = jnp.dot(x_ref[...], wu_ref[e], preferred_element_type=jnp.float32)
        pick = (lane == wide * experts + e).astype(jnp.bfloat16)
        share = jnp.dot(mix, pick, preferred_element_type=jnp.float32)
        hidden = gate / (1.0 + jnp.exp(-gate)) * upper * share
        hid_ref[:, e * width:(e + 1) * width] = hidden.astype(jnp.bfloat16)
    side = (narrow >> 1) ^ core
    for target, place in ((send_ref, 1 - side), (keep_ref, side)):
        for k in range(2):
            start = pl.multiple_of((2 * place + k) * block, block)
            out = jnp.dot(
                hid_ref[...], wd_ref[:, pl.ds(start, block)], preferred_element_type=jnp.float32
            )
            target[:, k * block:(k + 1) * block] = out.astype(target.dtype)


def local_small(
    queries,
    key_cache,
    cached_value_rows,
    lengths,
    residual,
    w_out,
    norm_gain,
    expert_ids,
    route_weights,
    w_gate,
    w_up,
    w_down,
):
    micro, per_micro, heads, width = queries.shape
    rows = micro * per_micro
    depth, columns = w_out.shape
    experts, model, hidden = w_gate.shape
    half = columns // 2
    vmem = pl.BlockSpec(memory_space=pltpu.VMEM)
    smem = pl.BlockSpec(memory_space=pltpu.SMEM)
    wide, narrow = lax.axis_index("wide"), lax.axis_index("narrow")
    where = jnp.stack([wide, narrow]).astype(jnp.int32)
    size = lax.axis_size("wide")
    turned = lax.ppermute(
        residual.reshape(rows, columns),
        ("wide", "narrow"),
        [(i, (i % size) * size + i // size) for i in range(size * size)],
    )
    given = (
        lengths,
        queries.reshape(rows * heads, width),
        key_cache.reshape(-1, width),
        cached_value_rows.reshape(-1, width),
        expert_ids.transpose(0, 2, 1),
        route_weights.transpose(0, 2, 1),
    )
    payload = pl.pallas_call(
        attend_kernel,
        out_shape=jax.ShapeDtypeStruct((rows, depth + 128), jnp.bfloat16),
        in_specs=[pl.BlockSpec(memory_space=pl.ANY)] * 6,
        out_specs=vmem,
        scratch_shapes=[pltpu.VMEM((rows * heads, width), jnp.float32)]
        + [pltpu.SMEM(given[0].shape, given[0].dtype)]
        + [pltpu.VMEM(g.shape, g.dtype) for g in given[1:]]
        + [pltpu.SemaphoreType.DMA((6,))],
        cost_estimate=pl.CostEstimate(flops=20000000000, bytes_accessed=1000000, transcendentals=0),
        compiler_params=pltpu.CompilerParams(vmem_limit_bytes=6 * 2**20),
    )(*[pltpu.with_memory_space_constraint(g, pltpu.HBM) for g in given])
    others = spread(payload)
    keep, send, mix = pl.pallas_call(
        project_kernel,
        out_shape=(
            jax.ShapeDtypeStruct((size * rows, half), jnp.float32),
            jax.ShapeDtypeStruct((size * rows, half), jnp.bfloat16),
            jax.ShapeDtypeStruct((size * rows, 128), jnp.bfloat16),
        ),
        in_specs=[smem] + [vmem] * 6,
        out_specs=(vmem, vmem, vmem),
        cost_estimate=pl.CostEstimate(flops=30000000000, bytes_accessed=1000000, transcendentals=0),
        compiler_params=pltpu.CompilerParams(vmem_limit_bytes=6 * 2**20),
    )(where, payload, *others, w_out, turned)
    part = (keep + flip_permute(send, "narrow", 1).astype(jnp.float32)).astype(jnp.bfloat16)
    stream = (
        part.astype(jnp.float32) + flip_permute(part, "narrow", 2).astype(jnp.float32)
    ).astype(jnp.bfloat16)
    mine = jnp.stack([stream] + spread(stream))
    other = flip_permute(mine, "narrow", 1)
    weights = [
        pltpu.with_memory_space_constraint(w, pltpu.VMEM)
        for w in (w_gate, w_up, w_down.reshape(experts * hidden, model))
    ]
    keep, send, own = pl.pallas_call(
        expert_kernel,
        out_shape=(
            pltpu.VMEM((size * rows, model // 2), jnp.float32),
            pltpu.VMEM((size * rows, model // 2), jnp.bfloat16),
            pltpu.VMEM((rows, columns), jnp.bfloat16),
        ),
        in_specs=[smem] + [vmem] * 7,
        out_specs=(vmem, vmem, vmem),
        scratch_shapes=[
            pltpu.VMEM((size * rows, model), jnp.bfloat16),
            pltpu.VMEM((size * rows, experts * hidden), jnp.bfloat16),
        ],
        compiler_params=pltpu.CompilerParams(vmem_limit_bytes=11 * 2**20),
    )(
        where,
        *[pltpu.with_memory_space_constraint(p, pltpu.VMEM) for p in (mine, other, mix)],
        norm_gain.reshape(1, model),
        *weights,
    )
    total = (keep + flip_permute(send, "narrow", 1).astype(jnp.float32)).astype(jnp.bfloat16)
    total = total.reshape(size, rows, model // 2)
    devices = range(size * size)
    got = [
        lax.ppermute(
            total[s],
            ("wide", "narrow"),
            [(i, i ^ (s * size) ^ (2 if i & 1 else 0)) for i in devices],
        ).astype(jnp.float32)
        for s in (2, 1, 3, 0)
    ]
    summed = got[0] + got[1] + got[2] + got[3]
    first = (narrow & 1) == 0
    left, right = summed[:, :columns], summed[:, columns:]
    cross = flip_permute(jnp.where(first, right, left).astype(jnp.bfloat16), "narrow", 1)
    result = own.astype(jnp.float32) + jnp.where(first, left, right) + cross.astype(jnp.float32)
    return result.astype(jnp.bfloat16).reshape(micro, per_micro, columns)


def solution(mesh):
    in_specs = (
        P(None, ("grp", "wide"), "narrow", None),
        P(None, ("grp", "wide"), None, "narrow", None),
        P(None, ("grp", "wide"), None, "narrow", None),
        P(None, ("grp", "wide")),
        P(None, ("grp", "wide"), "narrow"),
        P("narrow", "wide"),
        P(),
        P(None, ("grp", "wide"), None),
        P(None, ("grp", "wide"), None),
        P("wide", None, "narrow"),
        P("wide", None, "narrow"),
        P("wide", "narrow", None),
    )
    out_specs = P(None, ("grp", "wide"), "narrow")
    small = mesh.shape["wide"] == 4 and mesh.shape["narrow"] == 4
    body = local_small if small else local
    return jax.shard_map(body, mesh=mesh, in_specs=in_specs, out_specs=out_specs, check_vma=False)
```

```python
import math

import jax
import jax.numpy as jnp
from jax import lax
from jax.experimental import pallas as pl
from jax.experimental.pallas import tpu as pltpu
from jax.sharding import PartitionSpec as P

EXPERTS = 64
CAP = 3


def attend(query_rows, keys, values, valid_len):
    row_count, q_heads, head_size = query_rows.shape
    slot_count = keys.shape[1]
    kv_heads = keys.shape[2]
    flat_keys = keys.reshape(row_count, slot_count, kv_heads * head_size)
    flat_values = values.reshape(row_count, slot_count, kv_heads * head_size)
    position = jnp.arange(slot_count)
    usable = position[None, :] < valid_len[:, None]
    scores = jnp.einsum(
        "rgd,rcd->rgc", query_rows, flat_keys, preferred_element_type=jnp.float32
    ) / math.sqrt(head_size)
    scores = jnp.where(usable[:, None, :], scores, -1e30)
    largest = jnp.max(scores, axis=-1, keepdims=True)
    weight = jnp.exp(scores - largest)
    probs = (weight / jnp.sum(weight, axis=-1, keepdims=True)).astype(jnp.bfloat16)
    mixed = jnp.einsum("rgc,rcd->rgd", probs, flat_values, preferred_element_type=jnp.float32)
    results = mixed.astype(jnp.bfloat16)
    return results.reshape(row_count, q_heads * head_size)


def route_tables(chosen, weights, expert_count, capacity):
    row_count, top_count = chosen.shape
    pairs = chosen.reshape(-1)
    onehot = (pairs[:, None] == jnp.arange(expert_count)[None, :]).astype(jnp.int32)
    before = jnp.cumsum(onehot, axis=0) - onehot
    rank = jnp.sum(onehot * before, axis=1)
    slot = pairs * capacity + rank
    select = (slot[:, None] == jnp.arange(expert_count * capacity)[None, :]).astype(jnp.float32)
    select = select.reshape(row_count, top_count, expert_count * capacity)
    dispatch = jnp.sum(select, axis=1).astype(jnp.bfloat16)
    combine = jnp.sum(select * weights[:, :, None], axis=1)
    return (dispatch, combine)


def expert_block(pieces, norm_gain, w_gate, w_up, w_down):
    parts_count = pieces.shape[0]
    local_experts, model_width, hidden_width = w_gate.shape
    part_width = model_width // parts_count
    values = pieces.astype(jnp.float32)
    square = jnp.mean(values * values, axis=(0, 4), keepdims=True)
    gain_parts = norm_gain.reshape(parts_count, 1, 1, 1, part_width)
    normed = (values * lax.rsqrt(square + 1e-06) * gain_parts).astype(jnp.bfloat16)
    gate_parts = w_gate.reshape(local_experts, parts_count, part_width, hidden_width)
    up_parts = w_up.reshape(local_experts, parts_count, part_width, hidden_width)
    gate = jnp.einsum("nsjcd,jndf->sjcf", normed, gate_parts, preferred_element_type=jnp.float32)
    upper = jnp.einsum("nsjcd,jndf->sjcf", normed, up_parts, preferred_element_type=jnp.float32)
    hidden = (jax.nn.silu(gate) * upper).astype(jnp.bfloat16)
    narrow_count = lax.axis_size("narrow")
    down_parts = w_down.reshape(
        local_experts, w_down.shape[1], narrow_count, model_width // narrow_count
    )
    partial_out = jnp.einsum(
        "sjcf,jfnd->nsjcd", hidden, down_parts, preferred_element_type=jnp.float32
    )
    summed = lax.psum_scatter(
        partial_out.astype(jnp.bfloat16), "narrow", scatter_dimension=0, tiled=True
    ).astype(jnp.float32)[0]
    return lax.all_to_all(
        summed.astype(jnp.bfloat16), "wide", split_axis=0, concat_axis=0, tiled=True
    )


def local(
    queries,
    key_cache,
    cached_value_rows,
    lengths,
    residual,
    w_out,
    norm_gain,
    expert_ids,
    route_weights,
    w_gate,
    w_up,
    w_down,
):
    micro_count = queries.shape[0]
    wide_count = lax.axis_size("wide")
    local_experts = w_gate.shape[0]
    capacity = CAP
    attended = [
        attend(
            queries[index_values],
            key_cache[index_values],
            cached_value_rows[index_values],
            lengths[index_values],
        )
        for index_values in range(micro_count)
    ]
    terms = []
    for index_values in range(micro_count):
        columns = jnp.dot(
            lax.all_gather(attended[index_values], "wide", axis=0, tiled=True),
            w_out,
            preferred_element_type=jnp.float32,
        )
        terms.append(
            lax.all_to_all(
                columns.astype(jnp.bfloat16), "wide", split_axis=0, concat_axis=1, tiled=True
            ).astype(columns.dtype)
        )
    partial_sum = jnp.stack(terms)
    projected = lax.psum_scatter(
        partial_sum.astype(jnp.bfloat16), "narrow", scatter_dimension=2, tiled=True
    ).astype(jnp.float32)
    stream = (residual.astype(jnp.float32) + projected).astype(jnp.bfloat16)
    outputs = []
    for index_values in range(micro_count):
        dispatch, combine = route_tables(
            expert_ids[index_values], route_weights[index_values], EXPERTS, capacity
        )
        packed = lax.dot_general(
            dispatch,
            stream[index_values],
            (((0,), (0,)), ((), ())),
            preferred_element_type=jnp.float32,
        )
        packed = packed.astype(jnp.bfloat16).reshape(
            wide_count, local_experts, capacity, stream.shape[2]
        )
        back = (
            lambda rows_in: expert_block(
                lax.all_gather(rows_in[None], "narrow", axis=0, tiled=True),
                norm_gain,
                w_gate,
                w_up,
                w_down,
            )
        )(lax.all_to_all(packed, "wide", split_axis=0, concat_axis=0, tiled=True))
        returned = back.reshape(wide_count * local_experts * capacity, back.shape[3]).astype(
            jnp.float32
        )
        mixed = jnp.dot(combine, returned, precision=lax.Precision.HIGHEST)
        outputs.append((stream[index_values].astype(jnp.float32) + mixed).astype(jnp.bfloat16))
    return jnp.stack(outputs)


def flip_permute(value, axis, mask):
    size = lax.axis_size(axis)
    return lax.ppermute(value, axis, [(i, i ^ mask) for i in range(size)])


def spread(value):
    got = {s: flip_permute(value, "wide", s) for s in (1, 3, 2)}
    return [got[1], got[2], got[3]]


def attend_kernel(*refs):
    given, out_ref, mixed_ref, held, sems = refs[:6], refs[6], refs[7], refs[8:14], refs[14]
    copies = [
        pltpu.make_async_copy(source, target, sems.at[i])
        for i, (source, target) in enumerate(zip(given, held))
    ]
    for copy in copies:
        copy.start()
    for copy in copies:
        copy.wait()
    len_ref, q_ref, k_ref, v_ref, ids_ref, wts_ref = held
    rows, heads = out_ref.shape[0], q_ref.shape[0] // out_ref.shape[0]
    width = q_ref.shape[1]
    slots = k_ref.shape[0] // rows
    group = 256 // slots
    micro, per_micro = len_ref.shape
    row_request = lax.broadcasted_iota(jnp.int32, (group * heads, group * slots), 0) // heads
    column = lax.broadcasted_iota(jnp.int32, (group * heads, group * slots), 1)
    place = column - row_request * slots
    scores = []
    limits = []
    for g in range(rows // group):
        limit = jnp.zeros_like(place)
        for i in range(group):
            r = g * group + i
            limit = jnp.where(row_request == i, len_ref[r // per_micro, r % per_micro], limit)
        limits.append(limit)
        scores.append(
            lax.dot_general(
                q_ref[g * group * heads:(g + 1) * group * heads, :],
                k_ref[g * group * slots:(g + 1) * group * slots, :],
                (((1,), (1,)), ((), ())),
                preferred_element_type=jnp.float32,
            )
        )
    place = jnp.concatenate([place] * len(scores), axis=0)
    usable = (place >= 0) & (place < jnp.concatenate(limits, axis=0))
    scores = jnp.concatenate(scores, axis=0) * (1.0 / math.sqrt(width))
    scores = jnp.where(usable, scores, -1e30)
    weight = jnp.exp(scores - jnp.max(scores, axis=-1, keepdims=True))
    probs = (weight / jnp.sum(weight, axis=-1, keepdims=True)).astype(jnp.bfloat16)
    for g in range(rows // group):
        mixed_ref[g * group * heads:(g + 1) * group * heads, :] = jnp.dot(
            probs[g * group * heads:(g + 1) * group * heads, :],
            v_ref[g * group * slots:(g + 1) * group * slots, :],
            preferred_element_type=jnp.float32,
        )
    for h in range(heads):
        out_ref[:, h * width:(h + 1) * width] = mixed_ref[
            pl.ds(h, rows, stride=heads), :
        ].astype(jnp.bfloat16)
    lanes = 64
    expert = lax.broadcasted_iota(jnp.int32, (lanes, per_micro), 0)
    eye = (
        lax.broadcasted_iota(jnp.int32, (per_micro, per_micro), 0)
        == lax.broadcasted_iota(jnp.int32, (per_micro, per_micro), 1)
    ).astype(jnp.bfloat16)
    for m in range(micro):
        total = jnp.zeros((lanes, per_micro), jnp.float32)
        for t in range(ids_ref.shape[1]):
            total += jnp.where(
                expert == ids_ref[m, t:t + 1, :], wts_ref[m, t:t + 1, :], 0.0
            )
        high = total.astype(jnp.bfloat16)
        low = (total - high.astype(jnp.float32)).astype(jnp.bfloat16)
        both = jnp.concatenate([high, low], axis=0)
        out_ref[m * per_micro:(m + 1) * per_micro, heads * width:] = lax.dot_general(
            eye, both, (((1,), (1,)), ((), ())), preferred_element_type=jnp.float32
        ).astype(jnp.bfloat16)


def project_kernel(where_ref, own_ref, got1_ref, got2_ref, got3_ref, w_ref, res_ref,
                   keep_ref, send_ref, mix_ref):
    wide, narrow = where_ref[0], where_ref[1]
    depth = w_ref.shape[0]
    half = keep_ref.shape[1]
    rows = own_ref.shape[0]
    features = jnp.concatenate(
        [r[:, :depth] for r in (own_ref, got1_ref, got2_ref, got3_ref)], axis=0
    )
    mine = pl.ds(pl.multiple_of((narrow & 1) * half, half), half)
    other = pl.ds(pl.multiple_of((1 - (narrow & 1)) * half, half), half)
    spot = pl.ds(pl.multiple_of((wide ^ narrow) * rows, rows), rows)
    keep_ref[...] = jnp.dot(features, w_ref[:, mine], preferred_element_type=jnp.float32)
    keep_ref[spot, :] += res_ref[:, mine].astype(jnp.float32)
    part = jnp.dot(features, w_ref[:, other], preferred_element_type=jnp.float32)
    part_rows = lax.broadcasted_iota(jnp.int32, part.shape, 0) // rows
    extra = res_ref[:, other].astype(jnp.float32)
    extra = jnp.concatenate([extra] * (part.shape[0] // rows), axis=0)
    part = jnp.where(part_rows == (wide ^ narrow), part + extra, part)
    send_ref[...] = part.astype(jnp.bfloat16)
    mix_ref[...] = jnp.concatenate(
        [r[:, depth:] for r in (own_ref, got1_ref, got2_ref, got3_ref)], axis=0
    )


def expert_kernel(where_ref, mine_ref, other_ref, mix_ref, gain_ref,
                  wg_ref, wu_ref, wd_ref, keep_ref, send_ref, stream_ref,
                  x_ref, hid_ref):
    wide, narrow = where_ref[0], where_ref[1]
    core = narrow & 1
    blocks, total, half = mine_ref.shape
    rows = total // blocks
    experts, depth, width = wg_ref.shape
    block = 2 * half
    square = jnp.zeros((total, 1), jnp.float32)
    for s in range(blocks):
        for piece, side in ((mine_ref, core), (other_ref, 1 - core)):
            place = pl.multiple_of((wide ^ s) * (2 * half) + side * half, half)
            lifted = jnp.concatenate(
                [piece[s, (u ^ s) * rows:((u ^ s) + 1) * rows, :] for u in range(blocks)], axis=0
            )
            x_ref[:, pl.ds(place, half)] = lifted
            value = lifted.astype(jnp.float32)
            square += jnp.sum(value * value, axis=1, keepdims=True)
    own = pl.multiple_of(narrow * (2 * half), 2 * half)
    stream_ref[...] = x_ref[:rows, pl.ds(own, 2 * half)]
    scale = lax.rsqrt(square * (1.0 / depth) + 1e-6)
    for b in range(depth // 512):
        cols = slice(b * 512, (b + 1) * 512)
        x_ref[:, cols] = (
            x_ref[:, cols].astype(jnp.float32) * scale * gain_ref[:, cols]
        ).astype(jnp.bfloat16)
    mix = mix_ref[...]
    lane = lax.broadcasted_iota(jnp.int32, (mix.shape[1], width), 0) % (mix.shape[1] // 2)

    for e in range(experts):
        gate = jnp.dot(x_ref[...], wg_ref[e], preferred_element_type=jnp.float32)
        upper = jnp.dot(x_ref[...], wu_ref[e], preferred_element_type=jnp.float32)
        pick = (lane == wide * experts + e).astype(jnp.bfloat16)
        share = jnp.dot(mix, pick, preferred_element_type=jnp.float32)
        hidden = gate / (1.0 + jnp.exp(-gate)) * upper * share
        hid_ref[:, e * width:(e + 1) * width] = hidden.astype(jnp.bfloat16)
    side = (narrow >> 1) ^ core
    for target, place in ((send_ref, 1 - side), (keep_ref, side)):
        for k in range(2):
            start = pl.multiple_of((2 * place + k) * block, block)
            out = jnp.dot(
                hid_ref[...], wd_ref[:, pl.ds(start, block)], preferred_element_type=jnp.float32
            )
            target[:, k * block:(k + 1) * block] = out.astype(target.dtype)


def local_small(
    queries,
    key_cache,
    cached_value_rows,
    lengths,
    residual,
    w_out,
    norm_gain,
    expert_ids,
    route_weights,
    w_gate,
    w_up,
    w_down,
):
    micro, per_micro, heads, width = queries.shape
    rows = micro * per_micro
    depth, columns = w_out.shape
    experts, model, hidden = w_gate.shape
    half = columns // 2
    vmem = pl.BlockSpec(memory_space=pltpu.VMEM)
    smem = pl.BlockSpec(memory_space=pltpu.SMEM)
    wide, narrow = lax.axis_index("wide"), lax.axis_index("narrow")
    where = jnp.stack([wide, narrow]).astype(jnp.int32)
    size = lax.axis_size("wide")
    turned = lax.ppermute(
        residual.reshape(rows, columns),
        ("wide", "narrow"),
        [(i, (i % size) * size + i // size) for i in range(size * size)],
    )
    given = (
        lengths,
        queries.reshape(rows * heads, width),
        key_cache.reshape(-1, width),
        cached_value_rows.reshape(-1, width),
        expert_ids.transpose(0, 2, 1),
        route_weights.transpose(0, 2, 1),
    )
    payload = pl.pallas_call(
        attend_kernel,
        out_shape=jax.ShapeDtypeStruct((rows, depth + 128), jnp.bfloat16),
        in_specs=[pl.BlockSpec(memory_space=pl.ANY)] * 6,
        out_specs=vmem,
        scratch_shapes=[pltpu.VMEM((rows * heads, width), jnp.float32)]
        + [pltpu.SMEM(given[0].shape, given[0].dtype)]
        + [pltpu.VMEM(g.shape, g.dtype) for g in given[1:]]
        + [pltpu.SemaphoreType.DMA((6,))],
        cost_estimate=pl.CostEstimate(flops=20000000000, bytes_accessed=1000000, transcendentals=0),
        compiler_params=pltpu.CompilerParams(vmem_limit_bytes=6 * 2**20),
    )(*[pltpu.with_memory_space_constraint(g, pltpu.HBM) for g in given])
    payload, turned = lax.optimization_barrier((payload, turned))
    others = spread(payload)
    keep, send, mix = pl.pallas_call(
        project_kernel,
        out_shape=(
            jax.ShapeDtypeStruct((size * rows, half), jnp.float32),
            jax.ShapeDtypeStruct((size * rows, half), jnp.bfloat16),
            jax.ShapeDtypeStruct((size * rows, 128), jnp.bfloat16),
        ),
        in_specs=[smem] + [vmem] * 6,
        out_specs=(vmem, vmem, vmem),
        cost_estimate=pl.CostEstimate(flops=30000000000, bytes_accessed=1000000, transcendentals=0),
        compiler_params=pltpu.CompilerParams(vmem_limit_bytes=6 * 2**20),
    )(where, payload, *others, w_out, turned)
    part = (keep + flip_permute(send, "narrow", 1).astype(jnp.float32)).astype(jnp.bfloat16)
    stream = (
        part.astype(jnp.float32) + flip_permute(part, "narrow", 2).astype(jnp.float32)
    ).astype(jnp.bfloat16)
    mine = jnp.stack([stream] + spread(stream))
    other = flip_permute(mine, "narrow", 1)
    weights = [
        pltpu.with_memory_space_constraint(w, pltpu.VMEM)
        for w in (w_gate, w_up, w_down.reshape(experts * hidden, model))
    ]
    keep, send, own = pl.pallas_call(
        expert_kernel,
        out_shape=(
            pltpu.VMEM((size * rows, model // 2), jnp.float32),
            pltpu.VMEM((size * rows, model // 2), jnp.bfloat16),
            pltpu.VMEM((rows, columns), jnp.bfloat16),
        ),
        in_specs=[smem] + [vmem] * 7,
        out_specs=(vmem, vmem, vmem),
        scratch_shapes=[
            pltpu.VMEM((size * rows, model), jnp.bfloat16),
            pltpu.VMEM((size * rows, experts * hidden), jnp.bfloat16),
        ],
        compiler_params=pltpu.CompilerParams(vmem_limit_bytes=11 * 2**20),
    )(
        where,
        *[pltpu.with_memory_space_constraint(p, pltpu.VMEM) for p in (mine, other, mix)],
        norm_gain.reshape(1, model),
        *weights,
    )
    total = (keep + flip_permute(send, "narrow", 1).astype(jnp.float32)).astype(jnp.bfloat16)
    total = total.reshape(size, rows, model // 2)
    devices = range(size * size)
    got = [
        lax.ppermute(
            total[s],
            ("wide", "narrow"),
            [(i, i ^ (s * size) ^ (2 if i & 1 else 0)) for i in devices],
        ).astype(jnp.float32)
        for s in (2, 1, 3, 0)
    ]
    summed = got[0] + got[1] + got[2] + got[3]
    first = (narrow & 1) == 0
    left, right = summed[:, :columns], summed[:, columns:]
    cross = flip_permute(jnp.where(first, right, left).astype(jnp.bfloat16), "narrow", 1)
    result = own.astype(jnp.float32) + jnp.where(first, left, right) + cross.astype(jnp.float32)
    return result.astype(jnp.bfloat16).reshape(micro, per_micro, columns)


def solution(mesh):
    in_specs = (
        P(None, ("grp", "wide"), "narrow", None),
        P(None, ("grp", "wide"), None, "narrow", None),
        P(None, ("grp", "wide"), None, "narrow", None),
        P(None, ("grp", "wide")),
        P(None, ("grp", "wide"), "narrow"),
        P("narrow", "wide"),
        P(),
        P(None, ("grp", "wide"), None),
        P(None, ("grp", "wide"), None),
        P("wide", None, "narrow"),
        P("wide", None, "narrow"),
        P("wide", "narrow", None),
    )
    out_specs = P(None, ("grp", "wide"), "narrow")
    small = mesh.shape["wide"] == 4 and mesh.shape["narrow"] == 4
    body = local_small if small else local
    return jax.shard_map(body, mesh=mesh, in_specs=in_specs, out_specs=out_specs, check_vma=False)
```

```python
import math

import jax
import jax.numpy as jnp
from jax import lax
from jax.experimental import pallas as pl
from jax.experimental.pallas import tpu as pltpu
from jax.sharding import PartitionSpec as P

EXPERTS = 64
CAP = 3


def attend(query_rows, keys, values, valid_len):
    row_count, q_heads, head_size = query_rows.shape
    slot_count = keys.shape[1]
    kv_heads = keys.shape[2]
    flat_keys = keys.reshape(row_count, slot_count, kv_heads * head_size)
    flat_values = values.reshape(row_count, slot_count, kv_heads * head_size)
    position = jnp.arange(slot_count)
    usable = position[None, :] < valid_len[:, None]
    scores = jnp.einsum(
        "rgd,rcd->rgc", query_rows, flat_keys, preferred_element_type=jnp.float32
    ) / math.sqrt(head_size)
    scores = jnp.where(usable[:, None, :], scores, -1e30)
    largest = jnp.max(scores, axis=-1, keepdims=True)
    weight = jnp.exp(scores - largest)
    probs = (weight / jnp.sum(weight, axis=-1, keepdims=True)).astype(jnp.bfloat16)
    mixed = jnp.einsum("rgc,rcd->rgd", probs, flat_values, preferred_element_type=jnp.float32)
    results = mixed.astype(jnp.bfloat16)
    return results.reshape(row_count, q_heads * head_size)


def route_tables(chosen, weights, expert_count, capacity):
    row_count, top_count = chosen.shape
    pairs = chosen.reshape(-1)
    onehot = (pairs[:, None] == jnp.arange(expert_count)[None, :]).astype(jnp.int32)
    before = jnp.cumsum(onehot, axis=0) - onehot
    rank = jnp.sum(onehot * before, axis=1)
    slot = pairs * capacity + rank
    select = (slot[:, None] == jnp.arange(expert_count * capacity)[None, :]).astype(jnp.float32)
    select = select.reshape(row_count, top_count, expert_count * capacity)
    dispatch = jnp.sum(select, axis=1).astype(jnp.bfloat16)
    combine = jnp.sum(select * weights[:, :, None], axis=1)
    return (dispatch, combine)


def expert_block(pieces, norm_gain, w_gate, w_up, w_down):
    parts_count = pieces.shape[0]
    local_experts, model_width, hidden_width = w_gate.shape
    part_width = model_width // parts_count
    values = pieces.astype(jnp.float32)
    square = jnp.mean(values * values, axis=(0, 4), keepdims=True)
    gain_parts = norm_gain.reshape(parts_count, 1, 1, 1, part_width)
    normed = (values * lax.rsqrt(square + 1e-06) * gain_parts).astype(jnp.bfloat16)
    gate_parts = w_gate.reshape(local_experts, parts_count, part_width, hidden_width)
    up_parts = w_up.reshape(local_experts, parts_count, part_width, hidden_width)
    gate = jnp.einsum("nsjcd,jndf->sjcf", normed, gate_parts, preferred_element_type=jnp.float32)
    upper = jnp.einsum("nsjcd,jndf->sjcf", normed, up_parts, preferred_element_type=jnp.float32)
    hidden = (jax.nn.silu(gate) * upper).astype(jnp.bfloat16)
    narrow_count = lax.axis_size("narrow")
    down_parts = w_down.reshape(
        local_experts, w_down.shape[1], narrow_count, model_width // narrow_count
    )
    partial_out = jnp.einsum(
        "sjcf,jfnd->nsjcd", hidden, down_parts, preferred_element_type=jnp.float32
    )
    summed = lax.psum_scatter(
        partial_out.astype(jnp.bfloat16), "narrow", scatter_dimension=0, tiled=True
    ).astype(jnp.float32)[0]
    return lax.all_to_all(
        summed.astype(jnp.bfloat16), "wide", split_axis=0, concat_axis=0, tiled=True
    )


def local(
    queries,
    key_cache,
    cached_value_rows,
    lengths,
    residual,
    w_out,
    norm_gain,
    expert_ids,
    route_weights,
    w_gate,
    w_up,
    w_down,
):
    micro_count = queries.shape[0]
    wide_count = lax.axis_size("wide")
    local_experts = w_gate.shape[0]
    capacity = CAP
    attended = [
        attend(
            queries[index_values],
            key_cache[index_values],
            cached_value_rows[index_values],
            lengths[index_values],
        )
        for index_values in range(micro_count)
    ]
    terms = []
    for index_values in range(micro_count):
        columns = jnp.dot(
            lax.all_gather(attended[index_values], "wide", axis=0, tiled=True),
            w_out,
            preferred_element_type=jnp.float32,
        )
        terms.append(
            lax.all_to_all(
                columns.astype(jnp.bfloat16), "wide", split_axis=0, concat_axis=1, tiled=True
            ).astype(columns.dtype)
        )
    partial_sum = jnp.stack(terms)
    projected = lax.psum_scatter(
        partial_sum.astype(jnp.bfloat16), "narrow", scatter_dimension=2, tiled=True
    ).astype(jnp.float32)
    stream = (residual.astype(jnp.float32) + projected).astype(jnp.bfloat16)
    outputs = []
    for index_values in range(micro_count):
        dispatch, combine = route_tables(
            expert_ids[index_values], route_weights[index_values], EXPERTS, capacity
        )
        packed = lax.dot_general(
            dispatch,
            stream[index_values],
            (((0,), (0,)), ((), ())),
            preferred_element_type=jnp.float32,
        )
        packed = packed.astype(jnp.bfloat16).reshape(
            wide_count, local_experts, capacity, stream.shape[2]
        )
        back = (
            lambda rows_in: expert_block(
                lax.all_gather(rows_in[None], "narrow", axis=0, tiled=True),
                norm_gain,
                w_gate,
                w_up,
                w_down,
            )
        )(lax.all_to_all(packed, "wide", split_axis=0, concat_axis=0, tiled=True))
        returned = back.reshape(wide_count * local_experts * capacity, back.shape[3]).astype(
            jnp.float32
        )
        mixed = jnp.dot(combine, returned, precision=lax.Precision.HIGHEST)
        outputs.append((stream[index_values].astype(jnp.float32) + mixed).astype(jnp.bfloat16))
    return jnp.stack(outputs)


def flip_permute(value, axis, mask):
    size = lax.axis_size(axis)
    return lax.ppermute(value, axis, [(i, i ^ mask) for i in range(size)])


def spread(value):
    got = {s: flip_permute(value, "wide", s) for s in (1, 3, 2)}
    return [got[1], got[2], got[3]]


def attend_kernel(*refs):
    given, out_ref, mixed_ref, held, sems = refs[:6], refs[6], refs[7], refs[8:14], refs[14]
    copies = [
        pltpu.make_async_copy(source, target, sems.at[i])
        for i, (source, target) in enumerate(zip(given, held))
    ]
    for copy in copies:
        copy.start()
    for copy in copies:
        copy.wait()
    len_ref, q_ref, k_ref, v_ref, ids_ref, wts_ref = held
    rows, heads = out_ref.shape[0], q_ref.shape[0] // out_ref.shape[0]
    width = q_ref.shape[1]
    slots = k_ref.shape[0] // rows
    group = 256 // slots
    micro, per_micro = len_ref.shape
    row_request = lax.broadcasted_iota(jnp.int32, (group * heads, group * slots), 0) // heads
    column = lax.broadcasted_iota(jnp.int32, (group * heads, group * slots), 1)
    place = column - row_request * slots
    scores = []
    limits = []
    for g in range(rows // group):
        limit = jnp.zeros_like(place)
        for i in range(group):
            r = g * group + i
            limit = jnp.where(row_request == i, len_ref[r // per_micro, r % per_micro], limit)
        limits.append(limit)
        scores.append(
            lax.dot_general(
                q_ref[g * group * heads:(g + 1) * group * heads, :],
                k_ref[g * group * slots:(g + 1) * group * slots, :],
                (((1,), (1,)), ((), ())),
                preferred_element_type=jnp.float32,
            )
        )
    place = jnp.concatenate([place] * len(scores), axis=0)
    usable = (place >= 0) & (place < jnp.concatenate(limits, axis=0))
    scores = jnp.concatenate(scores, axis=0) * (1.0 / math.sqrt(width))
    scores = jnp.where(usable, scores, -1e30)
    weight = jnp.exp(scores - jnp.max(scores, axis=-1, keepdims=True))
    probs = (weight / jnp.sum(weight, axis=-1, keepdims=True)).astype(jnp.bfloat16)
    for g in range(rows // group):
        mixed_ref[g * group * heads:(g + 1) * group * heads, :] = jnp.dot(
            probs[g * group * heads:(g + 1) * group * heads, :],
            v_ref[g * group * slots:(g + 1) * group * slots, :],
            preferred_element_type=jnp.float32,
        )
    for h in range(heads):
        out_ref[:, h * width:(h + 1) * width] = mixed_ref[
            pl.ds(h, rows, stride=heads), :
        ].astype(jnp.bfloat16)
    lanes = 64
    expert = lax.broadcasted_iota(jnp.int32, (lanes, per_micro), 0)
    eye = (
        lax.broadcasted_iota(jnp.int32, (per_micro, per_micro), 0)
        == lax.broadcasted_iota(jnp.int32, (per_micro, per_micro), 1)
    ).astype(jnp.bfloat16)
    for m in range(micro):
        total = jnp.zeros((lanes, per_micro), jnp.float32)
        for t in range(ids_ref.shape[1]):
            total += jnp.where(
                expert == ids_ref[m, t:t + 1, :], wts_ref[m, t:t + 1, :], 0.0
            )
        high = total.astype(jnp.bfloat16)
        low = (total - high.astype(jnp.float32)).astype(jnp.bfloat16)
        both = jnp.concatenate([high, low], axis=0)
        out_ref[m * per_micro:(m + 1) * per_micro, heads * width:] = lax.dot_general(
            eye, both, (((1,), (1,)), ((), ())), preferred_element_type=jnp.float32
        ).astype(jnp.bfloat16)


def project_kernel(where_ref, own_ref, got1_ref, got2_ref, got3_ref, w_ref, res_ref,
                   keep_ref, send_ref, mix_ref):
    wide, narrow = where_ref[0], where_ref[1]
    depth = w_ref.shape[0]
    half = keep_ref.shape[1]
    rows = own_ref.shape[0]
    features = jnp.concatenate(
        [r[:, :depth] for r in (own_ref, got1_ref, got2_ref, got3_ref)], axis=0
    )
    mine = pl.ds(pl.multiple_of((narrow & 1) * half, half), half)
    other = pl.ds(pl.multiple_of((1 - (narrow & 1)) * half, half), half)
    spot = pl.ds(pl.multiple_of((wide ^ where_ref[2]) * rows, rows), rows)
    keep_ref[...] = jnp.dot(features, w_ref[:, mine], preferred_element_type=jnp.float32)
    keep_ref[spot, :] += res_ref[:, mine].astype(jnp.float32)
    part = jnp.dot(features, w_ref[:, other], preferred_element_type=jnp.float32)
    part_rows = lax.broadcasted_iota(jnp.int32, part.shape, 0) // rows
    extra = res_ref[:, other].astype(jnp.float32)
    extra = jnp.concatenate([extra] * (part.shape[0] // rows), axis=0)
    part = jnp.where(part_rows == (wide ^ where_ref[2]), part + extra, part)
    send_ref[...] = part.astype(jnp.bfloat16)
    mix_ref[...] = jnp.concatenate(
        [r[:, depth:] for r in (own_ref, got1_ref, got2_ref, got3_ref)], axis=0
    )


def expert_kernel(where_ref, mine_ref, other_ref, mix_ref, gain_ref,
                  wg_ref, wu_ref, wd_ref, keep_ref, send_ref, stream_ref,
                  x_ref, hid_ref):
    wide, narrow = where_ref[0], where_ref[1]
    core = narrow & 1
    blocks, total, half = mine_ref.shape
    rows = total // blocks
    experts, depth, width = wg_ref.shape
    block = 2 * half
    square = jnp.zeros((total, 1), jnp.float32)
    for s in range(blocks):
        for piece, side in ((mine_ref, core), (other_ref, 1 - core)):
            place = pl.multiple_of((wide ^ s) * (2 * half) + side * half, half)
            lifted = jnp.concatenate(
                [piece[s, (u ^ s) * rows:((u ^ s) + 1) * rows, :] for u in range(blocks)], axis=0
            )
            x_ref[:, pl.ds(place, half)] = lifted
            value = lifted.astype(jnp.float32)
            square += jnp.sum(value * value, axis=1, keepdims=True)
    own = pl.multiple_of(narrow * (2 * half), 2 * half)
    stream_ref[...] = x_ref[:rows, pl.ds(own, 2 * half)]
    scale = lax.rsqrt(square * (1.0 / depth) + 1e-6)
    for b in range(depth // 512):
        cols = slice(b * 512, (b + 1) * 512)
        x_ref[:, cols] = (
            x_ref[:, cols].astype(jnp.float32) * scale * gain_ref[:, cols]
        ).astype(jnp.bfloat16)
    mix = mix_ref[...]
    lane = lax.broadcasted_iota(jnp.int32, (mix.shape[1], width), 0) % (mix.shape[1] // 2)

    for e in range(experts):
        gate = jnp.dot(x_ref[...], wg_ref[e], preferred_element_type=jnp.float32)
        upper = jnp.dot(x_ref[...], wu_ref[e], preferred_element_type=jnp.float32)
        pick = (lane == wide * experts + e).astype(jnp.bfloat16)
        share = jnp.dot(mix, pick, preferred_element_type=jnp.float32)
        hidden = gate / (1.0 + jnp.exp(-gate)) * upper * share
        hid_ref[:, e * width:(e + 1) * width] = hidden.astype(jnp.bfloat16)
    side = (narrow >> 1) ^ core
    for target, place in ((send_ref, 1 - side), (keep_ref, side)):
        for k in range(2):
            start = pl.multiple_of((2 * place + k) * block, block)
            out = jnp.dot(
                hid_ref[...], wd_ref[:, pl.ds(start, block)], preferred_element_type=jnp.float32
            )
            target[:, k * block:(k + 1) * block] = out.astype(target.dtype)


def residual_route(size):
    route = []
    for n in range(size):
        near = sorted(range(size), key=lambda w: abs(w - n))
        column = n >> 1
        places = [2 * (column ^ 1), 2 * (column ^ 1) + 1, 2 * column, 2 * column + 1]
        route += [(w, n, to) for w, to in zip(near, places)]
    return route


def local_small(
    queries,
    key_cache,
    cached_value_rows,
    lengths,
    residual,
    w_out,
    norm_gain,
    expert_ids,
    route_weights,
    w_gate,
    w_up,
    w_down,
):
    micro, per_micro, heads, width = queries.shape
    rows = micro * per_micro
    depth, columns = w_out.shape
    experts, model, hidden = w_gate.shape
    half = columns // 2
    vmem = pl.BlockSpec(memory_space=pltpu.VMEM)
    smem = pl.BlockSpec(memory_space=pltpu.SMEM)
    wide, narrow = lax.axis_index("wide"), lax.axis_index("narrow")
    size = lax.axis_size("wide")
    route = residual_route(size)
    source = jnp.zeros((), jnp.int32)
    for w, n, to in route:
        source = jnp.where((wide == n) & (narrow == to), w, source)
    where = jnp.stack([wide, narrow, source]).astype(jnp.int32)
    turned = lax.ppermute(
        residual.reshape(rows, columns),
        ("wide", "narrow"),
        [(w * size + n, n * size + to) for w, n, to in route],
    )
    given = (
        lengths,
        queries.reshape(rows * heads, width),
        key_cache.reshape(-1, width),
        cached_value_rows.reshape(-1, width),
        expert_ids.transpose(0, 2, 1),
        route_weights.transpose(0, 2, 1),
    )
    payload = pl.pallas_call(
        attend_kernel,
        out_shape=jax.ShapeDtypeStruct((rows, depth + 128), jnp.bfloat16),
        in_specs=[pl.BlockSpec(memory_space=pl.ANY)] * 6,
        out_specs=vmem,
        scratch_shapes=[pltpu.VMEM((rows * heads, width), jnp.float32)]
        + [pltpu.SMEM(given[0].shape, given[0].dtype)]
        + [pltpu.VMEM(g.shape, g.dtype) for g in given[1:]]
        + [pltpu.SemaphoreType.DMA((6,))],
        cost_estimate=pl.CostEstimate(flops=20000000000, bytes_accessed=1000000, transcendentals=0),
        compiler_params=pltpu.CompilerParams(vmem_limit_bytes=6 * 2**20),
    )(*[pltpu.with_memory_space_constraint(g, pltpu.HBM) for g in given])
    others = spread(payload)
    keep, send, mix = pl.pallas_call(
        project_kernel,
        out_shape=(
            jax.ShapeDtypeStruct((size * rows, half), jnp.float32),
            jax.ShapeDtypeStruct((size * rows, half), jnp.bfloat16),
            jax.ShapeDtypeStruct((size * rows, 128), jnp.bfloat16),
        ),
        in_specs=[smem] + [vmem] * 6,
        out_specs=(vmem, vmem, vmem),
        cost_estimate=pl.CostEstimate(flops=30000000000, bytes_accessed=1000000, transcendentals=0),
        compiler_params=pltpu.CompilerParams(vmem_limit_bytes=6 * 2**20),
    )(where, payload, *others, w_out, turned)
    part = (keep + flip_permute(send, "narrow", 1).astype(jnp.float32)).astype(jnp.bfloat16)
    stream = (
        part.astype(jnp.float32) + flip_permute(part, "narrow", 2).astype(jnp.float32)
    ).astype(jnp.bfloat16)
    mine = jnp.stack([stream] + spread(stream))
    other = flip_permute(mine, "narrow", 1)
    weights = [
        pltpu.with_memory_space_constraint(w, pltpu.VMEM)
        for w in (w_gate, w_up, w_down.reshape(experts * hidden, model))
    ]
    keep, send, own = pl.pallas_call(
        expert_kernel,
        out_shape=(
            pltpu.VMEM((size * rows, model // 2), jnp.float32),
            pltpu.VMEM((size * rows, model // 2), jnp.bfloat16),
            pltpu.VMEM((rows, columns), jnp.bfloat16),
        ),
        in_specs=[smem] + [vmem] * 7,
        out_specs=(vmem, vmem, vmem),
        scratch_shapes=[
            pltpu.VMEM((size * rows, model), jnp.bfloat16),
            pltpu.VMEM((size * rows, experts * hidden), jnp.bfloat16),
        ],
        compiler_params=pltpu.CompilerParams(vmem_limit_bytes=11 * 2**20),
    )(
        where,
        *[pltpu.with_memory_space_constraint(p, pltpu.VMEM) for p in (mine, other, mix)],
        norm_gain.reshape(1, model),
        *weights,
    )
    total = (keep + flip_permute(send, "narrow", 1).astype(jnp.float32)).astype(jnp.bfloat16)
    total = total.reshape(size, rows, model // 2)
    devices = range(size * size)
    got = [
        lax.ppermute(
            total[s],
            ("wide", "narrow"),
            [(i, i ^ (s * size) ^ (2 if i & 1 else 0)) for i in devices],
        ).astype(jnp.float32)
        for s in (2, 1, 3, 0)
    ]
    summed = got[0] + got[1] + got[2] + got[3]
    first = (narrow & 1) == 0
    left, right = summed[:, :columns], summed[:, columns:]
    cross = flip_permute(jnp.where(first, right, left).astype(jnp.bfloat16), "narrow", 1)
    result = own.astype(jnp.float32) + jnp.where(first, left, right) + cross.astype(jnp.float32)
    return result.astype(jnp.bfloat16).reshape(micro, per_micro, columns)


def solution(mesh):
    in_specs = (
        P(None, ("grp", "wide"), "narrow", None),
        P(None, ("grp", "wide"), None, "narrow", None),
        P(None, ("grp", "wide"), None, "narrow", None),
        P(None, ("grp", "wide")),
        P(None, ("grp", "wide"), "narrow"),
        P("narrow", "wide"),
        P(),
        P(None, ("grp", "wide"), None),
        P(None, ("grp", "wide"), None),
        P("wide", None, "narrow"),
        P("wide", None, "narrow"),
        P("wide", "narrow", None),
    )
    out_specs = P(None, ("grp", "wide"), "narrow")
    small = mesh.shape["wide"] == 4 and mesh.shape["narrow"] == 4
    body = local_small if small else local
    return jax.shard_map(body, mesh=mesh, in_specs=in_specs, out_specs=out_specs, check_vma=False)
```

```python
import math

import jax
import jax.numpy as jnp
from jax import lax
from jax.experimental import pallas as pl
from jax.experimental.pallas import tpu as pltpu
from jax.sharding import PartitionSpec as P

EXPERTS = 64
CAP = 3


def attend(query_rows, keys, values, valid_len):
    row_count, q_heads, head_size = query_rows.shape
    slot_count = keys.shape[1]
    kv_heads = keys.shape[2]
    flat_keys = keys.reshape(row_count, slot_count, kv_heads * head_size)
    flat_values = values.reshape(row_count, slot_count, kv_heads * head_size)
    position = jnp.arange(slot_count)
    usable = position[None, :] < valid_len[:, None]
    scores = jnp.einsum(
        "rgd,rcd->rgc", query_rows, flat_keys, preferred_element_type=jnp.float32
    ) / math.sqrt(head_size)
    scores = jnp.where(usable[:, None, :], scores, -1e30)
    largest = jnp.max(scores, axis=-1, keepdims=True)
    weight = jnp.exp(scores - largest)
    probs = (weight / jnp.sum(weight, axis=-1, keepdims=True)).astype(jnp.bfloat16)
    mixed = jnp.einsum("rgc,rcd->rgd", probs, flat_values, preferred_element_type=jnp.float32)
    results = mixed.astype(jnp.bfloat16)
    return results.reshape(row_count, q_heads * head_size)


def route_tables(chosen, weights, expert_count, capacity):
    row_count, top_count = chosen.shape
    pairs = chosen.reshape(-1)
    onehot = (pairs[:, None] == jnp.arange(expert_count)[None, :]).astype(jnp.int32)
    before = jnp.cumsum(onehot, axis=0) - onehot
    rank = jnp.sum(onehot * before, axis=1)
    slot = pairs * capacity + rank
    select = (slot[:, None] == jnp.arange(expert_count * capacity)[None, :]).astype(jnp.float32)
    select = select.reshape(row_count, top_count, expert_count * capacity)
    dispatch = jnp.sum(select, axis=1).astype(jnp.bfloat16)
    combine = jnp.sum(select * weights[:, :, None], axis=1)
    return (dispatch, combine)


def expert_block(pieces, norm_gain, w_gate, w_up, w_down):
    parts_count = pieces.shape[0]
    local_experts, model_width, hidden_width = w_gate.shape
    part_width = model_width // parts_count
    values = pieces.astype(jnp.float32)
    square = jnp.mean(values * values, axis=(0, 4), keepdims=True)
    gain_parts = norm_gain.reshape(parts_count, 1, 1, 1, part_width)
    normed = (values * lax.rsqrt(square + 1e-06) * gain_parts).astype(jnp.bfloat16)
    gate_parts = w_gate.reshape(local_experts, parts_count, part_width, hidden_width)
    up_parts = w_up.reshape(local_experts, parts_count, part_width, hidden_width)
    gate = jnp.einsum("nsjcd,jndf->sjcf", normed, gate_parts, preferred_element_type=jnp.float32)
    upper = jnp.einsum("nsjcd,jndf->sjcf", normed, up_parts, preferred_element_type=jnp.float32)
    hidden = (jax.nn.silu(gate) * upper).astype(jnp.bfloat16)
    narrow_count = lax.axis_size("narrow")
    down_parts = w_down.reshape(
        local_experts, w_down.shape[1], narrow_count, model_width // narrow_count
    )
    partial_out = jnp.einsum(
        "sjcf,jfnd->nsjcd", hidden, down_parts, preferred_element_type=jnp.float32
    )
    summed = lax.psum_scatter(
        partial_out.astype(jnp.bfloat16), "narrow", scatter_dimension=0, tiled=True
    ).astype(jnp.float32)[0]
    return lax.all_to_all(
        summed.astype(jnp.bfloat16), "wide", split_axis=0, concat_axis=0, tiled=True
    )


def local(
    queries,
    key_cache,
    cached_value_rows,
    lengths,
    residual,
    w_out,
    norm_gain,
    expert_ids,
    route_weights,
    w_gate,
    w_up,
    w_down,
):
    micro_count = queries.shape[0]
    wide_count = lax.axis_size("wide")
    local_experts = w_gate.shape[0]
    capacity = CAP
    attended = [
        attend(
            queries[index_values],
            key_cache[index_values],
            cached_value_rows[index_values],
            lengths[index_values],
        )
        for index_values in range(micro_count)
    ]
    terms = []
    for index_values in range(micro_count):
        columns = jnp.dot(
            lax.all_gather(attended[index_values], "wide", axis=0, tiled=True),
            w_out,
            preferred_element_type=jnp.float32,
        )
        terms.append(
            lax.all_to_all(
                columns.astype(jnp.bfloat16), "wide", split_axis=0, concat_axis=1, tiled=True
            ).astype(columns.dtype)
        )
    partial_sum = jnp.stack(terms)
    projected = lax.psum_scatter(
        partial_sum.astype(jnp.bfloat16), "narrow", scatter_dimension=2, tiled=True
    ).astype(jnp.float32)
    stream = (residual.astype(jnp.float32) + projected).astype(jnp.bfloat16)
    outputs = []
    for index_values in range(micro_count):
        dispatch, combine = route_tables(
            expert_ids[index_values], route_weights[index_values], EXPERTS, capacity
        )
        packed = lax.dot_general(
            dispatch,
            stream[index_values],
            (((0,), (0,)), ((), ())),
            preferred_element_type=jnp.float32,
        )
        packed = packed.astype(jnp.bfloat16).reshape(
            wide_count, local_experts, capacity, stream.shape[2]
        )
        back = (
            lambda rows_in: expert_block(
                lax.all_gather(rows_in[None], "narrow", axis=0, tiled=True),
                norm_gain,
                w_gate,
                w_up,
                w_down,
            )
        )(lax.all_to_all(packed, "wide", split_axis=0, concat_axis=0, tiled=True))
        returned = back.reshape(wide_count * local_experts * capacity, back.shape[3]).astype(
            jnp.float32
        )
        mixed = jnp.dot(combine, returned, precision=lax.Precision.HIGHEST)
        outputs.append((stream[index_values].astype(jnp.float32) + mixed).astype(jnp.bfloat16))
    return jnp.stack(outputs)


def flip_permute(value, axis, mask):
    size = lax.axis_size(axis)
    return lax.ppermute(value, axis, [(i, i ^ mask) for i in range(size)])


def spread(value):
    got = {s: flip_permute(value, "wide", s) for s in (1, 3, 2)}
    return [got[1], got[2], got[3]]


def attend_kernel(*refs):
    given, out_ref, mixed_ref, held, sems = refs[:6], refs[6], refs[7], refs[8:14], refs[14]
    copies = [
        pltpu.make_async_copy(source, target, sems.at[i])
        for i, (source, target) in enumerate(zip(given, held))
    ]
    for copy in copies:
        copy.start()
    for copy in copies:
        copy.wait()
    len_ref, q_ref, k_ref, v_ref, ids_ref, wts_ref = held
    rows, heads = out_ref.shape[0], q_ref.shape[0] // out_ref.shape[0]
    width = q_ref.shape[1]
    slots = k_ref.shape[0] // rows
    group = 256 // slots
    micro, per_micro = len_ref.shape
    row_request = lax.broadcasted_iota(jnp.int32, (group * heads, group * slots), 0) // heads
    column = lax.broadcasted_iota(jnp.int32, (group * heads, group * slots), 1)
    place = column - row_request * slots
    scores = []
    limits = []
    for g in range(rows // group):
        limit = jnp.zeros_like(place)
        for i in range(group):
            r = g * group + i
            limit = jnp.where(row_request == i, len_ref[r // per_micro, r % per_micro], limit)
        limits.append(limit)
        scores.append(
            lax.dot_general(
                q_ref[g * group * heads:(g + 1) * group * heads, :],
                k_ref[g * group * slots:(g + 1) * group * slots, :],
                (((1,), (1,)), ((), ())),
                preferred_element_type=jnp.float32,
            )
        )
    place = jnp.concatenate([place] * len(scores), axis=0)
    usable = (place >= 0) & (place < jnp.concatenate(limits, axis=0))
    scores = jnp.concatenate(scores, axis=0) * (1.0 / math.sqrt(width))
    scores = jnp.where(usable, scores, -1e30)
    weight = jnp.exp(scores - jnp.max(scores, axis=-1, keepdims=True))
    probs = (weight / jnp.sum(weight, axis=-1, keepdims=True)).astype(jnp.bfloat16)
    for g in range(rows // group):
        mixed_ref[g * group * heads:(g + 1) * group * heads, :] = jnp.dot(
            probs[g * group * heads:(g + 1) * group * heads, :],
            v_ref[g * group * slots:(g + 1) * group * slots, :],
            preferred_element_type=jnp.float32,
        )
    for h in range(heads):
        out_ref[:, h * width:(h + 1) * width] = mixed_ref[
            pl.ds(h, rows, stride=heads), :
        ].astype(jnp.bfloat16)
    lanes = 64
    expert = lax.broadcasted_iota(jnp.int32, (lanes, per_micro), 0)
    eye = (
        lax.broadcasted_iota(jnp.int32, (per_micro, per_micro), 0)
        == lax.broadcasted_iota(jnp.int32, (per_micro, per_micro), 1)
    ).astype(jnp.bfloat16)
    for m in range(micro):
        total = jnp.zeros((lanes, per_micro), jnp.float32)
        for t in range(ids_ref.shape[1]):
            total += jnp.where(
                expert == ids_ref[m, t:t + 1, :], wts_ref[m, t:t + 1, :], 0.0
            )
        high = total.astype(jnp.bfloat16)
        low = (total - high.astype(jnp.float32)).astype(jnp.bfloat16)
        both = jnp.concatenate([high, low], axis=0)
        out_ref[m * per_micro:(m + 1) * per_micro, heads * width:] = lax.dot_general(
            eye, both, (((1,), (1,)), ((), ())), preferred_element_type=jnp.float32
        ).astype(jnp.bfloat16)


def project_kernel(where_ref, own_ref, got1_ref, got2_ref, got3_ref, w_ref, res_ref,
                   keep_ref, send_ref, mix_ref):
    wide, narrow = where_ref[0], where_ref[1]
    depth = w_ref.shape[0]
    half = keep_ref.shape[1]
    rows = own_ref.shape[0]
    features = jnp.concatenate(
        [r[:, :depth] for r in (own_ref, got1_ref, got2_ref, got3_ref)], axis=0
    )
    mine = pl.ds(pl.multiple_of((narrow & 1) * half, half), half)
    other = pl.ds(pl.multiple_of((1 - (narrow & 1)) * half, half), half)
    spot = pl.ds(pl.multiple_of((wide ^ where_ref[2]) * rows, rows), rows)
    keep_ref[...] = jnp.dot(features, w_ref[:, mine], preferred_element_type=jnp.float32)
    keep_ref[spot, :] += res_ref[:, mine].astype(jnp.float32)
    part = jnp.dot(features, w_ref[:, other], preferred_element_type=jnp.float32)
    part_rows = lax.broadcasted_iota(jnp.int32, part.shape, 0) // rows
    extra = res_ref[:, other].astype(jnp.float32)
    extra = jnp.concatenate([extra] * (part.shape[0] // rows), axis=0)
    part = jnp.where(part_rows == (wide ^ where_ref[2]), part + extra, part)
    send_ref[...] = part.astype(jnp.bfloat16)
    mix_ref[...] = jnp.concatenate(
        [r[:, depth:] for r in (own_ref, got1_ref, got2_ref, got3_ref)], axis=0
    )


def expert_kernel(where_ref, mine_ref, other_ref, mix_ref, gain_ref,
                  wg_ref, wu_ref, wd_ref, keep_ref, send_ref, stream_ref,
                  x_ref, hid_ref):
    wide, narrow = where_ref[0], where_ref[1]
    core = narrow & 1
    blocks, total, half = mine_ref.shape
    rows = total // blocks
    experts, depth, width = wg_ref.shape
    block = 2 * half
    square = jnp.zeros((total, 1), jnp.float32)
    for s in range(blocks):
        for piece, side in ((mine_ref, core), (other_ref, 1 - core)):
            place = pl.multiple_of((wide ^ s) * (2 * half) + side * half, half)
            lifted = jnp.concatenate(
                [piece[s, (u ^ s) * rows:((u ^ s) + 1) * rows, :] for u in range(blocks)], axis=0
            )
            x_ref[:, pl.ds(place, half)] = lifted
            value = lifted.astype(jnp.float32)
            square += jnp.sum(value * value, axis=1, keepdims=True)
    own = pl.multiple_of(narrow * (2 * half), 2 * half)
    stream_ref[...] = x_ref[:rows, pl.ds(own, 2 * half)]
    scale = lax.rsqrt(square * (1.0 / depth) + 1e-6)
    for b in range(depth // 512):
        cols = slice(b * 512, (b + 1) * 512)
        x_ref[:, cols] = (
            x_ref[:, cols].astype(jnp.float32) * scale * gain_ref[:, cols]
        ).astype(jnp.bfloat16)
    mix = mix_ref[...]
    lane = lax.broadcasted_iota(jnp.int32, (mix.shape[1], width), 0) % (mix.shape[1] // 2)

    for e in range(experts):
        gate = jnp.dot(x_ref[...], wg_ref[e], preferred_element_type=jnp.float32)
        upper = jnp.dot(x_ref[...], wu_ref[e], preferred_element_type=jnp.float32)
        pick = (lane == wide * experts + e).astype(jnp.bfloat16)
        share = jnp.dot(mix, pick, preferred_element_type=jnp.float32)
        hidden = gate / (1.0 + jnp.exp(-gate)) * upper * share
        hid_ref[:, e * width:(e + 1) * width] = hidden.astype(jnp.bfloat16)
    side = (narrow >> 1) ^ core
    for target, place in ((send_ref, 1 - side), (keep_ref, side)):
        for k in range(2):
            start = pl.multiple_of((2 * place + k) * block, block)
            out = jnp.dot(
                hid_ref[...], wd_ref[:, pl.ds(start, block)], preferred_element_type=jnp.float32
            )
            target[:, k * block:(k + 1) * block] = out.astype(target.dtype)


def residual_route(size):
    route = []
    for n in range(size):
        near = sorted(range(size), key=lambda w: abs(w - n))
        column = n >> 1
        places = [2 * (column ^ 1), 2 * (column ^ 1) + 1, 2 * column, 2 * column + 1]
        route += [(w, n, to) for w, to in zip(near, places)]
    return route


def local_small(
    queries,
    key_cache,
    cached_value_rows,
    lengths,
    residual,
    w_out,
    norm_gain,
    expert_ids,
    route_weights,
    w_gate,
    w_up,
    w_down,
):
    micro, per_micro, heads, width = queries.shape
    rows = micro * per_micro
    depth, columns = w_out.shape
    experts, model, hidden = w_gate.shape
    half = columns // 2
    vmem = pl.BlockSpec(memory_space=pltpu.VMEM)
    smem = pl.BlockSpec(memory_space=pltpu.SMEM)
    wide, narrow = lax.axis_index("wide"), lax.axis_index("narrow")
    size = lax.axis_size("wide")
    route = residual_route(size)
    source = jnp.zeros((), jnp.int32)
    for w, n, to in route:
        source = jnp.where((wide == n) & (narrow == to), w, source)
    where = jnp.stack([wide, narrow, source]).astype(jnp.int32)
    turned = lax.ppermute(
        residual.reshape(rows, columns),
        ("wide", "narrow"),
        [(w * size + n, n * size + to) for w, n, to in route],
    )
    given = (
        lengths,
        queries.reshape(rows * heads, width),
        key_cache.reshape(-1, width),
        cached_value_rows.reshape(-1, width),
        expert_ids.transpose(0, 2, 1),
        route_weights.transpose(0, 2, 1),
    )
    payload = pl.pallas_call(
        attend_kernel,
        out_shape=jax.ShapeDtypeStruct((rows, depth + 128), jnp.bfloat16),
        in_specs=[pl.BlockSpec(memory_space=pl.ANY)] * 6,
        out_specs=vmem,
        scratch_shapes=[pltpu.VMEM((rows * heads, width), jnp.float32)]
        + [pltpu.SMEM(given[0].shape, given[0].dtype)]
        + [pltpu.VMEM(g.shape, g.dtype) for g in given[1:]]
        + [pltpu.SemaphoreType.DMA((6,))],
        cost_estimate=pl.CostEstimate(flops=20000000000, bytes_accessed=1000000, transcendentals=0),
        compiler_params=pltpu.CompilerParams(vmem_limit_bytes=6 * 2**20),
    )(*[pltpu.with_memory_space_constraint(g, pltpu.HBM) for g in given])
    others = spread(payload)
    keep, send, mix = pl.pallas_call(
        project_kernel,
        out_shape=(
            jax.ShapeDtypeStruct((size * rows, half), jnp.float32),
            jax.ShapeDtypeStruct((size * rows, half), jnp.bfloat16),
            jax.ShapeDtypeStruct((size * rows, 128), jnp.bfloat16),
        ),
        in_specs=[smem] + [vmem] * 6,
        out_specs=(vmem, vmem, vmem),
        cost_estimate=pl.CostEstimate(flops=30000000000, bytes_accessed=1000000, transcendentals=0),
        compiler_params=pltpu.CompilerParams(vmem_limit_bytes=6 * 2**20),
    )(where, payload, *others, w_out, turned)
    part = (keep + flip_permute(send, "narrow", 1).astype(jnp.float32)).astype(jnp.bfloat16)
    stream = (
        part.astype(jnp.float32) + flip_permute(part, "narrow", 2).astype(jnp.float32)
    ).astype(jnp.bfloat16)
    mine = jnp.stack([stream] + spread(stream))
    other = flip_permute(mine, "narrow", 1)
    weights = [
        pltpu.with_memory_space_constraint(w, pltpu.VMEM)
        for w in (w_gate, w_up, w_down.reshape(experts * hidden, model))
    ]
    keep, send, own = pl.pallas_call(
        expert_kernel,
        out_shape=(
            pltpu.VMEM((size * rows, model // 2), jnp.float32),
            pltpu.VMEM((size * rows, model // 2), jnp.bfloat16),
            pltpu.VMEM((rows, columns), jnp.bfloat16),
        ),
        in_specs=[smem] + [vmem] * 7,
        out_specs=(vmem, vmem, vmem),
        scratch_shapes=[
            pltpu.VMEM((size * rows, model), jnp.bfloat16),
            pltpu.VMEM((size * rows, experts * hidden), jnp.bfloat16),
        ],
        compiler_params=pltpu.CompilerParams(vmem_limit_bytes=11 * 2**20),
    )(
        where,
        *[pltpu.with_memory_space_constraint(p, pltpu.VMEM) for p in (mine, other, mix)],
        norm_gain.reshape(1, model),
        *weights,
    )
    total = (keep + flip_permute(send, "narrow", 1).astype(jnp.float32)).astype(jnp.bfloat16)
    total = total.reshape(size, rows, model // 2)
    devices = range(size * size)
    got = [
        lax.ppermute(
            total[s],
            ("wide", "narrow"),
            [(i, i ^ (s * size) ^ (2 if i & 1 else 0)) for i in devices],
        ).astype(jnp.float32)
        for s in (2, 0, 1, 3)
    ]
    summed = got[0] + got[1] + got[2] + got[3]
    first = (narrow & 1) == 0
    left, right = summed[:, :columns], summed[:, columns:]
    cross = flip_permute(jnp.where(first, right, left).astype(jnp.bfloat16), "narrow", 1)
    result = own.astype(jnp.float32) + jnp.where(first, left, right) + cross.astype(jnp.float32)
    return result.astype(jnp.bfloat16).reshape(micro, per_micro, columns)


def solution(mesh):
    in_specs = (
        P(None, ("grp", "wide"), "narrow", None),
        P(None, ("grp", "wide"), None, "narrow", None),
        P(None, ("grp", "wide"), None, "narrow", None),
        P(None, ("grp", "wide")),
        P(None, ("grp", "wide"), "narrow"),
        P("narrow", "wide"),
        P(),
        P(None, ("grp", "wide"), None),
        P(None, ("grp", "wide"), None),
        P("wide", None, "narrow"),
        P("wide", None, "narrow"),
        P("wide", "narrow", None),
    )
    out_specs = P(None, ("grp", "wide"), "narrow")
    small = mesh.shape["wide"] == 4 and mesh.shape["narrow"] == 4
    body = local_small if small else local
    return jax.shard_map(body, mesh=mesh, in_specs=in_specs, out_specs=out_specs, check_vma=False)
```

```python
import math

import jax
import jax.numpy as jnp
from jax import lax
from jax.experimental import pallas as pl
from jax.experimental.pallas import tpu as pltpu
from jax.sharding import PartitionSpec as P

EXPERTS = 64
CAP = 3


def attend(query_rows, keys, values, valid_len):
    row_count, q_heads, head_size = query_rows.shape
    slot_count = keys.shape[1]
    kv_heads = keys.shape[2]
    flat_keys = keys.reshape(row_count, slot_count, kv_heads * head_size)
    flat_values = values.reshape(row_count, slot_count, kv_heads * head_size)
    position = jnp.arange(slot_count)
    usable = position[None, :] < valid_len[:, None]
    scores = jnp.einsum(
        "rgd,rcd->rgc", query_rows, flat_keys, preferred_element_type=jnp.float32
    ) / math.sqrt(head_size)
    scores = jnp.where(usable[:, None, :], scores, -1e30)
    largest = jnp.max(scores, axis=-1, keepdims=True)
    weight = jnp.exp(scores - largest)
    probs = (weight / jnp.sum(weight, axis=-1, keepdims=True)).astype(jnp.bfloat16)
    mixed = jnp.einsum("rgc,rcd->rgd", probs, flat_values, preferred_element_type=jnp.float32)
    results = mixed.astype(jnp.bfloat16)
    return results.reshape(row_count, q_heads * head_size)


def route_tables(chosen, weights, expert_count, capacity):
    row_count, top_count = chosen.shape
    pairs = chosen.reshape(-1)
    onehot = (pairs[:, None] == jnp.arange(expert_count)[None, :]).astype(jnp.int32)
    before = jnp.cumsum(onehot, axis=0) - onehot
    rank = jnp.sum(onehot * before, axis=1)
    slot = pairs * capacity + rank
    select = (slot[:, None] == jnp.arange(expert_count * capacity)[None, :]).astype(jnp.float32)
    select = select.reshape(row_count, top_count, expert_count * capacity)
    dispatch = jnp.sum(select, axis=1).astype(jnp.bfloat16)
    combine = jnp.sum(select * weights[:, :, None], axis=1)
    return (dispatch, combine)


def expert_block(pieces, norm_gain, w_gate, w_up, w_down):
    parts_count = pieces.shape[0]
    local_experts, model_width, hidden_width = w_gate.shape
    part_width = model_width // parts_count
    values = pieces.astype(jnp.float32)
    square = jnp.mean(values * values, axis=(0, 4), keepdims=True)
    gain_parts = norm_gain.reshape(parts_count, 1, 1, 1, part_width)
    normed = (values * lax.rsqrt(square + 1e-06) * gain_parts).astype(jnp.bfloat16)
    gate_parts = w_gate.reshape(local_experts, parts_count, part_width, hidden_width)
    up_parts = w_up.reshape(local_experts, parts_count, part_width, hidden_width)
    gate = jnp.einsum("nsjcd,jndf->sjcf", normed, gate_parts, preferred_element_type=jnp.float32)
    upper = jnp.einsum("nsjcd,jndf->sjcf", normed, up_parts, preferred_element_type=jnp.float32)
    hidden = (jax.nn.silu(gate) * upper).astype(jnp.bfloat16)
    narrow_count = lax.axis_size("narrow")
    down_parts = w_down.reshape(
        local_experts, w_down.shape[1], narrow_count, model_width // narrow_count
    )
    partial_out = jnp.einsum(
        "sjcf,jfnd->nsjcd", hidden, down_parts, preferred_element_type=jnp.float32
    )
    summed = lax.psum_scatter(
        partial_out.astype(jnp.bfloat16), "narrow", scatter_dimension=0, tiled=True
    ).astype(jnp.float32)[0]
    return lax.all_to_all(
        summed.astype(jnp.bfloat16), "wide", split_axis=0, concat_axis=0, tiled=True
    )


def local(
    queries,
    key_cache,
    cached_value_rows,
    lengths,
    residual,
    w_out,
    norm_gain,
    expert_ids,
    route_weights,
    w_gate,
    w_up,
    w_down,
):
    micro_count = queries.shape[0]
    wide_count = lax.axis_size("wide")
    local_experts = w_gate.shape[0]
    capacity = CAP
    attended = [
        attend(
            queries[index_values],
            key_cache[index_values],
            cached_value_rows[index_values],
            lengths[index_values],
        )
        for index_values in range(micro_count)
    ]
    terms = []
    for index_values in range(micro_count):
        columns = jnp.dot(
            lax.all_gather(attended[index_values], "wide", axis=0, tiled=True),
            w_out,
            preferred_element_type=jnp.float32,
        )
        terms.append(
            lax.all_to_all(
                columns.astype(jnp.bfloat16), "wide", split_axis=0, concat_axis=1, tiled=True
            ).astype(columns.dtype)
        )
    partial_sum = jnp.stack(terms)
    projected = lax.psum_scatter(
        partial_sum.astype(jnp.bfloat16), "narrow", scatter_dimension=2, tiled=True
    ).astype(jnp.float32)
    stream = (residual.astype(jnp.float32) + projected).astype(jnp.bfloat16)
    outputs = []
    for index_values in range(micro_count):
        dispatch, combine = route_tables(
            expert_ids[index_values], route_weights[index_values], EXPERTS, capacity
        )
        packed = lax.dot_general(
            dispatch,
            stream[index_values],
            (((0,), (0,)), ((), ())),
            preferred_element_type=jnp.float32,
        )
        packed = packed.astype(jnp.bfloat16).reshape(
            wide_count, local_experts, capacity, stream.shape[2]
        )
        back = (
            lambda rows_in: expert_block(
                lax.all_gather(rows_in[None], "narrow", axis=0, tiled=True),
                norm_gain,
                w_gate,
                w_up,
                w_down,
            )
        )(lax.all_to_all(packed, "wide", split_axis=0, concat_axis=0, tiled=True))
        returned = back.reshape(wide_count * local_experts * capacity, back.shape[3]).astype(
            jnp.float32
        )
        mixed = jnp.dot(combine, returned, precision=lax.Precision.HIGHEST)
        outputs.append((stream[index_values].astype(jnp.float32) + mixed).astype(jnp.bfloat16))
    return jnp.stack(outputs)


def flip_permute(value, axis, mask):
    size = lax.axis_size(axis)
    return lax.ppermute(value, axis, [(i, i ^ mask) for i in range(size)])


def spread(value):
    got = {s: flip_permute(value, "wide", s) for s in (1, 3, 2)}
    return [got[1], got[2], got[3]]


def attend_kernel(*refs):
    given, out_ref, mixed_ref, held, sems = refs[:6], refs[6], refs[7], refs[8:14], refs[14]
    copies = [
        pltpu.make_async_copy(source, target, sems.at[i])
        for i, (source, target) in enumerate(zip(given, held))
    ]
    for copy in copies:
        copy.start()
    for copy in copies:
        copy.wait()
    len_ref, q_ref, k_ref, v_ref, ids_ref, wts_ref = held
    rows, heads = out_ref.shape[0], q_ref.shape[0] // out_ref.shape[0]
    width = q_ref.shape[1]
    slots = k_ref.shape[0] // rows
    group = 256 // slots
    micro, per_micro = len_ref.shape
    row_request = lax.broadcasted_iota(jnp.int32, (group * heads, group * slots), 0) // heads
    column = lax.broadcasted_iota(jnp.int32, (group * heads, group * slots), 1)
    place = column - row_request * slots
    scores = []
    limits = []
    for g in range(rows // group):
        limit = jnp.zeros_like(place)
        for i in range(group):
            r = g * group + i
            limit = jnp.where(row_request == i, len_ref[r // per_micro, r % per_micro], limit)
        limits.append(limit)
        scores.append(
            lax.dot_general(
                q_ref[g * group * heads:(g + 1) * group * heads, :],
                k_ref[g * group * slots:(g + 1) * group * slots, :],
                (((1,), (1,)), ((), ())),
                preferred_element_type=jnp.float32,
            )
        )
    place = jnp.concatenate([place] * len(scores), axis=0)
    usable = (place >= 0) & (place < jnp.concatenate(limits, axis=0))
    scores = jnp.concatenate(scores, axis=0) * (1.0 / math.sqrt(width))
    scores = jnp.where(usable, scores, -1e30)
    weight = jnp.exp(scores - jnp.max(scores, axis=-1, keepdims=True))
    probs = (weight / jnp.sum(weight, axis=-1, keepdims=True)).astype(jnp.bfloat16)
    for g in range(rows // group):
        mixed_ref[g * group * heads:(g + 1) * group * heads, :] = jnp.dot(
            probs[g * group * heads:(g + 1) * group * heads, :],
            v_ref[g * group * slots:(g + 1) * group * slots, :],
            preferred_element_type=jnp.float32,
        )
    for h in range(heads):
        out_ref[:, h * width:(h + 1) * width] = mixed_ref[
            pl.ds(h, rows, stride=heads), :
        ].astype(jnp.bfloat16)
    lanes = 64
    expert = lax.broadcasted_iota(jnp.int32, (lanes, per_micro), 0)
    eye = (
        lax.broadcasted_iota(jnp.int32, (per_micro, per_micro), 0)
        == lax.broadcasted_iota(jnp.int32, (per_micro, per_micro), 1)
    ).astype(jnp.bfloat16)
    for m in range(micro):
        total = jnp.zeros((lanes, per_micro), jnp.float32)
        for t in range(ids_ref.shape[1]):
            total += jnp.where(
                expert == ids_ref[m, t:t + 1, :], wts_ref[m, t:t + 1, :], 0.0
            )
        high = total.astype(jnp.bfloat16)
        low = (total - high.astype(jnp.float32)).astype(jnp.bfloat16)
        both = jnp.concatenate([high, low], axis=0)
        out_ref[m * per_micro:(m + 1) * per_micro, heads * width:] = lax.dot_general(
            eye, both, (((1,), (1,)), ((), ())), preferred_element_type=jnp.float32
        ).astype(jnp.bfloat16)


def project_kernel(where_ref, own_ref, got1_ref, got2_ref, got3_ref, w_ref, res_ref,
                   keep_ref, send_ref, mix_ref):
    wide, narrow = where_ref[0], where_ref[1]
    depth = w_ref.shape[0]
    half = keep_ref.shape[1]
    rows = own_ref.shape[0]
    features = jnp.concatenate(
        [r[:, :depth] for r in (own_ref, got1_ref, got2_ref, got3_ref)], axis=0
    )
    mine = pl.ds(pl.multiple_of((narrow & 1) * half, half), half)
    other = pl.ds(pl.multiple_of((1 - (narrow & 1)) * half, half), half)
    spot = pl.ds(pl.multiple_of((wide ^ where_ref[2]) * rows, rows), rows)
    keep_ref[...] = jnp.dot(features, w_ref[:, mine], preferred_element_type=jnp.float32)
    keep_ref[spot, :] += res_ref[:, mine].astype(jnp.float32)
    part = jnp.dot(features, w_ref[:, other], preferred_element_type=jnp.float32)
    part_rows = lax.broadcasted_iota(jnp.int32, part.shape, 0) // rows
    extra = res_ref[:, other].astype(jnp.float32)
    extra = jnp.concatenate([extra] * (part.shape[0] // rows), axis=0)
    part = jnp.where(part_rows == (wide ^ where_ref[2]), part + extra, part)
    send_ref[...] = part.astype(jnp.bfloat16)
    mix_ref[...] = jnp.concatenate(
        [r[:, depth:] for r in (own_ref, got1_ref, got2_ref, got3_ref)], axis=0
    )


def down_columns(hid_ref, wd_ref, out_ref, place, block):
    for k in range(2):
        start = pl.multiple_of((2 * place + k) * block, block)
        out = jnp.dot(
            hid_ref[...], wd_ref[:, pl.ds(start, block)], preferred_element_type=jnp.float32
        )
        out_ref[:, k * block:(k + 1) * block] = out.astype(out_ref.dtype)


def expert_kernel(where_ref, mine_ref, other_ref, mix_ref, gain_ref,
                  wg_ref, wu_ref, wd_ref, hid_ref, send_ref, stream_ref,
                  x_ref):
    wide, narrow = where_ref[0], where_ref[1]
    core = narrow & 1
    blocks, total, half = mine_ref.shape
    rows = total // blocks
    experts, depth, width = wg_ref.shape
    block = 2 * half
    square = jnp.zeros((total, 1), jnp.float32)
    for s in range(blocks):
        for piece, side in ((mine_ref, core), (other_ref, 1 - core)):
            place = pl.multiple_of((wide ^ s) * (2 * half) + side * half, half)
            lifted = jnp.concatenate(
                [piece[s, (u ^ s) * rows:((u ^ s) + 1) * rows, :] for u in range(blocks)], axis=0
            )
            x_ref[:, pl.ds(place, half)] = lifted
            value = lifted.astype(jnp.float32)
            square += jnp.sum(value * value, axis=1, keepdims=True)
    own = pl.multiple_of(narrow * (2 * half), 2 * half)
    stream_ref[...] = x_ref[:rows, pl.ds(own, 2 * half)]
    scale = lax.rsqrt(square * (1.0 / depth) + 1e-6)
    for b in range(depth // 512):
        cols = slice(b * 512, (b + 1) * 512)
        x_ref[:, cols] = (
            x_ref[:, cols].astype(jnp.float32) * scale * gain_ref[:, cols]
        ).astype(jnp.bfloat16)
    mix = mix_ref[...]
    lane = lax.broadcasted_iota(jnp.int32, (mix.shape[1], width), 0) % (mix.shape[1] // 2)

    for e in range(experts):
        gate = jnp.dot(x_ref[...], wg_ref[e], preferred_element_type=jnp.float32)
        upper = jnp.dot(x_ref[...], wu_ref[e], preferred_element_type=jnp.float32)
        pick = (lane == wide * experts + e).astype(jnp.bfloat16)
        share = jnp.dot(mix, pick, preferred_element_type=jnp.float32)
        hidden = gate / (1.0 + jnp.exp(-gate)) * upper * share
        hid_ref[:, e * width:(e + 1) * width] = hidden.astype(jnp.bfloat16)
    down_columns(hid_ref, wd_ref, send_ref, 1 - ((narrow >> 1) ^ core), block)


def keep_kernel(where_ref, hid_ref, wd_ref, keep_ref):
    narrow = where_ref[1]
    down_columns(hid_ref, wd_ref, keep_ref, (narrow >> 1) ^ (narrow & 1), keep_ref.shape[1] // 2)


def residual_route(size):
    route = []
    for n in range(size):
        near = sorted(range(size), key=lambda w: abs(w - n))
        column = n >> 1
        places = [2 * (column ^ 1), 2 * (column ^ 1) + 1, 2 * column, 2 * column + 1]
        route += [(w, n, to) for w, to in zip(near, places)]
    return route


def local_small(
    queries,
    key_cache,
    cached_value_rows,
    lengths,
    residual,
    w_out,
    norm_gain,
    expert_ids,
    route_weights,
    w_gate,
    w_up,
    w_down,
):
    micro, per_micro, heads, width = queries.shape
    rows = micro * per_micro
    depth, columns = w_out.shape
    experts, model, hidden = w_gate.shape
    half = columns // 2
    vmem = pl.BlockSpec(memory_space=pltpu.VMEM)
    smem = pl.BlockSpec(memory_space=pltpu.SMEM)
    wide, narrow = lax.axis_index("wide"), lax.axis_index("narrow")
    size = lax.axis_size("wide")
    route = residual_route(size)
    source = jnp.zeros((), jnp.int32)
    for w, n, to in route:
        source = jnp.where((wide == n) & (narrow == to), w, source)
    where = jnp.stack([wide, narrow, source]).astype(jnp.int32)
    turned = lax.ppermute(
        residual.reshape(rows, columns),
        ("wide", "narrow"),
        [(w * size + n, n * size + to) for w, n, to in route],
    )
    given = (
        lengths,
        queries.reshape(rows * heads, width),
        key_cache.reshape(-1, width),
        cached_value_rows.reshape(-1, width),
        expert_ids.transpose(0, 2, 1),
        route_weights.transpose(0, 2, 1),
    )
    payload = pl.pallas_call(
        attend_kernel,
        out_shape=jax.ShapeDtypeStruct((rows, depth + 128), jnp.bfloat16),
        in_specs=[pl.BlockSpec(memory_space=pl.ANY)] * 6,
        out_specs=vmem,
        scratch_shapes=[pltpu.VMEM((rows * heads, width), jnp.float32)]
        + [pltpu.SMEM(given[0].shape, given[0].dtype)]
        + [pltpu.VMEM(g.shape, g.dtype) for g in given[1:]]
        + [pltpu.SemaphoreType.DMA((6,))],
        cost_estimate=pl.CostEstimate(flops=20000000000, bytes_accessed=1000000, transcendentals=0),
        compiler_params=pltpu.CompilerParams(vmem_limit_bytes=6 * 2**20),
    )(*[pltpu.with_memory_space_constraint(g, pltpu.HBM) for g in given])
    others = spread(payload)
    keep, send, mix = pl.pallas_call(
        project_kernel,
        out_shape=(
            jax.ShapeDtypeStruct((size * rows, half), jnp.float32),
            jax.ShapeDtypeStruct((size * rows, half), jnp.bfloat16),
            jax.ShapeDtypeStruct((size * rows, 128), jnp.bfloat16),
        ),
        in_specs=[smem] + [vmem] * 6,
        out_specs=(vmem, vmem, vmem),
        cost_estimate=pl.CostEstimate(flops=30000000000, bytes_accessed=1000000, transcendentals=0),
        compiler_params=pltpu.CompilerParams(vmem_limit_bytes=6 * 2**20),
    )(where, payload, *others, w_out, turned)
    part = (keep + flip_permute(send, "narrow", 1).astype(jnp.float32)).astype(jnp.bfloat16)
    stream = (
        part.astype(jnp.float32) + flip_permute(part, "narrow", 2).astype(jnp.float32)
    ).astype(jnp.bfloat16)
    mine = jnp.stack([stream] + spread(stream))
    other = flip_permute(mine, "narrow", 1)
    weights = [
        pltpu.with_memory_space_constraint(w, pltpu.VMEM)
        for w in (w_gate, w_up, w_down.reshape(experts * hidden, model))
    ]
    hid, send, own = pl.pallas_call(
        expert_kernel,
        out_shape=(
            pltpu.VMEM((size * rows, experts * hidden), jnp.bfloat16),
            pltpu.VMEM((size * rows, model // 2), jnp.bfloat16),
            pltpu.VMEM((rows, columns), jnp.bfloat16),
        ),
        in_specs=[smem] + [vmem] * 7,
        out_specs=(vmem, vmem, vmem),
        scratch_shapes=[
            pltpu.VMEM((size * rows, model), jnp.bfloat16),
        ],
        compiler_params=pltpu.CompilerParams(vmem_limit_bytes=11 * 2**20),
    )(
        where,
        *[pltpu.with_memory_space_constraint(p, pltpu.VMEM) for p in (mine, other, mix)],
        norm_gain.reshape(1, model),
        *weights,
    )
    keep = pl.pallas_call(
        keep_kernel,
        out_shape=pltpu.VMEM((size * rows, model // 2), jnp.float32),
        in_specs=[smem] + [vmem] * 2,
        out_specs=vmem,
        cost_estimate=pl.CostEstimate(flops=2 * 10**9, bytes_accessed=10**6, transcendentals=0),
        compiler_params=pltpu.CompilerParams(vmem_limit_bytes=4 * 2**20),
    )(where, pltpu.with_memory_space_constraint(hid, pltpu.VMEM), weights[2])
    total = (keep + flip_permute(send, "narrow", 1).astype(jnp.float32)).astype(jnp.bfloat16)
    total = total.reshape(size, rows, model // 2)
    devices = range(size * size)
    got = [
        lax.ppermute(
            total[s],
            ("wide", "narrow"),
            [(i, i ^ (s * size) ^ (2 if i & 1 else 0)) for i in devices],
        ).astype(jnp.float32)
        for s in (2, 0, 1, 3)
    ]
    summed = got[0] + got[1] + got[2] + got[3]
    first = (narrow & 1) == 0
    left, right = summed[:, :columns], summed[:, columns:]
    cross = flip_permute(jnp.where(first, right, left).astype(jnp.bfloat16), "narrow", 1)
    result = own.astype(jnp.float32) + jnp.where(first, left, right) + cross.astype(jnp.float32)
    return result.astype(jnp.bfloat16).reshape(micro, per_micro, columns)


def solution(mesh):
    in_specs = (
        P(None, ("grp", "wide"), "narrow", None),
        P(None, ("grp", "wide"), None, "narrow", None),
        P(None, ("grp", "wide"), None, "narrow", None),
        P(None, ("grp", "wide")),
        P(None, ("grp", "wide"), "narrow"),
        P("narrow", "wide"),
        P(),
        P(None, ("grp", "wide"), None),
        P(None, ("grp", "wide"), None),
        P("wide", None, "narrow"),
        P("wide", None, "narrow"),
        P("wide", "narrow", None),
    )
    out_specs = P(None, ("grp", "wide"), "narrow")
    small = mesh.shape["wide"] == 4 and mesh.shape["narrow"] == 4
    body = local_small if small else local
    return jax.shard_map(body, mesh=mesh, in_specs=in_specs, out_specs=out_specs, check_vma=False)
```

```python
import math

import jax
import jax.numpy as jnp
from jax import lax
from jax.experimental import pallas as pl
from jax.experimental.pallas import tpu as pltpu
from jax.sharding import PartitionSpec as P

EXPERTS = 64
CAP = 3


def attend(query_rows, keys, values, valid_len):
    row_count, q_heads, head_size = query_rows.shape
    slot_count = keys.shape[1]
    kv_heads = keys.shape[2]
    flat_keys = keys.reshape(row_count, slot_count, kv_heads * head_size)
    flat_values = values.reshape(row_count, slot_count, kv_heads * head_size)
    position = jnp.arange(slot_count)
    usable = position[None, :] < valid_len[:, None]
    scores = jnp.einsum(
        "rgd,rcd->rgc", query_rows, flat_keys, preferred_element_type=jnp.float32
    ) / math.sqrt(head_size)
    scores = jnp.where(usable[:, None, :], scores, -1e30)
    largest = jnp.max(scores, axis=-1, keepdims=True)
    weight = jnp.exp(scores - largest)
    probs = (weight / jnp.sum(weight, axis=-1, keepdims=True)).astype(jnp.bfloat16)
    mixed = jnp.einsum("rgc,rcd->rgd", probs, flat_values, preferred_element_type=jnp.float32)
    results = mixed.astype(jnp.bfloat16)
    return results.reshape(row_count, q_heads * head_size)


def route_tables(chosen, weights, expert_count, capacity):
    row_count, top_count = chosen.shape
    pairs = chosen.reshape(-1)
    onehot = (pairs[:, None] == jnp.arange(expert_count)[None, :]).astype(jnp.int32)
    before = jnp.cumsum(onehot, axis=0) - onehot
    rank = jnp.sum(onehot * before, axis=1)
    slot = pairs * capacity + rank
    select = (slot[:, None] == jnp.arange(expert_count * capacity)[None, :]).astype(jnp.float32)
    select = select.reshape(row_count, top_count, expert_count * capacity)
    dispatch = jnp.sum(select, axis=1).astype(jnp.bfloat16)
    combine = jnp.sum(select * weights[:, :, None], axis=1)
    return (dispatch, combine)


def expert_block(pieces, norm_gain, w_gate, w_up, w_down):
    parts_count = pieces.shape[0]
    local_experts, model_width, hidden_width = w_gate.shape
    part_width = model_width // parts_count
    values = pieces.astype(jnp.float32)
    square = jnp.mean(values * values, axis=(0, 4), keepdims=True)
    gain_parts = norm_gain.reshape(parts_count, 1, 1, 1, part_width)
    normed = (values * lax.rsqrt(square + 1e-06) * gain_parts).astype(jnp.bfloat16)
    gate_parts = w_gate.reshape(local_experts, parts_count, part_width, hidden_width)
    up_parts = w_up.reshape(local_experts, parts_count, part_width, hidden_width)
    gate = jnp.einsum("nsjcd,jndf->sjcf", normed, gate_parts, preferred_element_type=jnp.float32)
    upper = jnp.einsum("nsjcd,jndf->sjcf", normed, up_parts, preferred_element_type=jnp.float32)
    hidden = (jax.nn.silu(gate) * upper).astype(jnp.bfloat16)
    narrow_count = lax.axis_size("narrow")
    down_parts = w_down.reshape(
        local_experts, w_down.shape[1], narrow_count, model_width // narrow_count
    )
    partial_out = jnp.einsum(
        "sjcf,jfnd->nsjcd", hidden, down_parts, preferred_element_type=jnp.float32
    )
    summed = lax.psum_scatter(
        partial_out.astype(jnp.bfloat16), "narrow", scatter_dimension=0, tiled=True
    ).astype(jnp.float32)[0]
    return lax.all_to_all(
        summed.astype(jnp.bfloat16), "wide", split_axis=0, concat_axis=0, tiled=True
    )


def local(
    queries,
    key_cache,
    cached_value_rows,
    lengths,
    residual,
    w_out,
    norm_gain,
    expert_ids,
    route_weights,
    w_gate,
    w_up,
    w_down,
):
    micro_count = queries.shape[0]
    wide_count = lax.axis_size("wide")
    local_experts = w_gate.shape[0]
    capacity = CAP
    attended = [
        attend(
            queries[index_values],
            key_cache[index_values],
            cached_value_rows[index_values],
            lengths[index_values],
        )
        for index_values in range(micro_count)
    ]
    terms = []
    for index_values in range(micro_count):
        columns = jnp.dot(
            lax.all_gather(attended[index_values], "wide", axis=0, tiled=True),
            w_out,
            preferred_element_type=jnp.float32,
        )
        terms.append(
            lax.all_to_all(
                columns.astype(jnp.bfloat16), "wide", split_axis=0, concat_axis=1, tiled=True
            ).astype(columns.dtype)
        )
    partial_sum = jnp.stack(terms)
    projected = lax.psum_scatter(
        partial_sum.astype(jnp.bfloat16), "narrow", scatter_dimension=2, tiled=True
    ).astype(jnp.float32)
    stream = (residual.astype(jnp.float32) + projected).astype(jnp.bfloat16)
    outputs = []
    for index_values in range(micro_count):
        dispatch, combine = route_tables(
            expert_ids[index_values], route_weights[index_values], EXPERTS, capacity
        )
        packed = lax.dot_general(
            dispatch,
            stream[index_values],
            (((0,), (0,)), ((), ())),
            preferred_element_type=jnp.float32,
        )
        packed = packed.astype(jnp.bfloat16).reshape(
            wide_count, local_experts, capacity, stream.shape[2]
        )
        back = (
            lambda rows_in: expert_block(
                lax.all_gather(rows_in[None], "narrow", axis=0, tiled=True),
                norm_gain,
                w_gate,
                w_up,
                w_down,
            )
        )(lax.all_to_all(packed, "wide", split_axis=0, concat_axis=0, tiled=True))
        returned = back.reshape(wide_count * local_experts * capacity, back.shape[3]).astype(
            jnp.float32
        )
        mixed = jnp.dot(combine, returned, precision=lax.Precision.HIGHEST)
        outputs.append((stream[index_values].astype(jnp.float32) + mixed).astype(jnp.bfloat16))
    return jnp.stack(outputs)


def flip_permute(value, axis, mask):
    size = lax.axis_size(axis)
    return lax.ppermute(value, axis, [(i, i ^ mask) for i in range(size)])


def spread(value):
    got = {s: flip_permute(value, "wide", s) for s in (1, 3, 2)}
    return [got[1], got[2], got[3]]


def attend_kernel(*refs):
    given, out_ref, mixed_ref, held, sems = refs[:6], refs[6], refs[7], refs[8:14], refs[14]
    copies = [
        pltpu.make_async_copy(source, target, sems.at[i])
        for i, (source, target) in enumerate(zip(given, held))
    ]
    for copy in copies:
        copy.start()
    for copy in copies:
        copy.wait()
    len_ref, q_ref, k_ref, v_ref, ids_ref, wts_ref = held
    rows, heads = out_ref.shape[0], q_ref.shape[0] // out_ref.shape[0]
    width = q_ref.shape[1]
    slots = k_ref.shape[0] // rows
    group = 256 // slots
    micro, per_micro = len_ref.shape
    row_request = lax.broadcasted_iota(jnp.int32, (group * heads, group * slots), 0) // heads
    column = lax.broadcasted_iota(jnp.int32, (group * heads, group * slots), 1)
    place = column - row_request * slots
    scores = []
    limits = []
    for g in range(rows // group):
        limit = jnp.zeros_like(place)
        for i in range(group):
            r = g * group + i
            limit = jnp.where(row_request == i, len_ref[r // per_micro, r % per_micro], limit)
        limits.append(limit)
        scores.append(
            lax.dot_general(
                q_ref[g * group * heads:(g + 1) * group * heads, :],
                k_ref[g * group * slots:(g + 1) * group * slots, :],
                (((1,), (1,)), ((), ())),
                preferred_element_type=jnp.float32,
            )
        )
    place = jnp.concatenate([place] * len(scores), axis=0)
    usable = (place >= 0) & (place < jnp.concatenate(limits, axis=0))
    scores = jnp.concatenate(scores, axis=0) * (1.0 / math.sqrt(width))
    scores = jnp.where(usable, scores, -1e30)
    weight = jnp.exp(scores - jnp.max(scores, axis=-1, keepdims=True))
    probs = (weight / jnp.sum(weight, axis=-1, keepdims=True)).astype(jnp.bfloat16)
    for g in range(rows // group):
        mixed_ref[g * group * heads:(g + 1) * group * heads, :] = jnp.dot(
            probs[g * group * heads:(g + 1) * group * heads, :],
            v_ref[g * group * slots:(g + 1) * group * slots, :],
            preferred_element_type=jnp.float32,
        )
    for h in range(heads):
        out_ref[:, h * width:(h + 1) * width] = mixed_ref[
            pl.ds(h, rows, stride=heads), :
        ].astype(jnp.bfloat16)
    lanes = 64
    expert = lax.broadcasted_iota(jnp.int32, (lanes, per_micro), 0)
    eye = (
        lax.broadcasted_iota(jnp.int32, (per_micro, per_micro), 0)
        == lax.broadcasted_iota(jnp.int32, (per_micro, per_micro), 1)
    ).astype(jnp.bfloat16)
    for m in range(micro):
        total = jnp.zeros((lanes, per_micro), jnp.float32)
        for t in range(ids_ref.shape[1]):
            total += jnp.where(
                expert == ids_ref[m, t:t + 1, :], wts_ref[m, t:t + 1, :], 0.0
            )
        high = total.astype(jnp.bfloat16)
        low = (total - high.astype(jnp.float32)).astype(jnp.bfloat16)
        both = jnp.concatenate([high, low], axis=0)
        out_ref[m * per_micro:(m + 1) * per_micro, heads * width:] = lax.dot_general(
            eye, both, (((1,), (1,)), ((), ())), preferred_element_type=jnp.float32
        ).astype(jnp.bfloat16)


def project_kernel(where_ref, own_ref, got1_ref, got2_ref, got3_ref, w_ref, res_ref,
                   keep_ref, send_ref, mix_ref):
    wide, narrow = where_ref[0], where_ref[1]
    depth = w_ref.shape[0]
    half = keep_ref.shape[1]
    rows = own_ref.shape[0]
    features = jnp.concatenate(
        [r[:, :depth] for r in (own_ref, got1_ref, got2_ref, got3_ref)], axis=0
    )
    mine = pl.ds(pl.multiple_of((narrow & 1) * half, half), half)
    other = pl.ds(pl.multiple_of((1 - (narrow & 1)) * half, half), half)
    spot = pl.ds(pl.multiple_of((wide ^ where_ref[2]) * rows, rows), rows)
    keep_ref[...] = jnp.dot(features, w_ref[:, mine], preferred_element_type=jnp.float32)
    keep_ref[spot, :] += res_ref[:, mine].astype(jnp.float32)
    part = jnp.dot(features, w_ref[:, other], preferred_element_type=jnp.float32)
    part_rows = lax.broadcasted_iota(jnp.int32, part.shape, 0) // rows
    extra = res_ref[:, other].astype(jnp.float32)
    extra = jnp.concatenate([extra] * (part.shape[0] // rows), axis=0)
    part = jnp.where(part_rows == (wide ^ where_ref[2]), part + extra, part)
    send_ref[...] = part.astype(jnp.bfloat16)
    mix_ref[...] = jnp.concatenate(
        [r[:, depth:] for r in (own_ref, got1_ref, got2_ref, got3_ref)], axis=0
    )


def down_columns(hid_ref, wd_ref, out_ref, place, block):
    for k in range(2):
        start = pl.multiple_of((2 * place + k) * block, block)
        out = jnp.dot(
            hid_ref[...], wd_ref[:, pl.ds(start, block)], preferred_element_type=jnp.float32
        )
        out_ref[:, k * block:(k + 1) * block] = out.astype(out_ref.dtype)


def expert_kernel(where_ref, mine_ref, other_ref, mix_ref, gain_ref,
                  wg_ref, wu_ref, wd_ref, hid_ref, send_ref, stream_ref,
                  x_ref):
    wide, narrow = where_ref[0], where_ref[1]
    core = narrow & 1
    blocks, total, half = mine_ref.shape
    rows = total // blocks
    experts, depth, width = wg_ref.shape
    block = 2 * half
    square = jnp.zeros((total, 1), jnp.float32)
    for s in range(blocks):
        for piece, side in ((mine_ref, core), (other_ref, 1 - core)):
            place = pl.multiple_of((wide ^ s) * (2 * half) + side * half, half)
            lifted = jnp.concatenate(
                [piece[s, (u ^ s) * rows:((u ^ s) + 1) * rows, :] for u in range(blocks)], axis=0
            )
            x_ref[:, pl.ds(place, half)] = lifted
            value = lifted.astype(jnp.float32)
            square += jnp.sum(value * value, axis=1, keepdims=True)
    own = pl.multiple_of(narrow * (2 * half), 2 * half)
    stream_ref[...] = x_ref[:rows, pl.ds(own, 2 * half)]
    scale = lax.rsqrt(square * (1.0 / depth) + 1e-6)
    for b in range(depth // 512):
        cols = slice(b * 512, (b + 1) * 512)
        x_ref[:, cols] = (
            x_ref[:, cols].astype(jnp.float32) * scale * gain_ref[:, cols]
        ).astype(jnp.bfloat16)
    mix = mix_ref[...]
    lane = lax.broadcasted_iota(jnp.int32, (mix.shape[1], width), 0) % (mix.shape[1] // 2)

    for e in range(experts):
        gate = jnp.dot(x_ref[...], wg_ref[e], preferred_element_type=jnp.float32)
        upper = jnp.dot(x_ref[...], wu_ref[e], preferred_element_type=jnp.float32)
        pick = (lane == wide * experts + e).astype(jnp.bfloat16)
        share = jnp.dot(mix, pick, preferred_element_type=jnp.float32)
        hidden = gate / (1.0 + jnp.exp(-gate)) * upper * share
        hid_ref[:, e * width:(e + 1) * width] = hidden.astype(jnp.bfloat16)
    down_columns(hid_ref, wd_ref, send_ref, 1 - ((narrow >> 1) ^ core), block)


def keep_kernel(where_ref, hid_ref, wd_ref, keep_ref):
    narrow = where_ref[1]
    down_columns(hid_ref, wd_ref, keep_ref, (narrow >> 1) ^ (narrow & 1), keep_ref.shape[1] // 2)


def residual_route(size):
    route = []
    for n in range(size):
        near = sorted(range(size), key=lambda w: abs(w - n))
        column = n >> 1
        places = [2 * (column ^ 1), 2 * (column ^ 1) + 1, 2 * column, 2 * column + 1]
        route += [(w, n, to) for w, to in zip(near, places)]
    return route


def local_small(
    queries,
    key_cache,
    cached_value_rows,
    lengths,
    residual,
    w_out,
    norm_gain,
    expert_ids,
    route_weights,
    w_gate,
    w_up,
    w_down,
):
    micro, per_micro, heads, width = queries.shape
    rows = micro * per_micro
    depth, columns = w_out.shape
    experts, model, hidden = w_gate.shape
    half = columns // 2
    vmem = pl.BlockSpec(memory_space=pltpu.VMEM)
    smem = pl.BlockSpec(memory_space=pltpu.SMEM)
    wide, narrow = lax.axis_index("wide"), lax.axis_index("narrow")
    size = lax.axis_size("wide")
    route = residual_route(size)
    source = jnp.zeros((), jnp.int32)
    for w, n, to in route:
        source = jnp.where((wide == n) & (narrow == to), w, source)
    where = jnp.stack([wide, narrow, source]).astype(jnp.int32)
    turned = lax.ppermute(
        residual.reshape(rows, columns),
        ("wide", "narrow"),
        [(w * size + n, n * size + to) for w, n, to in route],
    )
    given = (
        lengths,
        queries.reshape(rows * heads, width),
        key_cache.reshape(-1, width),
        cached_value_rows.reshape(-1, width),
        expert_ids.transpose(0, 2, 1),
        route_weights.transpose(0, 2, 1),
    )
    payload = pl.pallas_call(
        attend_kernel,
        out_shape=jax.ShapeDtypeStruct((rows, depth + 128), jnp.bfloat16),
        in_specs=[pl.BlockSpec(memory_space=pl.ANY)] * 6,
        out_specs=vmem,
        scratch_shapes=[pltpu.VMEM((rows * heads, width), jnp.float32)]
        + [pltpu.SMEM(given[0].shape, given[0].dtype)]
        + [pltpu.VMEM(g.shape, g.dtype) for g in given[1:]]
        + [pltpu.SemaphoreType.DMA((6,))],
        cost_estimate=pl.CostEstimate(flops=20000000000, bytes_accessed=1000000, transcendentals=0),
        compiler_params=pltpu.CompilerParams(vmem_limit_bytes=6 * 2**20),
    )(*[pltpu.with_memory_space_constraint(g, pltpu.HBM) for g in given])
    others = spread(payload)
    keep, send, mix = pl.pallas_call(
        project_kernel,
        out_shape=(
            jax.ShapeDtypeStruct((size * rows, half), jnp.float32),
            jax.ShapeDtypeStruct((size * rows, half), jnp.bfloat16),
            jax.ShapeDtypeStruct((size * rows, 128), jnp.bfloat16),
        ),
        in_specs=[smem] + [vmem] * 6,
        out_specs=(vmem, vmem, vmem),
        cost_estimate=pl.CostEstimate(flops=30000000000, bytes_accessed=1000000, transcendentals=0),
        compiler_params=pltpu.CompilerParams(vmem_limit_bytes=6 * 2**20),
    )(where, payload, *others, w_out, turned)
    part = (keep + flip_permute(send, "narrow", 1).astype(jnp.float32)).astype(jnp.bfloat16)
    stream = (
        part.astype(jnp.float32) + flip_permute(part, "narrow", 2).astype(jnp.float32)
    ).astype(jnp.bfloat16)
    got = jnp.stack(spread(stream))
    twin = flip_permute(stream, "narrow", 1)
    mine = jnp.concatenate([stream[None], got])
    other = jnp.concatenate([twin[None], flip_permute(got, "narrow", 1)])
    weights = [
        pltpu.with_memory_space_constraint(w, pltpu.VMEM)
        for w in (w_gate, w_up, w_down.reshape(experts * hidden, model))
    ]
    hid, send, own = pl.pallas_call(
        expert_kernel,
        out_shape=(
            pltpu.VMEM((size * rows, experts * hidden), jnp.bfloat16),
            pltpu.VMEM((size * rows, model // 2), jnp.bfloat16),
            pltpu.VMEM((rows, columns), jnp.bfloat16),
        ),
        in_specs=[smem] + [vmem] * 7,
        out_specs=(vmem, vmem, vmem),
        scratch_shapes=[
            pltpu.VMEM((size * rows, model), jnp.bfloat16),
        ],
        compiler_params=pltpu.CompilerParams(vmem_limit_bytes=12 * 2**20),
    )(
        where,
        *[pltpu.with_memory_space_constraint(p, pltpu.VMEM) for p in (mine, other, mix)],
        norm_gain.reshape(1, model),
        *weights,
    )
    keep = pl.pallas_call(
        keep_kernel,
        out_shape=pltpu.VMEM((size * rows, model // 2), jnp.float32),
        in_specs=[smem] + [vmem] * 2,
        out_specs=vmem,
        cost_estimate=pl.CostEstimate(flops=2 * 10**9, bytes_accessed=10**6, transcendentals=0),
        compiler_params=pltpu.CompilerParams(vmem_limit_bytes=4 * 2**20),
    )(where, pltpu.with_memory_space_constraint(hid, pltpu.VMEM), weights[2])
    total = (keep + flip_permute(send, "narrow", 1).astype(jnp.float32)).astype(jnp.bfloat16)
    total = total.reshape(size, rows, model // 2)
    devices = range(size * size)
    got = [
        lax.ppermute(
            total[s],
            ("wide", "narrow"),
            [(i, i ^ (s * size) ^ (2 if i & 1 else 0)) for i in devices],
        ).astype(jnp.float32)
        for s in (2, 0, 1, 3)
    ]
    summed = got[0] + got[1] + got[2] + got[3]
    first = (narrow & 1) == 0
    left, right = summed[:, :columns], summed[:, columns:]
    cross = flip_permute(jnp.where(first, right, left).astype(jnp.bfloat16), "narrow", 1)
    result = own.astype(jnp.float32) + jnp.where(first, left, right) + cross.astype(jnp.float32)
    return result.astype(jnp.bfloat16).reshape(micro, per_micro, columns)


def solution(mesh):
    in_specs = (
        P(None, ("grp", "wide"), "narrow", None),
        P(None, ("grp", "wide"), None, "narrow", None),
        P(None, ("grp", "wide"), None, "narrow", None),
        P(None, ("grp", "wide")),
        P(None, ("grp", "wide"), "narrow"),
        P("narrow", "wide"),
        P(),
        P(None, ("grp", "wide"), None),
        P(None, ("grp", "wide"), None),
        P("wide", None, "narrow"),
        P("wide", None, "narrow"),
        P("wide", "narrow", None),
    )
    out_specs = P(None, ("grp", "wide"), "narrow")
    small = mesh.shape["wide"] == 4 and mesh.shape["narrow"] == 4
    body = local_small if small else local
    return jax.shard_map(body, mesh=mesh, in_specs=in_specs, out_specs=out_specs, check_vma=False)
```
